32 devices in a mesh: seq: 8 (over y, x, core), head: 4 (over z).
Axes of the slice: x: 2, y: 2, z: 4, core: 2. Of those that a mesh axis runs over, the one named last changes fastest.
Arguments:
- tokens: bfloat16 [48, 192, 1152], P('seq'), may hold values from -6 to 6
- cotangent: bfloat16 [48, 192, 1152], P('seq'), may hold values from -6 to 6
- modulation: float32 [48, 6, 1152], P('seq'), may hold values from -3 to 3
- counts: int32 [48, 8], P('seq'), may hold values from 8 to 24, as said below
- master: float32 [768, 144, 144], P(('seq', 'head'))
- left_stat: float32 [768, 144, 144], P(('seq', 'head')), as said below
- right_stat: float32 [768, 144, 144], P(('seq', 'head')), as said below
- left_root: float32 [768, 144, 144], P(('seq', 'head')), as said below
- right_root: float32 [768, 144, 144], P(('seq', 'head')), as said below
- bias_in: float32 [16, 432], P('head'), may hold values from -2 to 2
- bias_in_sq: float32 [16, 432], P('head'), may hold values from 184.32 to 737.28
- bias_out: float32 [2, 1152], replicated, may hold values from -2 to 2
- bias_out_sq: float32 [2, 1152], replicated, may hold values from 737.28 to 3072
Outputs:
- output: bfloat16 [48, 192, 1152], P('seq')
- grad_tokens: bfloat16 [48, 192, 1152], P('seq')
- grad_modulation: float32 [48, 6, 1152], P('seq', None, 'head')
- weight_grad: float32 [768, 144, 144], P(('seq', 'head'))
- left_new: float32 [768, 144, 144], P(('seq', 'head'))
- right_new: float32 [768, 144, 144], P(('seq', 'head'))
- master_new: float32 [768, 144, 144], P(('seq', 'head'))
- in_bias_grad: float32 [16, 432], P('head')
- in_bias_sq_new: float32 [16, 432], P('head')
- in_bias_new: float32 [16, 432], P('head')
- out_bias_grad: float32 [2, 1152], replicated
- out_bias_sq_new: float32 [2, 1152], replicated
- out_bias_new: float32 [2, 1152], replicated
The draws below stay inside these ranges and needn't reach their ends.
Inputs may be any that keep to these rules, and one draw needn't show every extreme that they name: Each image's counts sum to 128; in every image some position range holds 24 kept rows. `left_stat`: symmetric. `right_stat`: symmetric. `left_root`: symmetric. `right_root`: symmetric.
All inputs are finite; a program needn't handle non-finite values.
Results may differ from the reference program's by a relative error of at most 0.014.
Values may be sent and summed in bfloat16 or wider, within the bound.
No kernel may reach another device: no remote copies, remote signals or barrier semaphores. Data moves between devices by JAX's collectives and lax.ppermute only.
A program may use at most 320 MiB of HBM per device.

```python
import math
from functools import partial
import jax
import jax.numpy as jnp
from jax import lax

D = 1152
HEADS = 16
HEAD_DIM = 72
FF = 4608
PATCHES = 256
RANGES = 8
BLOCK = 144
IMG_BLOCK = 8
HEAD_GROUPS = 4
IMAGES = 48
SLOTS = 24
ALLSLOTS = 192
PACKW = 3456
ROW_TILES = 8
COL_TILES = 24
TILES_DEV = 24
TILES_ALL = 768
BIAS_W = 432
N_SEQ = 8


def draw_counts(key, part):
    key = jax.random.fold_in(key, 1)
    quarter = PATCHES // (4 * RANGES)
    middle = PATCHES // (2 * RANGES)
    many_keys = jax.random.split(key, IMAGES + 1)

    def ordering(single):
        return jax.random.permutation(single, RANGES)
    orders = jax.vmap(ordering)(many_keys[1:])
    moves = jax.random.randint(many_keys[0], (IMAGES, RANGES // 2), -quarter, quarter + 1)
    moves = moves.at[:, 0].set(quarter)
    paired = jnp.stack([moves, -moves], axis=-1).reshape(IMAGES, RANGES)
    row_index = jnp.arange(IMAGES)[:, None]
    placed = jnp.zeros((IMAGES, RANGES), jnp.int32).at[row_index, orders].set(paired)
    return (placed + middle).astype(jnp.int32)


def draw_master(key, part):
    key = jax.random.fold_in(key, 6)
    number = jnp.arange(TILES_ALL)
    within = number % TILES_DEV
    owner = number // (HEAD_GROUPS * TILES_DEV)
    local_tile = owner * TILES_DEV + within
    column_tile = local_tile % COL_TILES
    columns = column_tile[:, None] * BLOCK + jnp.arange(BLOCK)[None, :]
    qwidth = HEADS * HEAD_DIM // HEAD_GROUPS
    ffwidth = FF // HEAD_GROUPS
    scaling = jnp.where(columns < 3 * qwidth, D ** (-0.5), jnp.where(columns < 4 * qwidth, 4.0 * D ** (-0.5), jnp.where(columns < 4 * qwidth + ffwidth, D ** (-0.5), FF ** (-0.5))))
    noise = jax.random.normal(key, (TILES_ALL, BLOCK, BLOCK), jnp.float32)
    return noise * scaling.astype(jnp.float32)[:, None, :]


def statistic(key):
    diag_key, off_key = jax.random.split(key)
    level = BLOCK * 0.05 * (IMAGES * PATCHES // 2)
    diagonal = level * jax.random.uniform(diag_key, (TILES_ALL, BLOCK), jnp.float32, 1.0, 4.0)
    noise = jax.random.normal(off_key, (TILES_ALL, BLOCK, BLOCK), jnp.float32)
    noise = (noise + jnp.swapaxes(noise, 1, 2)) * (0.2 * 2.5 * level / BLOCK ** 0.5 / 1.4142135)
    identity = jnp.eye(BLOCK, dtype=jnp.float32)
    return noise * (1.0 - identity)[None] + identity[None] * diagonal[:, :, None]


def inverse_root(key):
    diag_key, off_key = jax.random.split(key)
    level = (BLOCK * 0.05 * (IMAGES * PATCHES // 2)) ** (-0.25)
    exponent = jax.random.uniform(diag_key, (TILES_ALL, BLOCK), jnp.float32, -0.6931472, 0.6931472)
    diagonal = level * jnp.exp(exponent)
    noise = jax.random.normal(off_key, (TILES_ALL, BLOCK, BLOCK), jnp.float32)
    noise = (noise + jnp.swapaxes(noise, 1, 2)) * (0.2 * level / BLOCK ** 0.5 / 1.4142135)
    identity = jnp.eye(BLOCK, dtype=jnp.float32)
    return noise * (1.0 - identity)[None] + identity[None] * diagonal[:, :, None]


def draw_left_stat(key, part):
    key = jax.random.fold_in(key, 2)
    return statistic(key)


def draw_right_stat(key, part):
    key = jax.random.fold_in(key, 3)
    return statistic(key)


def draw_left_root(key, part):
    key = jax.random.fold_in(key, 4)
    return inverse_root(key)


def draw_right_root(key, part):
    key = jax.random.fold_in(key, 5)
    return inverse_root(key)


def levels(key, dims, cuts, smallest, high):
    gain, own = 1.0, jax.random.fold_in(key, 6)
    for position, parts in cuts:
        draws = jnp.exp(jax.random.uniform(jax.random.fold_in(own, position), (parts,), jnp.float32, smallest / len(cuts), high / len(cuts)))
        gain = gain * jnp.repeat(draws, dims[position] // parts).reshape([-1 if axis == position else 1 for axis in range(len(dims))])
    return gain


def gaussian(own_key, dims, deviation, reach, cuts=(), kind=jnp.bfloat16):
    loudness = levels(own_key, dims, cuts, -0.22, 0.18) if cuts else 1.0
    drawn = jax.random.normal(own_key, dims, jnp.float32) * deviation * loudness
    return jnp.minimum(jnp.maximum(drawn, -reach), reach).astype(kind)


def setup_inputs(seed: int = 0) -> dict:
    streams_of = jax.random.split(jax.random.key(seed), 14)
    return {
        "tokens": gaussian(streams_of[0], (IMAGES, ALLSLOTS, D), 1.0, 6.0, ((0, 8),)),
        "cotangent": gaussian(streams_of[1], (IMAGES, ALLSLOTS, D), 1.0, 6.0, ((0, 8),)),
        "modulation": gaussian(streams_of[2], (IMAGES, 6, D), 0.5, 3.0, ((0, 8),), jnp.float32),
        "counts": draw_counts(jax.random.fold_in(streams_of[13], 71), 0),
        "master": draw_master(jax.random.fold_in(streams_of[13], 71), 0),
        "left_stat": draw_left_stat(jax.random.fold_in(streams_of[13], 71), 0),
        "right_stat": draw_right_stat(jax.random.fold_in(streams_of[13], 71), 0),
        "left_root": draw_left_root(jax.random.fold_in(streams_of[13], 71), 0),
        "right_root": draw_right_root(jax.random.fold_in(streams_of[13], 71), 0),
        "bias_in": gaussian(streams_of[9], (HEADS, BIAS_W), 0.3, 2.0, ((0, 4),), jnp.float32),
        "bias_in_sq": jnp.clip(jnp.exp(math.log(737.28) - 1.3862944 * jax.random.uniform(streams_of[10], (HEADS, BIAS_W), jnp.float32) ** levels(streams_of[10], (HEADS, BIAS_W), ((0, 4),), -0.2, 0.2)), 184.32, 737.28),
        "bias_out": gaussian(streams_of[11], (2, D), 0.3, 2.0, (), jnp.float32),
        "bias_out_sq": jnp.clip(jnp.exp(jax.random.uniform(streams_of[12], (2, D), jnp.float32, math.log(737.28), math.log(3072.0))), 737.28, 3072.0),
    }


@jax.custom_vjp
def low(v):
    return lax.optimization_barrier(v.astype(jnp.bfloat16)).astype(jnp.float32)

@jax.custom_vjp
def low_back(v):
    return v

def low_keep(v):
    return (low(v), None)

def low_pass(kept, grad):
    return (grad,)

def back_keep(v):
    return (v, None)

def back_low(kept, grad):
    return (low(grad),)
low.defvjp(low_keep, low_pass)
low_back.defvjp(back_keep, back_low)
norm_epsilon = 1e-06
decay_rate = 0.5
weight_rate = 0.3
bias_rate = 0.1
root_epsilon = 1e-08
highest = lax.Precision.HIGHEST

def rounded(values):
    return low_back(low(values))

def normalize(values):
    center = lax.optimization_barrier(jnp.mean(values, -1, keepdims=True))
    centered = values - center
    spread = lax.optimization_barrier(jnp.mean(centered * centered, -1, keepdims=True))
    return centered * lax.rsqrt(spread + norm_epsilon)

def tiles_to_slab(tiles):
    grouped = tiles.reshape(N_SEQ, HEAD_GROUPS, TILES_DEV, BLOCK, BLOCK).transpose(1, 0, 2, 3, 4)
    grouped = grouped.reshape(HEAD_GROUPS, ROW_TILES, COL_TILES, BLOCK, BLOCK).transpose(0, 1, 3, 2, 4)
    return grouped.reshape(HEAD_GROUPS, D, PACKW)

def slab_to_tiles(slab):
    grouped = slab.reshape(HEAD_GROUPS, ROW_TILES, BLOCK, COL_TILES, BLOCK).transpose(0, 1, 3, 2, 4)
    grouped = grouped.reshape(HEAD_GROUPS, N_SEQ, TILES_DEV, BLOCK, BLOCK).transpose(1, 0, 2, 3, 4)
    return grouped.reshape(TILES_ALL, BLOCK, BLOCK)

def attend_group(pieces):
    queries, keys_in, values_in, allowed = pieces
    scores = jnp.einsum('ishe,ithe->ihst', queries, keys_in, precision=highest) * HEAD_DIM ** (-0.5)
    scores = low_back(scores)
    scores = jnp.where(allowed[:, None, None, :], scores, -jnp.inf)
    weights_soft = jax.nn.softmax(scores, axis=-1)
    return jnp.einsum('ihst,ithe->ishe', low(weights_soft), values_in, precision=highest)

def forward(tokens_in, modulate, slab, bias_in, bias_out, allowed):
    local_heads = HEADS // HEAD_GROUPS
    qwidth = local_heads * HEAD_DIM
    ffwidth = FF // HEAD_GROUPS
    weights = low(slab)
    w_qkv = weights[:, :, :3 * qwidth]
    w_out = weights[:, :, 3 * qwidth:4 * qwidth]
    w_up = weights[:, :, 4 * qwidth:4 * qwidth + ffwidth]
    w_down = weights[:, :, 4 * qwidth + ffwidth:]
    shift_one = modulate[:, 0][:, None, :]
    scale_one = modulate[:, 1][:, None, :]
    gate_one = modulate[:, 2][:, None, :]
    shift_two = modulate[:, 3][:, None, :]
    scale_two = modulate[:, 4][:, None, :]
    gate_two = modulate[:, 5][:, None, :]
    act_one = low(normalize(tokens_in) * (1.0 + scale_one) + shift_one)
    qkv = jnp.einsum('isd,gde->isge', act_one, w_qkv, precision=highest)
    qkv = qkv.reshape(IMAGES, ALLSLOTS, HEAD_GROUPS, 3, local_heads, HEAD_DIM)
    q_bias = bias_in[:, :HEAD_DIM].reshape(HEAD_GROUPS, local_heads, HEAD_DIM)
    v_bias = bias_in[:, HEAD_DIM:2 * HEAD_DIM].reshape(HEAD_GROUPS, local_heads, HEAD_DIM)
    queries = rounded(qkv[:, :, :, 0] + q_bias).reshape(IMAGES, ALLSLOTS, HEADS, HEAD_DIM)
    keys_all = rounded(qkv[:, :, :, 1]).reshape(IMAGES, ALLSLOTS, HEADS, HEAD_DIM)
    values_all = rounded(qkv[:, :, :, 2] + v_bias).reshape(IMAGES, ALLSLOTS, HEADS, HEAD_DIM)
    groups = IMAGES // IMG_BLOCK
    attended = lax.map(jax.checkpoint(attend_group), (queries.reshape(groups, IMG_BLOCK, ALLSLOTS, HEADS, HEAD_DIM), keys_all.reshape(groups, IMG_BLOCK, ALLSLOTS, HEADS, HEAD_DIM), values_all.reshape(groups, IMG_BLOCK, ALLSLOTS, HEADS, HEAD_DIM), allowed.reshape(groups, IMG_BLOCK, ALLSLOTS)))
    attended = rounded(attended.reshape(IMAGES, ALLSLOTS, HEAD_GROUPS, qwidth))
    attn = low_back(jnp.einsum('isge,gde->isd', attended, w_out, precision=highest) + bias_out[0])
    hidden = tokens_in + gate_one * attn
    act_two = low(normalize(hidden) * (1.0 + scale_two) + shift_two)
    up_bias = bias_in[:, 2 * HEAD_DIM:].reshape(HEAD_GROUPS, ffwidth)
    upper = low_back(jnp.einsum('isd,gdf->isgf', act_two, w_up, precision=highest) + up_bias)
    activated = low(jax.nn.gelu(upper, approximate=True))
    mlp = low_back(jnp.einsum('isgf,gdf->isd', activated, w_down, precision=highest) + bias_out[1])
    result = hidden + gate_two * mlp
    return result * allowed.astype(jnp.float32)[:, :, None]

def reference(tokens, cotangent, modulation, counts, master, left_stat, right_stat, left_root, right_root, bias_in, bias_in_sq, bias_out, bias_out_sq):
    slot_index = jnp.arange(ALLSLOTS) % SLOTS
    range_index = jnp.arange(ALLSLOTS) // SLOTS
    allowed = slot_index[None, :] < counts[:, range_index]
    slab = tiles_to_slab(master)
    result, pullback = jax.vjp(partial(forward, allowed=allowed), tokens.astype(jnp.float32), modulation, slab, bias_in, bias_out)
    grad_tokens, grad_modulation, grad_slab, in_bias_grad, out_bias_grad = pullback(cotangent.astype(jnp.float32))
    weight_grad = slab_to_tiles(grad_slab)
    left_new = decay_rate * left_stat + (1.0 - decay_rate) * jnp.einsum('kab,kcb->kac', weight_grad, weight_grad, precision=highest)
    right_new = decay_rate * right_stat + (1.0 - decay_rate) * jnp.einsum('kba,kbc->kac', weight_grad, weight_grad, precision=highest)
    stepped = jnp.einsum('kab,kbc->kac', left_root, weight_grad, precision=highest)
    stepped = jnp.einsum('kab,kbc->kac', stepped, right_root, precision=highest)
    master_new = master - weight_rate * stepped
    in_bias_sq_new = decay_rate * bias_in_sq + (1.0 - decay_rate) * in_bias_grad * in_bias_grad
    in_bias_new = bias_in - bias_rate * in_bias_grad / (jnp.sqrt(in_bias_sq_new) + root_epsilon)
    out_bias_sq_new = decay_rate * bias_out_sq + (1.0 - decay_rate) * out_bias_grad * out_bias_grad
    out_bias_new = bias_out - bias_rate * out_bias_grad / (jnp.sqrt(out_bias_sq_new) + root_epsilon)
    return (result.astype(jnp.bfloat16), grad_tokens.astype(jnp.bfloat16), grad_modulation, weight_grad, left_new, right_new, master_new, in_bias_grad, in_bias_sq_new, in_bias_new, out_bias_grad, out_bias_sq_new, out_bias_new)
```

```python
import jax
import jax.numpy as jnp
from jax import lax
from jax.sharding import Mesh, PartitionSpec as P

HEADS = 16
HEAD_DIM = 72
FF = 4608
KEPT = 128

norm_epsilon = 1e-06
decay_rate = 0.5
weight_rate = 0.3
bias_rate = 0.1
root_epsilon = 1e-08
score_scale = HEAD_DIM ** (-0.5)
bf16 = jnp.bfloat16
f32 = jnp.float32
CORE_SWAP = [(0, 1), (1, 0)]


def normalize(values):
    center = jnp.mean(values, -1, keepdims=True)
    centered = values - center
    inverse = lax.rsqrt(jnp.mean(centered * centered, -1, keepdims=True) + norm_epsilon)
    return (centered * inverse, inverse)


def norm_back(grad_in, normed, inverse):
    inner = jnp.mean(grad_in * normed, -1, keepdims=True)
    return inverse * (grad_in - jnp.mean(grad_in, -1, keepdims=True) - normed * inner)


def smooth(values):
    return jax.nn.gelu(values, approximate=True)


def dot(a, b):
    return lax.dot_general(a, b, (((1,), (0,)), ((), ())), preferred_element_type=f32)


def dot_t(a, b):
    return lax.dot_general(a, b, (((1,), (1,)), ((), ())), preferred_element_type=f32)


def t_dot(a, b):
    return lax.dot_general(a, b, (((0,), (0,)), ((), ())), preferred_element_type=f32)


def over_core(values):
    return lax.ppermute(values, "core", CORE_SWAP)


def over_head(values, offset):
    return lax.ppermute(values, "head", [(i, i ^ offset) for i in range(4)])


def over_sup(values, offset):
    return lax.ppermute(values, "sup", [(i, i ^ offset) for i in range(4)])


def columns_of(tiles, picks):
    return jnp.concatenate([tiles[k] for k in picks], 1)


def attn_half(tiles, half):
    return jnp.concatenate([lax.dynamic_index_in_dim(tiles, 2 * k + half, 0, False) for k in range(4)], 1)


def mlp_half(tiles, half):
    return jnp.concatenate(
        [lax.dynamic_index_in_dim(tiles, 8 + 8 * w + 4 * half + k, 0, False) for w in range(2) for k in range(4)], 1
    )


def gather_sup(block, place):
    pieces = jnp.stack([block] + [over_sup(block, k) for k in (1, 2, 3)])
    return pieces[jnp.arange(4) ^ place].reshape(4 * block.shape[0], block.shape[1])


def scatter_sup(blocks, place):
    blocks = blocks.reshape(4, -1, blocks.shape[-1])
    total = lax.dynamic_index_in_dim(blocks, place, 0, False).astype(f32)
    for k in (1, 2, 3):
        total += over_sup(lax.dynamic_index_in_dim(blocks, place ^ k, 0, False), k).astype(f32)
    return total


def weights_of(master, place, core):
    tiles = master.astype(bf16)
    if master.shape[0] == 24:
        out = []
        for half_of in (attn_half, mlp_half):
            mine = half_of(tiles, core)
            got = over_core(half_of(tiles, 1 - core))
            block = jnp.concatenate([jnp.where(core == 0, mine, got), jnp.where(core == 0, got, mine)], 0)
            far = over_head(block, 2)
            out.append((gather_sup(block, place), gather_sup(far, place)))
        return out
    tiles = lax.all_gather(tiles, ("sup", "core"), axis=0, tiled=True)
    side = tiles.shape[1]
    slab = tiles.reshape(8, 24, side, side).transpose(1, 0, 2, 3).reshape(24, 8 * side, side)
    out = []
    for half_of in (attn_half, mlp_half):
        block = half_of(slab, core)
        out.append((block, over_head(block, 2)))
    return out


def tiles_of(block):
    side = block.shape[0]
    return block.reshape(side, -1, side).transpose(1, 0, 2)


def grads_of(attn_near, attn_far, mlp_near, mlp_far, tiles_dev, place, core):
    if tiles_dev == 24:
        out = []
        for near, far in ((attn_near, attn_far), (mlp_near, mlp_far)):
            near = scatter_sup(near.astype(bf16), place)
            far = scatter_sup(far.astype(bf16), place)
            total = (near + over_head(far.astype(bf16), 2).astype(f32)).reshape(2, -1, near.shape[-1])
            mine = lax.dynamic_index_in_dim(total, core, 0, False)
            got = over_core(lax.dynamic_index_in_dim(total, 1 - core, 0, False).astype(bf16)).astype(f32)
            out.append(tiles_of(jnp.where(core == 0, mine, got)))
            out.append(tiles_of(jnp.where(core == 0, got, mine)))
        a0, a1, m0, m1 = out
    else:
        out = []
        for near, far in ((attn_near, attn_far), (mlp_near, mlp_far)):
            near = (near + over_head(far.astype(bf16), 2).astype(f32)).astype(bf16)
            both = lax.all_gather(near, "core").astype(f32)
            for part in (both[0], both[1]):
                side = part.shape[0] // 8
                out.append(part.reshape(8, side, -1, side).transpose(2, 0, 1, 3))
        a0, a1, m0, m1 = out
    attn = jnp.stack([a0, a1], 1)
    attn = attn.reshape((8,) + attn.shape[2:])
    mlp = jnp.concatenate([m0[:4], m1[:4], m0[4:], m1[4:]], 0)
    tiles = jnp.concatenate([attn, mlp], 0)
    if tiles_dev == 24:
        return tiles
    side = tiles.shape[-1]
    tiles = tiles.transpose(1, 0, 2, 3).reshape(192, side, side)
    tiles = lax.psum_scatter(tiles, "sup", scatter_dimension=0, tiled=True)
    return lax.dynamic_slice_in_dim(tiles, core * tiles_dev, tiles_dev, 0)


def sum_rows(own, other, pair):
    total = own.astype(f32) + over_core(other.astype(bf16)).astype(f32)
    half = total.shape[0] // 2
    keep = lax.dynamic_slice_in_dim(total, pair * half, half, 0)
    send = lax.dynamic_slice_in_dim(total, (1 - pair) * half, half, 0).astype(bf16)
    return keep + over_head(send, 1).astype(f32)


def share_rows(mine, pair):
    got = over_head(mine, 1)
    own = jnp.where(pair == 0, jnp.concatenate([mine, got], 0), jnp.concatenate([got, mine], 0))
    return jnp.concatenate([own, over_core(own)], 0)


def attend(q, k, v):
    scores = jnp.einsum("ishe,ithe->ihst", q, k, preferred_element_type=f32) * score_scale
    return jax.nn.softmax(scores, -1)


def on_device(
    tokens,
    cotangent,
    modulation,
    counts,
    master,
    left_stat,
    right_stat,
    left_root,
    right_root,
    bias_in,
    bias_in_sq,
    bias_out,
    bias_out_sq,
):
    images, slots, width = tokens.shape
    place = lax.axis_index("sup")
    core = lax.axis_index("core")
    head = lax.axis_index("head")
    pair = head % 2
    number = images // 2
    first = (head // 2) * number
    rows = number * KEPT
    half = rows // 2
    parts = half // (KEPT // 2)
    (attn_near, attn_far), (mlp_near, mlp_far) = weights_of(master, place, core)

    per_range = slots // counts.shape[1]
    start = jnp.cumsum(counts, 1) - counts
    slot = jnp.arange(per_range)[None, None, :]
    target = jnp.where(slot < counts[:, :, None], start[:, :, None] + slot, -1).reshape(images, 1, slots)
    select = (target == jnp.arange(KEPT)[None, :, None]).astype(bf16)
    select_own = lax.dynamic_slice_in_dim(select, first, number, 0)

    def compact(values):
        values = lax.dynamic_slice_in_dim(values, first, number, 0)
        return jnp.einsum("irs,isd->ird", select_own, values, preferred_element_type=f32).astype(bf16).reshape(rows, width)

    def expand(values):
        values = values.reshape(images, KEPT, width)
        return jnp.einsum("irs,ird->isd", select, values, preferred_element_type=f32).astype(bf16)

    x_own = compact(tokens)
    g_own = compact(cotangent)
    mod_own = lax.dynamic_slice_in_dim(modulation, first, number, 0)
    x_all = jnp.concatenate([x_own, over_core(x_own)], 0)
    g_all = jnp.concatenate([g_own, over_core(g_own)], 0)
    mod_all = jnp.concatenate([mod_own, over_core(mod_own)], 0)
    x_mine = lax.dynamic_slice_in_dim(x_own, pair * half, half, 0).astype(f32)
    g_mine = lax.dynamic_slice_in_dim(g_own, pair * half, half, 0).astype(f32)
    mod_mine = lax.dynamic_slice_in_dim(
        jnp.repeat(mod_own, 2, axis=0), pair * parts, parts, 0
    )

    def vec_all(index):
        return jnp.repeat(mod_all[:, index], KEPT, axis=0)

    def vec_mine(index):
        return jnp.repeat(mod_mine[:, index], KEPT // 2, axis=0)

    def part_sums(values):
        return jnp.sum(values.reshape(parts, KEPT // 2, width), 1)

    def my_heads(values):
        return lax.dynamic_slice_in_dim(values, 2 * core, 2, 0)

    bias_near = my_heads(bias_in)
    bias_far = my_heads(over_head(bias_in, 2))

    normed_one, _ = normalize(x_all.astype(f32))
    act_one = (normed_one * (1.0 + vec_all(1)) + vec_all(0)).astype(bf16)
    number_all = 2 * number
    saved = []
    attn_own = 0.0
    for weights, bias in ((attn_near, bias_near), (attn_far, bias_far)):
        qkv = dot(act_one, weights[:, :432])
        q = (qkv[:, :144] + bias[:, :HEAD_DIM].reshape(144)).astype(bf16)
        k = qkv[:, 144:288].astype(bf16)
        v = (qkv[:, 288:] + bias[:, HEAD_DIM : 2 * HEAD_DIM].reshape(144)).astype(bf16)
        q, k, v = (t.reshape(number_all, KEPT, 2, HEAD_DIM) for t in (q, k, v))
        p = attend(q, k, v)
        o = jnp.einsum("ihst,ithe->ishe", p.astype(bf16), v, preferred_element_type=f32)
        o = o.astype(bf16).reshape(2 * rows, 144)
        saved.append((q, k, v, p, o))
        attn_own = attn_own + dot_t(o, weights[:, 432:])
    attn = sum_rows(attn_own[:rows], attn_own[rows:], pair) + bias_out[0]
    hidden = x_mine + vec_mine(2) * attn
    normed_two, inverse_two = normalize(hidden)
    act_two = share_rows((normed_two * (1.0 + vec_mine(4)) + vec_mine(3)).astype(bf16), pair)

    grad_mlp = (vec_all(5) * g_all.astype(f32)).astype(bf16)
    mlp_sum = 0.0
    db_sum = 0.0
    mlp_grads = []
    up_sums = []
    for weights, bias in ((mlp_near, bias_near), (mlp_far, bias_far)):
        w_up, w_down = weights[:, :576], weights[:, 576:]
        upper = dot(act_two, w_up) + bias[:, 2 * HEAD_DIM :].reshape(576)
        activated, pull = jax.vjp(smooth, upper)
        activated = activated.astype(bf16)
        (grad_upper,) = pull(dot(grad_mlp, w_down))
        grad_upper = grad_upper.astype(bf16)
        db_sum = db_sum + dot_t(grad_upper, w_up)
        mlp_sum = mlp_sum + dot_t(activated, w_down)
        mlp_grads.append(jnp.concatenate([t_dot(act_two, grad_upper), t_dot(grad_mlp, activated)], 1))
        up_sums.append(jnp.sum(grad_upper.astype(f32), 0))
    db = sum_rows(db_sum[:rows], db_sum[rows:], pair)
    mlp = sum_rows(mlp_sum[:rows], mlp_sum[rows:], pair) + bias_out[1]
    output = (hidden + vec_mine(5) * mlp).astype(bf16)
    grad_hidden = g_mine + norm_back(db * (1.0 + vec_mine(4)), normed_two, inverse_two)
    grad_attn = (vec_mine(2) * grad_hidden).astype(bf16)
    grad_attn_all = share_rows(grad_attn, pair)
    da_sum = 0.0
    attn_grads = []
    qv_sums = []
    for weights, (q, k, v, p, o) in zip((attn_near, attn_far), saved):
        do = dot(grad_attn_all, weights[:, 432:]).astype(bf16).reshape(q.shape)
        dp = jnp.einsum("ishe,ithe->ihst", do, v, preferred_element_type=f32)
        ds = (p * (dp - jnp.sum(p * dp, -1, keepdims=True))).astype(bf16)
        dq = jnp.einsum("ihst,ithe->ishe", ds, k, preferred_element_type=f32) * score_scale
        dk = jnp.einsum("ihst,ishe->ithe", ds, q, preferred_element_type=f32) * score_scale
        dv = jnp.einsum("ihst,ishe->ithe", p.astype(bf16), do, preferred_element_type=f32)
        dqkv = jnp.concatenate([t.astype(bf16).reshape(2 * rows, 144) for t in (dq, dk, dv)], 1)
        da_sum = da_sum + dot_t(dqkv, weights[:, :432])
        attn_grads.append(jnp.concatenate([t_dot(act_one, dqkv), t_dot(grad_attn_all, o)], 1))
        sums = jnp.sum(dqkv.astype(f32), 0)
        qv_sums.append((sums[:144], sums[288:]))
    da = sum_rows(da_sum[:rows], da_sum[rows:], pair)
    normed_one, inverse_one = normalize(x_mine)
    grad_tokens = (grad_hidden + norm_back(da * (1.0 + vec_mine(1)), normed_one, inverse_one)).astype(bf16)
    sums = jnp.stack(
        [
            part_sums(da),
            part_sums(da * normed_one),
            part_sums(grad_hidden * attn),
            part_sums(db),
            part_sums(db * normed_two),
            part_sums(g_mine * mlp),
        ],
        1,
    )
    sums = lax.all_gather(sums, "head", axis=0, tiled=True).reshape(images, 2, 6, width).sum(1)
    quarter = width // 4
    grad_modulation = lax.dynamic_slice_in_dim(sums, head * quarter, quarter, 2)
    output = expand(lax.all_gather(output, "head", axis=0, tiled=True))
    grad_tokens = expand(lax.all_gather(grad_tokens, "head", axis=0, tiled=True))

    def bias_block(index):
        q, v = qv_sums[index]
        return jnp.concatenate([q.reshape(2, HEAD_DIM), v.reshape(2, HEAD_DIM), up_sums[index].reshape(2, -1)], 1)

    in_part = jnp.zeros((HEADS, bias_in.shape[1]), f32)
    in_part = lax.dynamic_update_slice_in_dim(in_part, bias_block(0), head * 4 + 2 * core, 0)
    in_part = lax.dynamic_update_slice_in_dim(in_part, bias_block(1), (head ^ 2) * 4 + 2 * core, 0)
    grad_mlp_mine = (vec_mine(5) * g_mine).astype(bf16).astype(f32)
    out_part = jnp.stack([jnp.sum(grad_attn.astype(f32), 0), jnp.sum(grad_mlp_mine, 0)], 0)
    small = jnp.concatenate([in_part.reshape(-1), out_part.reshape(-1)])
    small = lax.psum(small, ("sup", "core", "head"))
    in_bias_grad = lax.dynamic_slice_in_dim(small[: in_part.size].reshape(in_part.shape), head * 4, 4, 0)
    out_bias_grad = small[in_part.size :].reshape(bias_out.shape)

    weight_grad = grads_of(
        attn_grads[0], attn_grads[1], mlp_grads[0], mlp_grads[1], master.shape[0], place, core
    )
    low = weight_grad.astype(bf16)
    left_new = decay_rate * left_stat + (1.0 - decay_rate) * jnp.einsum(
        "kab,kcb->kac", low, low, preferred_element_type=f32
    )
    right_new = decay_rate * right_stat + (1.0 - decay_rate) * jnp.einsum(
        "kba,kbc->kac", low, low, preferred_element_type=f32
    )
    stepped = jnp.einsum("kab,kbc->kac", left_root.astype(bf16), low, preferred_element_type=f32)
    stepped = jnp.einsum("kab,kbc->kac", stepped.astype(bf16), right_root.astype(bf16), preferred_element_type=f32)
    master_new = master - weight_rate * stepped
    in_bias_sq_new = decay_rate * bias_in_sq + (1.0 - decay_rate) * in_bias_grad * in_bias_grad
    in_bias_new = bias_in - bias_rate * in_bias_grad / (jnp.sqrt(in_bias_sq_new) + root_epsilon)
    out_bias_sq_new = decay_rate * bias_out_sq + (1.0 - decay_rate) * out_bias_grad * out_bias_grad
    out_bias_new = bias_out - bias_rate * out_bias_grad / (jnp.sqrt(out_bias_sq_new) + root_epsilon)
    return (
        output,
        grad_tokens,
        grad_modulation,
        weight_grad,
        left_new,
        right_new,
        master_new,
        in_bias_grad,
        in_bias_sq_new,
        in_bias_new,
        out_bias_grad,
        out_bias_sq_new,
        out_bias_new,
    )


def solution(mesh):
    devices = mesh.devices
    inner = Mesh(
        devices.reshape(devices.shape[0] // 2, 2, devices.shape[1]), ("sup", "core", "head")
    )
    seq = ("sup", "core")
    tile = P(("sup", "core", "head"), None, None)
    return jax.shard_map(
        on_device,
        mesh=inner,
        in_specs=(
            P(seq, None, None),
            P(seq, None, None),
            P(seq, None, None),
            P(seq, None),
            tile,
            tile,
            tile,
            tile,
            tile,
            P("head", None),
            P("head", None),
            P(),
            P(),
        ),
        out_specs=(
            P(seq, None, None),
            P(seq, None, None),
            P(seq, None, "head"),
            tile,
            tile,
            tile,
            tile,
            P("head", None),
            P("head", None),
            P("head", None),
            P(),
            P(),
            P(),
        ),
        check_vma=False,
    )
```

```python
import functools

import jax
import jax.numpy as jnp
from jax import lax
from jax.experimental import pallas as pl
from jax.experimental.pallas import tpu as pltpu
from jax.sharding import Mesh, PartitionSpec as P

HEADS = 16
HEAD_DIM = 72
KEPT = 128
SIDE = 144
RANGES = 8
SLOTS = 24
WIDTH = 1152
QKV = 432
PAIRED = 144
UP = 576

norm_epsilon = 1e-06
decay_rate = 0.5
weight_rate = 0.3
bias_rate = 0.1
root_epsilon = 1e-08
score_scale = HEAD_DIM ** (-0.5)
bf16 = jnp.bfloat16
f32 = jnp.float32
CORE_SWAP = [(0, 1), (1, 0)]

SUP, ORDER, CORE, HEAD, HALF, FIRST = range(6)
ANY = pl.BlockSpec(memory_space=pl.ANY)
VMEM = pl.BlockSpec(memory_space=pltpu.VMEM)
SMEM = pl.BlockSpec(memory_space=pltpu.SMEM)


def dot(a, b):
    return lax.dot_general(a, b, (((1,), (0,)), ((), ())), preferred_element_type=f32)


def dot_t(a, b):
    return lax.dot_general(a, b, (((1,), (1,)), ((), ())), preferred_element_type=f32)


def t_dot(a, b):
    return lax.dot_general(a, b, (((0,), (0,)), ((), ())), preferred_element_type=f32)


def normalize(values):
    center = jnp.mean(values, -1, keepdims=True)
    centered = values - center
    inverse = lax.rsqrt(jnp.mean(centered * centered, -1, keepdims=True) + norm_epsilon)
    return (centered * inverse, inverse)


def norm_back(grad_in, normed, inverse):
    inner = jnp.mean(grad_in * normed, -1, keepdims=True)
    return inverse * (grad_in - jnp.mean(grad_in, -1, keepdims=True) - normed * inner)


def over_core(values):
    return lax.ppermute(values, "core", CORE_SWAP)


def over_head(values, offset):
    return lax.ppermute(values, "head", [(i, i ^ offset) for i in range(4)])


def over_sup(values, offset):
    return lax.ppermute(values, "sup", [(i, i ^ offset) for i in range(4)])


def shaped(shape, dtype):
    return jax.ShapeDtypeStruct(shape, dtype)


def call(body, name, inputs, outputs, scratch=(), flops=0, aliases=None, vmem=56):
    arrays = [array for array, _ in inputs]
    shapes = [shaped(shape, dtype) for shape, dtype, _ in outputs]
    size = sum(a.size * a.dtype.itemsize for a in arrays + shapes)
    return pl.pallas_call(
        body,
        name=name,
        out_shape=shapes,
        in_specs=[spec for _, spec in inputs],
        out_specs=[spec for _, _, spec in outputs],
        scratch_shapes=list(scratch),
        input_output_aliases=aliases or {},
        cost_estimate=pl.CostEstimate(flops=flops, bytes_accessed=size, transcendentals=0),
        compiler_params=pltpu.CompilerParams(vmem_limit_bytes=vmem * 1024 * 1024),
    )(*arrays)


def started(copies):
    for copy in copies:
        copy.start()
    return copies


def finish(copies):
    for copy in copies:
        copy.wait()


def pack_attn(info, master, mine, other, held, sem):
    finish(started([pltpu.make_async_copy(master.at[pl.ds(0, 8)], held, sem)]))
    core = info[CORE]
    for out, half in ((mine, core), (other, 1 - core)):
        out[...] = jnp.concatenate([held[2 * k + half].astype(bf16) for k in range(4)], 1)


def pack_mlp(info, master, mine, other, held, sem):
    finish(started([pltpu.make_async_copy(master.at[pl.ds(8, 16)], held, sem)]))
    core = info[CORE]
    for out, half in ((mine, core), (other, 1 - core)):
        out[...] = jnp.concatenate(
            [held[8 * w + 4 * half + k].astype(bf16) for w in range(2) for k in range(4)], 1
        )


def pack(info, master):
    held = lambda count: [pltpu.VMEM((count, SIDE, SIDE), f32), pltpu.SemaphoreType.DMA]
    outs = lambda width: [((SIDE, width), bf16, VMEM)] * 2
    attn = call(pack_attn, "pack_attn", [(info, SMEM), (master, ANY)], outs(4 * SIDE), held(8))
    mlp = call(pack_mlp, "pack_mlp", [(info, SMEM), (master, ANY)], outs(8 * SIDE), held(16))
    return attn, mlp


def piece_copies(info, pieces, target, sems):
    copies = []
    for k in range(4):
        for j in range(2):
            row = ((info[SUP] ^ k) * 2 + (info[ORDER] ^ j)) * SIDE
            copies.append(
                pltpu.make_async_copy(
                    pieces[k].at[pl.ds(j * SIDE, SIDE)],
                    target.at[pl.ds(pl.multiple_of(row, 16), SIDE)],
                    sems.at[2 * k + j],
                )
            )
    return copies


def gather_pieces(block):
    return [block] + [over_sup(block, k) for k in (1, 2, 3)]


def weight_pieces(info, master, core):
    out = []
    if master.shape[0] == 24:
        for mine, other in pack(info, master):
            block = jnp.concatenate([mine, over_core(other)], 0)
            out.append(block)
        attn, mlp = out
        attn_far = over_head(attn, 2)
        near = gather_pieces(attn)
        far = gather_pieces(attn_far)
        mlp_far = over_head(mlp, 2)
        return (near, far), (gather_pieces(mlp), gather_pieces(mlp_far))
    tiles = lax.all_gather(master.astype(bf16), ("sup", "core"), axis=0, tiled=True)
    slab = tiles.reshape(8, 24, SIDE, SIDE).transpose(1, 0, 2, 3).reshape(24, 8 * SIDE, SIDE)
    take = lambda k: lax.dynamic_index_in_dim(slab, k, 0, False)
    attn = jnp.concatenate([take(2 * k + core) for k in range(4)], 1)
    mlp = jnp.concatenate([take(8 + 8 * w + 4 * core + k) for w in range(2) for k in range(4)], 1)
    for block in (attn, mlp):
        out.append(tuple([part[288 * k : 288 * k + 288] for k in range(4)] for part in (block, over_head(block, 2))))
    return out


def kept_target(counts, image, slot):
    target = jnp.full(slot.shape, -1, jnp.int32)
    start = 0
    for s in range(RANGES):
        number = counts[image, s]
        place = slot - s * SLOTS
        target = jnp.where((place >= 0) & (place < number), place + start, target)
        start = start + number
    return target


def rows_body(number, info, counts, tokens, cotangent, modulation, act, dm, x_mine, g_mine, tok, cot, x_own, g_own, sems):
    first = info[FIRST]
    copies = started(
        [
            pltpu.make_async_copy(tokens.at[pl.ds(first, number)], tok, sems.at[0]),
            pltpu.make_async_copy(cotangent.at[pl.ds(first, number)], cot, sems.at[1]),
        ]
    )
    finish(copies)
    slots = tok.shape[1]
    for i in range(number):
        image = first + i
        target = kept_target(counts, image, lax.broadcasted_iota(jnp.int32, (1, slots), 1))
        select = (target == lax.broadcasted_iota(jnp.int32, (KEPT, slots), 0)).astype(f32).astype(bf16)
        rows = pl.ds(i * KEPT, KEPT)
        mod = modulation[image]
        x = dot(select, tok[i])
        x_own[rows, :] = x.astype(bf16)
        normed, _ = normalize(x)
        act[rows, :] = (normed * (1.0 + mod[1:2]) + mod[0:1]).astype(bf16)
        g = dot(select, cot[i])
        g_own[rows, :] = g.astype(bf16)
        dm[rows, :] = (mod[5:6] * g).astype(bf16)
    half = x_mine.shape[0]
    mine = pl.ds(pl.multiple_of(info[HALF] * half, 64), half)
    x_mine[...] = x_own[mine, :]
    g_mine[...] = g_own[mine, :]


def kept_rows(info, counts, tokens, cotangent, modulation, number):
    slots = tokens.shape[1]
    rows = number * KEPT
    half = rows // 2
    return call(
        functools.partial(rows_body, number),
        "kept_rows",
        [(info, SMEM), (counts, SMEM), (tokens, ANY), (cotangent, ANY), (modulation, VMEM)],
        [((rows, WIDTH), bf16, VMEM)] * 2 + [((half, WIDTH), bf16, VMEM)] * 2,
        [pltpu.VMEM((number, slots, WIDTH), bf16)] * 2
        + [pltpu.VMEM((rows, WIDTH), bf16)] * 2
        + [pltpu.SemaphoreType.DMA((2,))],
        flops=4 * rows * slots * WIDTH,
    )


def expand_body(images, extra, info, counts, p0, p1, p2, p3, out, *rest):
    if extra:
        sums, held, sems = rest
    else:
        held, sems = rest
    pieces = (p0, p1, p2, p3)
    size = p0.shape[0]
    half = size - extra
    copies = started(
        [
            pltpu.make_async_copy(
                pieces[k], held.at[pl.ds(pl.multiple_of((info[HEAD] ^ k) * size, 16), size)], sems.at[k]
            )
            for k in range(4)
        ]
    )
    finish(copies)
    slots = out.shape[1]
    parts = half // 64
    for i in range(images):
        slot = lax.broadcasted_iota(jnp.int32, (slots, KEPT), 0)
        target = kept_target(counts, i, slot)
        spread = (target == lax.broadcasted_iota(jnp.int32, (slots, KEPT), 1)).astype(f32).astype(bf16)
        chunks = []
        for chunk in (2 * i, 2 * i + 1):
            row = (chunk // parts) * size + (chunk % parts) * 64
            chunks.append(held[row : row + 64, :])
        out[i] = dot(spread, jnp.concatenate(chunks, 0)).astype(bf16)
        if extra:
            total = jnp.zeros((6, WIDTH), f32)
            for chunk in (2 * i, 2 * i + 1):
                base = (chunk // parts) * size + half
                block = held[base : base + extra, :].astype(f32)
                at = (chunk % parts) * 6
                total = total + block[at : at + 6] + block[extra // 2 + at : extra // 2 + at + 6]
            quarter = WIDTH // 4
            picked = total[:, :quarter]
            for k in range(1, 4):
                picked = jnp.where(info[HEAD] == k, total[:, k * quarter : (k + 1) * quarter], picked)
            sums[i] = picked


def expand(info, counts, mine, images, slots, extra):
    pieces = [mine] + [over_head(mine, k) for k in (1, 2, 3)]
    outs = [((images, slots, WIDTH), bf16, VMEM)]
    if extra:
        outs.append(((images, 6, WIDTH // 4), f32, VMEM))
    return call(
        functools.partial(expand_body, images, extra),
        "expand_rows",
        [(info, SMEM), (counts, SMEM)] + [(p, ANY) for p in pieces],
        outs,
        [pltpu.VMEM((4 * mine.shape[0], WIDTH), bf16), pltpu.SemaphoreType.DMA((4,))],
        flops=2 * images * slots * KEPT * WIDTH,
    )


def first_sum_body(mine, got, out):
    out[...] = (mine[...].astype(f32) + got[...].astype(f32)).astype(bf16)


def sum_rows(parts):
    own_send, own_keep, other_send, other_keep = parts
    got = over_core(other_send)
    (send,) = call(first_sum_body, "first_sum", [(own_send, VMEM), (got, VMEM)], [(own_send.shape, bf16, VMEM)])
    return own_keep, over_core(other_keep), over_head(send, 1)


def three(terms):
    return terms[0][...].astype(f32) + terms[1][...].astype(f32) + terms[2][...].astype(f32)


def share_rows(mine):
    far = over_head(mine, 1)
    return mine, far, over_core(mine), over_core(far)


def share_copies(info, pieces, target, sems):
    half = pieces[0].shape[0]
    copies = []
    for k in range(4):
        row = (k // 2) * 2 * half + (info[HALF] ^ (k % 2)) * half
        copies.append(
            pltpu.make_async_copy(pieces[k], target.at[pl.ds(pl.multiple_of(row, 64), half)], sems.at[k])
        )
    return copies


def split_halves(info, full, outs):
    half = outs[0].shape[0]
    for k in range(2):
        send = pl.ds(pl.multiple_of((2 * k + 1 - info[HALF]) * half, 64), half)
        keep = pl.ds(pl.multiple_of((2 * k + info[HALF]) * half, 64), half)
        outs[2 * k][...] = full[send, :].astype(bf16)
        outs[2 * k + 1][...] = full[keep, :].astype(bf16)


def head_mask():
    return lax.broadcasted_iota(jnp.int32, (KEPT, PAIRED), 1) < HEAD_DIM


def split_heads(values, mask):
    zero = jnp.zeros_like(values)
    return jnp.concatenate([jnp.where(mask, values, zero), jnp.where(mask, zero, values)], 0)


def attend_body(number, info, act_own, act_other, bias, w0, w1, w2, w3, weights, qkv, probs, mixed, sems):
    finish(started(piece_copies(info, (w0, w1, w2, w3), weights, sems)))
    mask = head_mask()
    for i in range(2 * number):
        act = act_own if i < number else act_other
        here = slice((i % number) * KEPT, (i % number + 1) * KEPT)
        rows = slice(i * KEPT, (i + 1) * KEPT)
        three_parts = (dot(act[here, :], weights[:, :QKV]) + bias[...]).astype(bf16)
        qkv[rows, :] = three_parts
        q, k, v = (three_parts[:, j * PAIRED : (j + 1) * PAIRED] for j in range(3))
        scores = dot_t(split_heads(q, mask), k) * score_scale
        raised = jnp.exp(scores - jnp.max(scores, -1, keepdims=True))
        p = raised / jnp.sum(raised, -1, keepdims=True)
        probs[i] = p
        low = p.astype(bf16)
        wide = jnp.concatenate([low[:KEPT], low[KEPT:]], 1)
        mixed[rows, :] = dot(wide, split_heads(v, mask)).astype(bf16)


def attend(info, act_own, act_other, bias, pieces, number):
    rows = 2 * number * KEPT
    return call(
        functools.partial(attend_body, number),
        "attend",
        [(info, SMEM), (act_own, VMEM), (act_other, VMEM), (bias, VMEM)] + [(p, ANY) for p in pieces],
        [
            ((WIDTH, QKV + PAIRED), bf16, VMEM),
            ((rows, QKV), bf16, VMEM),
            ((2 * number, 2 * KEPT, KEPT), f32, VMEM),
            ((rows, PAIRED), bf16, VMEM),
        ],
        [pltpu.SemaphoreType.DMA((8,))],
        flops=2 * rows * WIDTH * QKV,
    )


def project_body(info, near_w, far_w, near, far, *rest):
    outs, full = rest[:4], rest[4]
    wa = near_w[:, QKV:]
    wb = far_w[:, QKV:]
    for i in range(near.shape[0] // 256):
        rows = slice(i * 256, (i + 1) * 256)
        full[rows, :] = (dot_t(near[rows, :], wa) + dot_t(far[rows, :], wb)).astype(bf16)
    split_halves(info, full, outs)


def halves_of(rows):
    return [((rows // 4, WIDTH), bf16, VMEM)] * 4


def project(info, near_w, far_w, near, far):
    rows = near.shape[0]
    return call(
        project_body,
        "project",
        [(info, SMEM), (near_w, VMEM), (far_w, VMEM), (near, VMEM), (far, VMEM)],
        halves_of(rows),
        [pltpu.VMEM((rows, WIDTH), bf16)],
        flops=4 * rows * WIDTH * PAIRED,
    )


def middle_body(number, info, modulation, bias_out, x_mine, t0, t1, t2, hidden, attn, act):
    half = x_mine.shape[0]
    parts = half // 64
    for t in range(parts):
        rows = slice(t * 64, (t + 1) * 64)
        mod = modulation[info[FIRST] + (info[HALF] * parts + t) // 2]
        a = t0[rows, :].astype(f32) + t1[rows, :].astype(f32) + t2[rows, :].astype(f32) + bias_out[0:1, :]
        h = x_mine[rows, :].astype(f32) + mod[2:3] * a
        attn[rows, :] = a
        hidden[rows, :] = h
        normed, _ = normalize(h)
        act[rows, :] = (normed * (1.0 + mod[4:5]) + mod[3:4]).astype(bf16)


def middle(info, modulation, bias_out, x_mine, terms, number):
    half = x_mine.shape[0]
    return call(
        functools.partial(middle_body, number),
        "middle",
        [(info, SMEM), (modulation, VMEM), (bias_out, VMEM), (x_mine, VMEM)] + [(t, VMEM) for t in terms],
        [((half, WIDTH), f32, VMEM)] * 2 + [((half, WIDTH), bf16, VMEM)],
    )


def mlp_weights_body(info, *refs):
    pieces, (up, down, near, far, sems) = refs[:8], refs[8:]
    copies = started(piece_copies(info, pieces[:4], near, sems.at[0]))
    copies += started(piece_copies(info, pieces[4:], far, sems.at[1]))
    finish(copies)
    for i in range(8):
        rows = slice(i * SIDE, (i + 1) * SIDE)
        a, b = near[rows, :], far[rows, :]
        up[rows, :] = jnp.concatenate([a[:, :UP], b[:, :UP]], 1)
        down[rows, :] = jnp.concatenate([a[:, UP:], b[:, UP:]], 1)


def mlp_weights(info, near, far):
    square = (WIDTH, 2 * UP)
    return call(
        mlp_weights_body,
        "mlp_weights",
        [(info, SMEM)] + [(p, ANY) for p in near + far],
        [(square, bf16, VMEM)] * 2,
        [pltpu.VMEM(square, bf16)] * 2 + [pltpu.SemaphoreType.DMA((2, 8))],
    )


def smooth_both(u):
    c = 0.7978845608028654
    cube = 0.044715
    square = u * u
    t = jnp.tanh(c * u * (1.0 + cube * square))
    half_up = 0.5 * (1.0 + t)
    slope = half_up + 0.5 * u * (1.0 - t * t) * (c * (1.0 + 3.0 * cube * square))
    return u * half_up, slope


def mlp_body(number, info, bias, dm_own, dm_other, up, down, s0, s1, s2, s3, *rest):
    act, f, du, g0, g1, g2, g3, db, sems = rest
    finish(started(share_copies(info, (s0, s1, s2, s3), act, sems)))
    for i in range(2 * number):
        rows = slice(i * KEPT, (i + 1) * KEPT)
        here = slice((i % number) * KEPT, (i % number + 1) * KEPT)
        dm = dm_own if i < number else dm_other
        u = dot(act[rows, :], up[...]) + bias[...]
        value, slope = smooth_both(u)
        f[rows, :] = value.astype(bf16)
        low = (dot(dm[here, :], down[...]) * slope).astype(bf16)
        du[rows, :] = low
        db[rows, :] = dot_t(low, up[...]).astype(bf16)
    split_halves(info, db, (g0, g1, g2, g3))


def mlp(info, bias, dm_own, dm_other, up, down, pieces, number):
    rows = 2 * number * KEPT
    full = ((rows, WIDTH), bf16, VMEM)
    return call(
        functools.partial(mlp_body, number),
        "mlp",
        [(info, SMEM), (bias, VMEM), (dm_own, VMEM), (dm_other, VMEM), (up, VMEM), (down, VMEM)]
        + [(p, ANY) for p in pieces],
        [full] * 3 + halves_of(rows),
        [pltpu.VMEM((rows, WIDTH), bf16), pltpu.SemaphoreType.DMA((4,))],
        flops=6 * rows * WIDTH * WIDTH,
    )


def down_body(info, f, down, *rest):
    outs, full = rest[:4], rest[4]
    for i in range(f.shape[0] // 256):
        rows = slice(i * 256, (i + 1) * 256)
        full[rows, :] = dot_t(f[rows, :], down[...]).astype(bf16)
    split_halves(info, full, outs)


def down_rows(info, f, down):
    rows = f.shape[0]
    return call(
        down_body,
        "down",
        [(info, SMEM), (f, VMEM), (down, VMEM)],
        halves_of(rows),
        [pltpu.VMEM((rows, WIDTH), bf16)],
        flops=2 * rows * WIDTH * WIDTH,
    )


def two_rows(values):
    high = values.astype(bf16)
    return [high.astype(f32), values - high.astype(f32)]


def stacked(rows, count):
    width = rows[0].shape[1]
    place = lax.broadcasted_iota(jnp.int32, (count, width), 0)
    out = jnp.zeros((count, width), f32)
    for k, row in enumerate(rows):
        out = jnp.where(place == k, row, out)
    return out


def block_copies(info, full, extra, outs, sems):
    copies = []
    for k in range(4):
        row = pl.multiple_of((info[SUP] ^ k) * 288, 16)
        copies.append(pltpu.make_async_copy(full.at[pl.ds(row, 288)], outs[k].at[pl.ds(0, 288)], sems.at[2 * k]))
        copies.append(pltpu.make_async_copy(extra, outs[k].at[pl.ds(288, 16)], sems.at[2 * k + 1]))
    return copies


def column_sums(ref):
    half = ref.shape[0] // 2
    first = jnp.sum(ref[:half, :].astype(f32), 0, keepdims=True)
    return first + jnp.sum(ref[half:, :].astype(f32), 0, keepdims=True)


def mlp_grads_body(info, act, du, f, dm_own, dm_other, o0, o1, o2, o3, dm, full, extra, sems):
    rows = dm_own.shape[0]
    dm[:rows, :] = dm_own[...]
    dm[rows:, :] = dm_other[...]
    for i in range(3):
        part = slice(i * 384, (i + 1) * 384)
        full[part, :WIDTH] = t_dot(act[:, part], du[...]).astype(bf16)
        full[part, WIDTH:] = t_dot(dm[:, part], f[...]).astype(bf16)
    sums = jnp.concatenate([column_sums(du), column_sums(dm)], 1)
    extra[...] = stacked(two_rows(sums), 16).astype(bf16)
    finish(started(block_copies(info, full, extra, (o0, o1, o2, o3), sems)))


def mlp_grads(info, act, du, f, dm_own, dm_other):
    rows = act.shape[0]
    return call(
        mlp_grads_body,
        "mlp_grads",
        [(info, SMEM), (act, VMEM), (du, VMEM), (f, VMEM), (dm_own, VMEM), (dm_other, VMEM)],
        [((304, 2 * WIDTH), bf16, ANY)] * 4,
        [
            pltpu.VMEM((rows, WIDTH), bf16),
            pltpu.VMEM((WIDTH, 2 * WIDTH), bf16),
            pltpu.VMEM((16, 2 * WIDTH), bf16),
            pltpu.SemaphoreType.DMA((8,)),
        ],
        flops=4 * rows * WIDTH * WIDTH,
    )


def output_body(number, info, modulation, bias_out, hidden, g_mine, t0, t1, t2, out, sums):
    half = hidden.shape[0]
    parts = half // 64
    for t in range(parts):
        rows = slice(t * 64, (t + 1) * 64)
        mod = modulation[info[FIRST] + (info[HALF] * parts + t) // 2]
        m = t0[rows, :].astype(f32) + t1[rows, :].astype(f32) + t2[rows, :].astype(f32) + bias_out[1:2, :]
        out[rows, :] = (hidden[rows, :] + mod[5:6] * m).astype(bf16)
        sums[t : t + 1, :] = jnp.sum(g_mine[rows, :].astype(f32) * m, 0, keepdims=True)


def output_rows(info, modulation, bias_out, hidden, g_mine, terms, number):
    half = hidden.shape[0]
    return call(
        functools.partial(output_body, number),
        "output_rows",
        [(info, SMEM), (modulation, VMEM), (bias_out, VMEM), (hidden, VMEM), (g_mine, VMEM)]
        + [(t, VMEM) for t in terms],
        [((half, WIDTH), bf16, VMEM), ((half // 64, WIDTH), f32, VMEM)],
    )


def back_middle_body(number, info, modulation, hidden, attn, g_mine, t0, t1, t2, dh, dat, sums):
    half = hidden.shape[0]
    parts = half // 64
    for t in range(parts):
        rows = slice(t * 64, (t + 1) * 64)
        mod = modulation[info[FIRST] + (info[HALF] * parts + t) // 2]
        db = t0[rows, :].astype(f32) + t1[rows, :].astype(f32) + t2[rows, :].astype(f32)
        normed, inverse = normalize(hidden[rows, :])
        grad = g_mine[rows, :].astype(f32) + norm_back(db * (1.0 + mod[4:5]), normed, inverse)
        dh[rows, :] = grad
        dat[rows, :] = (mod[2:3] * grad).astype(bf16)
        sums[3 * t : 3 * t + 1, :] = jnp.sum(grad * attn[rows, :], 0, keepdims=True)
        sums[3 * t + 1 : 3 * t + 2, :] = jnp.sum(db, 0, keepdims=True)
        sums[3 * t + 2 : 3 * t + 3, :] = jnp.sum(db * normed, 0, keepdims=True)


def back_middle(info, modulation, hidden, attn, g_mine, terms, number):
    half = hidden.shape[0]
    return call(
        functools.partial(back_middle_body, number),
        "back_middle",
        [(info, SMEM), (modulation, VMEM), (hidden, VMEM), (attn, VMEM), (g_mine, VMEM)]
        + [(t, VMEM) for t in terms],
        [((half, WIDTH), f32, VMEM), ((half, WIDTH), bf16, VMEM), ((3 * (half // 64), WIDTH), f32, VMEM)],
    )


def attend_back_body(number, info, near_w, far_w, near_qkv, far_qkv, near_p, far_p, s0, s1, s2, s3, *rest):
    dat, dqkv, g0, g1, g2, g3, da, sems = rest
    copies = started(share_copies(info, (s0, s1, s2, s3), dat, sems))
    mask = head_mask()
    groups = (
        (near_w[:, QKV:], near_w[:, :QKV], near_qkv, near_p),
        (far_w[:, QKV:], far_w[:, :QKV], far_qkv, far_p),
    )
    finish(copies)
    for i in range(2 * number):
        rows = slice(i * KEPT, (i + 1) * KEPT)
        grads = []
        total = 0.0
        for out_w, in_w, qkv, probs in groups:
            do = dot(dat[rows, :], out_w).astype(bf16)
            here = qkv[rows, :]
            q, k, v = (here[:, j * PAIRED : (j + 1) * PAIRED] for j in range(3))
            p = probs[i]
            both = split_heads(do, mask)
            dp = dot_t(both, v)
            ds = (p * (dp - jnp.sum(p * dp, -1, keepdims=True))).astype(bf16)
            wide = jnp.concatenate([ds[:KEPT], ds[KEPT:]], 1)
            dq = dot(wide, split_heads(k, mask)) * score_scale
            dk = t_dot(ds, split_heads(q, mask)) * score_scale
            dv = t_dot(p.astype(bf16), both)
            grad = jnp.concatenate([dq, dk, dv], 1).astype(bf16)
            grads.append(grad)
            total = total + dot_t(grad, in_w)
        dqkv[rows, :] = jnp.concatenate(grads, 1)
        da[rows, :] = total.astype(bf16)
    split_halves(info, da, (g0, g1, g2, g3))


def attend_back(info, near, far, pieces, number):
    rows = 2 * number * KEPT
    return call(
        functools.partial(attend_back_body, number),
        "attend_back",
        [(info, SMEM)]
        + [(a, VMEM) for a in (near[0], far[0], near[1], far[1], near[2], far[2])]
        + [(p, ANY) for p in pieces],
        [((rows, WIDTH), bf16, VMEM), ((rows, 2 * QKV), bf16, VMEM)] + halves_of(rows),
        [pltpu.VMEM((rows, WIDTH), bf16), pltpu.SemaphoreType.DMA((4,))],
        flops=4 * rows * WIDTH * 576,
    )


def attn_grads_body(info, act_own, act_other, dat, dqkv, near_o, far_o, o0, o1, o2, o3, act, mixed, full, extra, sems):
    rows = act_own.shape[0]
    act[:rows, :] = act_own[...]
    act[rows:, :] = act_other[...]
    mixed[...] = jnp.concatenate([near_o[...], far_o[...]], 1)
    for i in range(3):
        part = slice(i * 384, (i + 1) * 384)
        a = t_dot(act[:, part], dqkv[...])
        b = t_dot(dat[:, part], mixed[...])
        full[part, :] = jnp.concatenate([a, b], 1).astype(bf16)
    sums = column_sums(dqkv)
    sums = jnp.concatenate([sums, jnp.zeros((1, 2 * PAIRED), f32)], 1)
    extra[...] = stacked(two_rows(sums) + two_rows(column_sums(dat)), 16).astype(bf16)
    finish(started(block_copies(info, full, extra, (o0, o1, o2, o3), sems)))


def attn_grads(info, act_own, act_other, dat, dqkv, near_o, far_o):
    rows = dat.shape[0]
    return call(
        attn_grads_body,
        "attn_grads",
        [(info, SMEM)] + [(a, VMEM) for a in (act_own, act_other, dat, dqkv, near_o, far_o)],
        [((304, WIDTH), bf16, ANY)] * 4,
        [
            pltpu.VMEM((rows, WIDTH), bf16),
            pltpu.VMEM((rows, 2 * PAIRED), bf16),
            pltpu.VMEM((WIDTH, WIDTH), bf16),
            pltpu.VMEM((16, WIDTH), bf16),
            pltpu.SemaphoreType.DMA((8,)),
        ],
        flops=2 * rows * WIDTH * WIDTH,
    )


def last_rows_body(number, info, modulation, x_mine, dh, t0, t1, t2, back_sums, gate_sums, out, sums):
    half = x_mine.shape[0]
    parts = half // 64
    extra = (out.shape[0] - half) // 2
    sums[...] = jnp.zeros_like(sums)
    for t in range(parts):
        rows = slice(t * 64, (t + 1) * 64)
        mod = modulation[info[FIRST] + (info[HALF] * parts + t) // 2]
        da = t0[rows, :].astype(f32) + t1[rows, :].astype(f32) + t2[rows, :].astype(f32)
        normed, inverse = normalize(x_mine[rows, :].astype(f32))
        out[rows, :] = (dh[rows, :] + norm_back(da * (1.0 + mod[1:2]), normed, inverse)).astype(bf16)
        sums[6 * t : 6 * t + 1, :] = jnp.sum(da, 0, keepdims=True)
        sums[6 * t + 1 : 6 * t + 2, :] = jnp.sum(da * normed, 0, keepdims=True)
        sums[6 * t + 2 : 6 * t + 5, :] = back_sums[3 * t : 3 * t + 3, :]
        sums[6 * t + 5 : 6 * t + 6, :] = gate_sums[t : t + 1, :]
    high = sums[...].astype(bf16)
    out[half : half + extra, :] = high
    out[half + extra :, :] = (sums[...] - high.astype(f32)).astype(bf16)


def last_rows(info, modulation, x_mine, dh, terms, back_sums, gate_sums, number):
    half = x_mine.shape[0]
    extra = -(-6 * (half // 64) // 16) * 16
    (out,) = call(
        functools.partial(last_rows_body, number),
        "last_rows",
        [(info, SMEM), (modulation, VMEM), (x_mine, VMEM), (dh, VMEM)]
        + [(t, VMEM) for t in terms]
        + [(back_sums, VMEM), (gate_sums, VMEM)],
        [((half + 2 * extra, WIDTH), bf16, VMEM)],
        [pltpu.VMEM((extra, WIDTH), f32)],
    )
    return out, 2 * extra


def join_body(wide, info, b0, b1, b2, b3, near, far, vectors, held):
    blocks = (b0, b1, b2, b3)
    width = near.shape[1]
    total = b0[:288, :].astype(f32)
    for b in blocks[1:]:
        total = total + b[:288, :].astype(f32)
    for k in range(4):
        held[info[SUP] ^ k] = blocks[k][288:304, :].astype(f32)
    extra = held[0] + held[1] + held[2] + held[3]
    first = extra[0:1] + extra[1:2]
    if wide:
        cut = ((0, UP, 2 * UP, 3 * UP), (UP, 2 * UP, 3 * UP, 4 * UP))
        sums, row = first[:, :WIDTH], first[:, WIDTH:]
        near_sums, far_sums = sums[:, :UP], sums[:, UP:]
    else:
        cut = ((0, QKV, 2 * QKV, 2 * QKV + PAIRED), (QKV, 2 * QKV, 2 * QKV + PAIRED, WIDTH))
        row = extra[2:3] + extra[3:4]
        near_sums, far_sums = first[:, :QKV], first[:, QKV : 2 * QKV]
        pad = jnp.zeros((1, UP - QKV), f32)
        near_sums = jnp.concatenate([near_sums, pad], 1)
        far_sums = jnp.concatenate([far_sums, pad], 1)
    picks = lambda c: jnp.concatenate([total[:, c[0] : c[1]], total[:, c[2] : c[3]]], 1)
    near[...] = picks(cut[0])
    far[:288, :] = picks(cut[1]).astype(bf16)
    rows = two_rows(far_sums)
    if wide:
        zero = jnp.zeros((1, WIDTH - UP), f32)
        rows = [jnp.concatenate([r, zero], 1) for r in rows] + two_rows(row)
        kept = two_rows(row)
    else:
        kept = two_rows(row)
        rows = rows + [part[:, c : c + UP] for part in kept for c in (0, UP)]
    far[288:304, :] = stacked(rows, 16).astype(bf16)
    low = lambda value: value.astype(bf16).astype(f32)
    near_wide = jnp.concatenate([near_sums, jnp.zeros((1, WIDTH - UP), f32)], 1)
    vectors[...] = stacked([near_wide, low(kept[0]) + low(kept[1])], 8)


def join(info, blocks, wide):
    width = 2 * UP if wide else UP
    return call(
        functools.partial(join_body, wide),
        "join_blocks",
        [(info, SMEM)] + [(b, VMEM) for b in blocks],
        [((288, width), f32, VMEM), ((304, width), bf16, VMEM), ((8, WIDTH), f32, VMEM)],
        [pltpu.VMEM((4, 16, blocks[0].shape[1]), f32)],
    )


def strip_body(wide, info, near, vectors, got, keep, send, total):
    core = info[CORE]
    mine = pl.ds(pl.multiple_of(core * SIDE, 16), SIDE)
    theirs = pl.ds(pl.multiple_of((1 - core) * SIDE, 16), SIDE)
    keep[...] = near[mine, :] + got[mine, :].astype(f32)
    send[:SIDE, :] = (near[theirs, :] + got[theirs, :].astype(f32)).astype(bf16)
    extra = got[288:304, :].astype(f32)
    sums = vectors[0:1, :UP] + extra[0:1, :UP] + extra[1:2, :UP]
    if wide:
        row = extra[2:3] + extra[3:4]
    else:
        row = jnp.concatenate([extra[2:3] + extra[4:5], extra[3:4] + extra[5:6]], 1)
    row = vectors[1:2, :] + row
    rows = two_rows(sums)
    low = lambda value: value.astype(bf16).astype(f32)
    rounded = low(rows[0]) + low(rows[1])
    if wide:
        zero = jnp.zeros((1, WIDTH - UP), f32)
        rows = [jnp.concatenate([r, zero], 1) for r in rows]
    send[SIDE:, :] = stacked(rows, 16).astype(bf16)
    total[...] = stacked([jnp.concatenate([rounded, jnp.zeros((1, WIDTH - UP), f32)], 1), row], 8)


def strip(info, near, vectors, got, wide):
    width = near.shape[1]
    return call(
        functools.partial(strip_body, wide),
        "strip",
        [(info, SMEM), (near, VMEM), (vectors, VMEM), (got, VMEM)],
        [((SIDE, width), f32, VMEM), ((SIDE + 16, width), bf16, VMEM), ((8, WIDTH), f32, VMEM)],
    )


def shampoo_body(wide, info, keep, got, left, right, left_root, right_root, master, *rest):
    if wide:
        grads, lefts, rights, news = rest[:4]
        rest = rest[4:]
    else:
        grads, lefts, rights, news = rest[4:8]
        rest = rest[8:]
    (in_l, in_r, in_lr, in_rr, in_m, out_g, out_l, out_r, out_m, sems) = rest
    count = 16 if wide else 8
    first = 8 if wide else 0
    here = pl.ds(first, count)
    copies = started(
        [
            pltpu.make_async_copy(src.at[here], dst, sems.at[k])
            for k, (src, dst) in enumerate(
                ((left, in_l), (right, in_r), (left_root, in_lr), (right_root, in_rr), (master, in_m))
            )
        ]
    )
    core = info[CORE]
    finish(copies)
    for k in range(count // 2):
        columns = slice(k * SIDE, (k + 1) * SIDE)
        for value, half in ((keep[:, columns], core), (got[:SIDE, columns].astype(f32), 1 - core)):
            place = 8 * (k // 4) + 4 * half + k % 4 if wide else 2 * k + half
            out_g[place] = value
            low = value.astype(bf16)
            out_l[place] = decay_rate * in_l[place] + (1.0 - decay_rate) * dot_t(low, low)
            out_r[place] = decay_rate * in_r[place] + (1.0 - decay_rate) * t_dot(low, low)
            step = dot(in_lr[place].astype(bf16), low).astype(bf16)
            step = dot(step, in_rr[place].astype(bf16))
            out_m[place] = in_m[place] - weight_rate * step
    copies = started(
        [
            pltpu.make_async_copy(src, dst.at[here], sems.at[k])
            for k, (src, dst) in enumerate(((out_g, grads), (out_l, lefts), (out_r, rights), (out_m, news)))
        ]
    )
    finish(copies)


def shampoo(info, keep, got, states, previous, wide):
    count = 16 if wide else 8
    whole = (states[0].shape, f32, ANY)
    inputs = [(info, SMEM), (keep, VMEM), (got, VMEM)] + [(s, ANY) for s in states]
    aliases = None
    if not wide:
        aliases = {len(inputs) + k: k for k in range(4)}
        inputs += [(p, ANY) for p in previous]
    return call(
        functools.partial(shampoo_body, wide),
        "shampoo",
        inputs,
        [whole] * 4,
        [pltpu.VMEM((count, SIDE, SIDE), f32)] * 9 + [pltpu.SemaphoreType.DMA((5,))],
        flops=8 * count * 256**3,
        aliases=aliases,
    )


def heads_of(qkv, up):
    rows = []
    for j in range(2):
        rows.append(
            jnp.concatenate(
                [
                    qkv[:, j * HEAD_DIM : (j + 1) * HEAD_DIM],
                    qkv[:, 2 * PAIRED + j * HEAD_DIM : 2 * PAIRED + (j + 1) * HEAD_DIM],
                    up[:, j * 288 : (j + 1) * 288],
                ],
                1,
            )
        )
    return rows


def bias_body(info, attn_total, attn_got, mlp_total, mlp_got, b_in, s_in, b_out, s_out, g_in, m_in, n_in, g_out, m_out, n_out):
    joined = lambda got: got[SIDE : SIDE + 1, :].astype(f32) + got[SIDE + 1 : SIDE + 2, :].astype(f32)
    mine = heads_of(attn_total[0:1, :QKV], mlp_total[0:1, :UP])
    theirs = heads_of(joined(attn_got)[:, :QKV], joined(mlp_got)[:, :UP])
    zero = info[CORE] == 0
    rows = [jnp.where(zero, a, b) for a, b in zip(mine, theirs)]
    rows += [jnp.where(zero, b, a) for a, b in zip(mine, theirs)]
    for grad, base, square, g_ref, m_ref, n_ref in (
        (stacked(rows, 4), b_in, s_in, g_in, m_in, n_in),
        (stacked([attn_total[1:2, :], mlp_total[1:2, :]], 2), b_out, s_out, g_out, m_out, n_out),
    ):
        new = decay_rate * square[...] + (1.0 - decay_rate) * grad * grad
        g_ref[...] = grad
        m_ref[...] = new
        n_ref[...] = base[...] - bias_rate * grad / (jnp.sqrt(new) + root_epsilon)


def bias_step(info, attn, mlp_part, bias_in, bias_in_sq, bias_out, bias_out_sq):
    arrays = list(attn) + list(mlp_part) + [bias_in, bias_in_sq, bias_out, bias_out_sq]
    return call(
        bias_body,
        "bias_step",
        [(info, SMEM)] + [(a, VMEM) for a in arrays],
        [(bias_in.shape, f32, VMEM)] * 3 + [(bias_out.shape, f32, VMEM)] * 3,
    )


def bias_rows_body(info, near, far, qkv_near, qkv_far, up):
    ups = []
    for ref, out in ((near, qkv_near), (far, qkv_far)):
        rows = []
        for j in range(2):
            low, high = ref[j : j + 1, :], ref[j + 2 : j + 3, :]
            rows.append(jnp.where(info[CORE] == 0, low, high))
        both = lambda a, b: jnp.concatenate([rows[0][:, a:b], rows[1][:, a:b]], 1)
        out[...] = jnp.concatenate(
            [both(0, HEAD_DIM), jnp.zeros((1, PAIRED), f32), both(HEAD_DIM, 2 * HEAD_DIM)], 1
        )
        ups.append(both(2 * HEAD_DIM, QKV))
    up[...] = jnp.concatenate(ups, 1)


def bias_rows(info, near, far):
    return call(
        bias_rows_body,
        "bias_rows",
        [(info, SMEM), (near, VMEM), (far, VMEM)],
        [((1, QKV), f32, VMEM)] * 2 + [((1, 2 * UP), f32, VMEM)],
    )


def finish_whole(attn_blocks, mlp_blocks, states, biases, core, head):
    left_stat, right_stat, left_root, right_root, master = states
    bias_in, bias_in_sq, bias_out, bias_out_sq = biases
    far_of = lambda v: over_head(v, 2)

    def halves(blocks, splits):
        full = jnp.concatenate([b[:288] for b in blocks], 0)
        near = jnp.concatenate([full[:, a:b] for a, b in splits[0]], 1).astype(f32)
        far = jnp.concatenate([full[:, a:b] for a, b in splits[1]], 1)
        near = (near + far_of(far).astype(f32)).astype(bf16)
        both = lax.all_gather(near, "core").astype(f32)
        return [part.reshape(8, SIDE, -1, SIDE).transpose(2, 0, 1, 3) for part in (both[0], both[1])]

    a0, a1 = halves(attn_blocks, (((0, 432), (864, 1008)), ((432, 864), (1008, 1152))))
    m0, m1 = halves(mlp_blocks, (((0, 576), (1152, 1728)), ((576, 1152), (1728, 2304))))
    attn = jnp.stack([a0, a1], 1).reshape(8, 8, SIDE, SIDE)
    tiles = jnp.concatenate([attn, m0[:4], m1[:4], m0[4:], m1[4:]], 0)
    tiles = tiles.transpose(1, 0, 2, 3).reshape(192, SIDE, SIDE)
    tiles = lax.psum_scatter(tiles, "sup", scatter_dimension=0, tiled=True)
    count = master.shape[0]
    grad = lax.dynamic_slice_in_dim(tiles, core * count, count, 0)
    low = grad.astype(bf16)
    product = lambda spec, a, b: jnp.einsum(spec, a.astype(bf16), b.astype(bf16), preferred_element_type=f32)
    left_new = decay_rate * left_stat + (1.0 - decay_rate) * product("kab,kcb->kac", low, low)
    right_new = decay_rate * right_stat + (1.0 - decay_rate) * product("kba,kbc->kac", low, low)
    step = product("kab,kbc->kac", product("kab,kbc->kac", left_root, low), right_root)
    master_new = master - weight_rate * step
    attn_rows = attn_blocks[0][288:304].astype(f32)
    mlp_rows = mlp_blocks[0][288:304].astype(f32)
    vector = jnp.concatenate(
        [attn_rows[0] + attn_rows[1], attn_rows[2] + attn_rows[3], mlp_rows[0] + mlp_rows[1]]
    )
    vector = lax.psum(vector, "sup")
    qkv, dat = vector[: 2 * QKV], vector[WIDTH : 2 * WIDTH]
    up, dm = vector[2 * WIDTH : 3 * WIDTH], vector[3 * WIDTH :]
    rows = jnp.stack([dat, dm], 0)
    swap = lax.psum(rows, "head") * 0.5
    qkv = qkv[:QKV] + far_of(qkv[QKV:])
    up = up[:UP] + far_of(up[UP:])
    parts = [jnp.concatenate(heads_of(qkv[None], up[None]), 0)]
    grad_in = lax.all_gather(parts[0], "core", axis=0, tiled=True)
    out = [grad, left_new, right_new, master_new]
    for g, b, s in ((grad_in, bias_in, bias_in_sq), (swap, bias_out, bias_out_sq)):
        new = decay_rate * s + (1.0 - decay_rate) * g * g
        out += [g, new, b - bias_rate * g / (jnp.sqrt(new) + root_epsilon)]
    return out


def on_device(
    tokens,
    cotangent,
    modulation,
    counts,
    master,
    left_stat,
    right_stat,
    left_root,
    right_root,
    bias_in,
    bias_in_sq,
    bias_out,
    bias_out_sq,
):
    images, slots, _ = tokens.shape
    core = lax.axis_index("core")
    head = lax.axis_index("head")
    number = images // 2
    strips = master.shape[0] == 24
    place = lax.axis_index("sup") if strips else 0
    order = core if strips else 0
    info = jnp.stack(
        [jnp.asarray(v, jnp.int32) for v in (place, order, core, head, head % 2, (head // 2) * number, 0, 0)]
    )
    (attn_near, attn_far), (mlp_near, mlp_far) = weight_pieces(info, master, core)
    act_own, dm_own, x_mine, g_mine = kept_rows(info, counts, tokens, cotangent, modulation, number)
    act_other = over_core(act_own)
    dm_other = over_core(dm_own)
    bias_near, bias_far, bias_up = bias_rows(info, bias_in, over_head(bias_in, 2))

    near = attend(info, act_own, act_other, bias_near, attn_near, number)
    far = attend(info, act_own, act_other, bias_far, attn_far, number)
    terms = sum_rows(project(info, near[0], far[0], near[3], far[3]))
    hidden, attn, act_mine = middle(info, modulation, bias_out, x_mine, terms, number)
    pieces = share_rows(act_mine)
    w_up, w_down = mlp_weights(info, mlp_near, mlp_far)
    act_two, f, du, *db_parts = mlp(info, bias_up, dm_own, dm_other, w_up, w_down, pieces, number)
    db_terms = sum_rows(db_parts)
    mlp_blocks = mlp_grads(info, act_two, du, f, dm_own, dm_other)
    mlp_terms = sum_rows(down_rows(info, f, w_down))
    dh, dat_mine, back_sums = back_middle(info, modulation, hidden, attn, g_mine, db_terms, number)
    dat_pieces = share_rows(dat_mine)
    output_mine, gate_sums = output_rows(info, modulation, bias_out, hidden, g_mine, mlp_terms, number)
    (output,) = expand(info, counts, output_mine, images, slots, 0)
    dat, dqkv, *da_parts = attend_back(info, near, far, dat_pieces, number)
    da_terms = sum_rows(da_parts)
    attn_blocks = attn_grads(info, act_own, act_other, dat, dqkv, near[3], far[3])
    last, extra = last_rows(info, modulation, x_mine, dh, da_terms, back_sums, gate_sums, number)
    grad_tokens, grad_modulation = expand(info, counts, last, images, slots, extra)

    states = (left_stat, right_stat, left_root, right_root, master)
    biases = (bias_in, bias_in_sq, bias_out, bias_out_sq)
    if strips:
        parts = []
        previous = None
        for blocks, wide in ((mlp_blocks, True), (attn_blocks, False)):
            blocks = [blocks[0]] + [over_sup(blocks[k], k) for k in (1, 2, 3)]
            near_sum, far_sum, vectors = join(info, blocks, wide)
            keep, send, total = strip(info, near_sum, vectors, over_head(far_sum, 2), wide)
            got = over_core(send)
            previous = shampoo(info, keep, got, states, previous, wide)
            parts.append((total, got))
        weights = list(previous)
        steps = bias_step(info, parts[1], parts[0], *biases)
        tail = weights + list(steps)
    else:
        tail = finish_whole(attn_blocks, mlp_blocks, states, biases, core, head)
    return (output, grad_tokens, grad_modulation, *tail)


def solution(mesh):
    devices = mesh.devices
    inner = Mesh(
        devices.reshape(devices.shape[0] // 2, 2, devices.shape[1]), ("sup", "core", "head")
    )
    seq = ("sup", "core")
    tile = P(("sup", "core", "head"), None, None)
    rows = P(seq, None, None)
    return jax.shard_map(
        on_device,
        mesh=inner,
        in_specs=(rows, rows, rows, P(seq, None), tile, tile, tile, tile, tile)
        + (P("head", None), P("head", None), P(), P()),
        out_specs=(rows, rows, P(seq, None, "head"), tile, tile, tile, tile)
        + (P("head", None),) * 3
        + (P(),) * 3,
        check_vma=False,
    )
```

```python
import functools

import jax
import jax.numpy as jnp
from jax import lax
from jax.experimental import pallas as pl
from jax.experimental.pallas import tpu as pltpu
from jax.sharding import Mesh, PartitionSpec as P

HEADS = 16
HEAD_DIM = 72
KEPT = 128
SIDE = 144
RANGES = 8
SLOTS = 24
WIDTH = 1152
QKV = 432
PAIRED = 144
UP = 576

norm_epsilon = 1e-06
decay_rate = 0.5
weight_rate = 0.3
bias_rate = 0.1
root_epsilon = 1e-08
score_scale = HEAD_DIM ** (-0.5)
bf16 = jnp.bfloat16
f32 = jnp.float32
CORE_SWAP = [(0, 1), (1, 0)]
HEAD_AXES = ("hp", "hq")

SUP, ORDER, CORE, HEAD, HALF, FIRST, GROUP = range(7)
ANY = pl.BlockSpec(memory_space=pl.ANY)
VMEM = pl.BlockSpec(memory_space=pltpu.VMEM)
SMEM = pl.BlockSpec(memory_space=pltpu.SMEM)


def dot(a, b):
    return lax.dot_general(a, b, (((1,), (0,)), ((), ())), preferred_element_type=f32)


def dot_t(a, b):
    return lax.dot_general(a, b, (((1,), (1,)), ((), ())), preferred_element_type=f32)


def t_dot(a, b):
    return lax.dot_general(a, b, (((0,), (0,)), ((), ())), preferred_element_type=f32)


def normalize(values):
    center = jnp.mean(values, -1, keepdims=True)
    centered = values - center
    inverse = lax.rsqrt(jnp.mean(centered * centered, -1, keepdims=True) + norm_epsilon)
    return (centered * inverse, inverse)


def norm_back(grad_in, normed, inverse):
    inner = jnp.mean(grad_in * normed, -1, keepdims=True)
    return inverse * (grad_in - jnp.mean(grad_in, -1, keepdims=True) - normed * inner)


def over_both(values):
    pairs = [(i, i ^ 5) for i in range(8)]
    return lax.ppermute(values, ("core", "hp", "hq"), pairs)


def over_core(values):
    return lax.ppermute(values, "core", CORE_SWAP)


def over_head(values, offset):
    return lax.ppermute(values, HEAD_AXES, [(i, i ^ offset) for i in range(4)])


def over_sup(values, offset):
    return lax.ppermute(values, "sup", [(i, i ^ offset) for i in range(4)])


def shaped(shape, dtype):
    return jax.ShapeDtypeStruct(shape, dtype)


LAST = [None]
TIMES = dict(last_rows=10, relay_last=5, expand_rows=3, back_middle=10)
COST = 0.02


def call(body, name, inputs, outputs, scratch=(), flops=0, aliases=None, vmem=56, after=(), cost=0, grid=()):
    inputs = list(inputs)
    count = len(inputs)
    if LAST[0] is not None and all(LAST[0] is not array for array, _ in inputs):
        inputs.append((LAST[0], ANY))
    inputs += [(a, ANY) for a in after]
    arrays = [array for array, _ in inputs]
    shapes = [shaped(shape, dtype) for shape, dtype, _ in outputs]

    size = sum(a.size * a.dtype.itemsize for a in arrays[:count] + shapes)

    def ordered(*refs):
        return body(*refs[:count], *refs[len(arrays) :])

    results = pl.pallas_call(
        ordered,
        name=name,
        grid=grid,
        out_shape=shapes,
        in_specs=[spec for _, spec in inputs],
        out_specs=[spec for _, _, spec in outputs],
        scratch_shapes=list(scratch),
        input_output_aliases=aliases or {},
        cost_estimate=pl.CostEstimate(flops=int(1.0e9 * TIMES.get(name, 0.02)), bytes_accessed=0, transcendentals=0),
        compiler_params=pltpu.CompilerParams(vmem_limit_bytes=vmem * 1024 * 1024),
    )(*arrays)
    LAST[0] = min(results, key=lambda a: a.size * a.dtype.itemsize)
    return results


def chunks_of(rows, size):
    return [slice(at, min(at + size, rows)) for at in range(0, rows, size)]


def started(copies):
    for copy in copies:
        copy.start()
    return copies


def finish(copies):
    for copy in copies:
        copy.wait()


def pack_body(info, master, bias, mine, other, rows, mlp_mine, mlp_other, held, sems):
    copies = started(
        [pltpu.make_async_copy(master.at[pl.ds(8 * k, 8)], held.at[pl.ds(8 * k, 8)], sems.at[k]) for k in range(3)]
    )
    core = info[CORE]
    heads = [jnp.where(core == 0, bias[j : j + 1, :], bias[j + 2 : j + 3, :]) for j in range(2)]
    both = lambda a, b: jnp.concatenate([heads[0][:, a:b], heads[1][:, a:b]], 1)
    blank = jnp.zeros((1, PAIRED), f32)
    first = jnp.concatenate([both(0, HEAD_DIM), blank, both(HEAD_DIM, 2 * HEAD_DIM), blank], 1)
    rows[...] = stacked(three_rows(first) + three_rows(both(2 * HEAD_DIM, QKV)), 16).astype(bf16)
    copies[0].wait()
    for out, half in ((mine, core), (other, 1 - core)):
        out[...] = jnp.concatenate([held[2 * k + half].astype(bf16) for k in range(4)], 1)
    finish(copies[1:])
    for out, half in ((mlp_mine, core), (mlp_other, 1 - core)):
        out[...] = jnp.concatenate(
            [held[8 + 8 * w + 4 * half + k].astype(bf16) for w in range(2) for k in range(4)], 1
        )


def pack(info, master, bias_in):
    outs = lambda width: [((SIDE, width), bf16, VMEM)] * 2
    return call(
        pack_body,
        "pack",
        [(info, SMEM), (master, ANY), (bias_in, VMEM)],
        outs(4 * SIDE) + [((16, 4 * SIDE), bf16, VMEM)] + outs(8 * SIDE),
        [pltpu.VMEM((24, SIDE, SIDE), f32), pltpu.SemaphoreType.DMA((3,))],
    )


def piece_copies(info, pieces, target, sems, sup=None):
    copies = []
    sup = info[SUP] if sup is None else sup
    for k in range(4):
        for j in range(2):
            row = ((sup ^ k) * 2 + (info[ORDER] ^ j)) * SIDE
            copies.append(
                pltpu.make_async_copy(
                    pieces[k].at[pl.ds(j * SIDE, SIDE)],
                    target.at[pl.ds(pl.multiple_of(row, 16), SIDE)],
                    sems.at[2 * k + j],
                )
            )
    return copies


def gather_pieces(block):
    return [block] + [over_sup(block, k) for k in (1, 2, 3)]


def whole_pieces(master, core):
    tiles = lax.all_gather(master.astype(bf16), ("sup", "core"), axis=0, tiled=True)
    slab = tiles.reshape(8, 24, SIDE, SIDE).transpose(1, 0, 2, 3).reshape(24, 8 * SIDE, SIDE)
    take = lambda k: lax.dynamic_index_in_dim(slab, k, 0, False)
    attn = jnp.concatenate([take(2 * k + core) for k in range(4)], 1)
    mlp = jnp.concatenate([take(8 + 8 * w + 4 * core + k) for w in range(2) for k in range(4)], 1)
    out = []
    far = over_head(attn, 2)
    pieces = [[part[288 * k : 288 * k + 288] for k in range(4)] for part in (attn, far)]
    return pieces, [p.reshape(4, 288, 2 * UP) for p in (mlp, over_head(mlp, 2))]


def later_body(mine, got, out):
    out[: mine.shape[0], :] = mine[...]
    out[mine.shape[0] :, :] = got[...]


def copies_body(mine, *rest):
    out = rest[-1]
    for k in range(out.shape[0]):
        out[k, : mine.shape[0], :] = mine[...]
        if len(rest) > 1:
            out[k, mine.shape[0] :, :] = rest[0][...]


def copies_of(parts, count):
    rows = sum(p.shape[0] for p in parts)
    return call(
        copies_body, "copies", [(p, VMEM) for p in parts], [((count, rows, parts[0].shape[1]), bf16, VMEM)]
    )[0]


def to_all(values, axis):
    return lax.all_to_all(values, axis, 0, 0)


def later_block(mine, got, after=()):
    rows = mine.shape[0] + got.shape[0]
    return call(
        later_body, "later_block", [(mine, VMEM), (got, VMEM)], [((rows, mine.shape[1]), bf16, VMEM)], after=after
    )[0]


def small_body(counts, modulation, out):
    images = out.shape[0]
    out[:, :6, :] = modulation[...]
    place = lax.broadcasted_iota(jnp.int32, (2, WIDTH), 1)
    for i in range(images):
        row = jnp.zeros((2, WIDTH), f32)
        for s in range(RANGES):
            row = jnp.where(place == s, counts[i, s].astype(f32), row)
        out[i, 6:8, :] = row


def small_rows(counts, modulation):
    shape = (modulation.shape[0], 8, WIDTH)
    return call(small_body, "small_rows", [(counts, SMEM), (modulation, VMEM)], [(shape, f32, VMEM)])[0]


def kept_target_of(row, slot):
    target = jnp.full(slot.shape, -1.0, f32)
    start = jnp.zeros((1, 1), f32)
    for s in range(RANGES):
        number = row[:, s : s + 1]
        place = slot - s * SLOTS
        target = jnp.where((place >= 0) & (place < number), place + start, target)
        start = start + number
    return target


def rows_body(number, info, small, tokens, cotangent, far_small, far_tokens, act, dm, x_mine, g_mine, tok, cot, x_own, g_own, sems):
    first = info[FIRST]
    copies = started(
        [
            pltpu.make_async_copy(tokens.at[pl.ds(first, number)], tok.at[pl.ds(0, number)], sems.at[0]),
            pltpu.make_async_copy(far_tokens.at[pl.ds(first, number)], tok.at[pl.ds(number, number)], sems.at[1]),
            pltpu.make_async_copy(cotangent.at[pl.ds(first, number)], cot, sems.at[2]),
        ]
    )
    finish(copies)
    slots = tok.shape[1]
    slot = lax.broadcasted_iota(jnp.int32, (1, slots), 1).astype(f32)
    place = lax.broadcasted_iota(jnp.int32, (KEPT, slots), 0).astype(f32)
    for i in range(2 * number):
        mod = (small if i < number else far_small)[first + i % number]
        select = (kept_target_of(mod[6:7], slot) == place).astype(f32).astype(bf16)
        rows = slice(i * KEPT, (i + 1) * KEPT)
        x = dot(select, tok[i])
        normed, _ = normalize(x)
        act[rows, :] = (normed * (1.0 + mod[1:2]) + mod[0:1]).astype(bf16)
        if i < number:
            x_own[rows, :] = x.astype(bf16)
            g = dot(select, cot[i])
            g_own[rows, :] = g.astype(bf16)
            dm[rows, :] = (mod[5:6] * g).astype(bf16)
    half = x_mine.shape[0]
    mine = pl.ds(pl.multiple_of(info[HALF] * half, 64), half)
    x_mine[...] = x_own[mine, :]
    g_mine[...] = g_own[mine, :]


def kept_rows(info, small, tokens, cotangent, far_small, far_tokens, number):
    slots = tokens.shape[1]
    rows = number * KEPT
    half = rows // 2
    return call(
        functools.partial(rows_body, number),
        "kept_rows",
        [(info, SMEM), (small, VMEM), (tokens, ANY), (cotangent, ANY), (far_small, VMEM), (far_tokens, ANY)],
        [((2 * rows, WIDTH), bf16, VMEM), ((rows, WIDTH), bf16, VMEM)] + [((half, WIDTH), bf16, VMEM)] * 2,
        [pltpu.VMEM((2 * number, slots, WIDTH), bf16), pltpu.VMEM((number, slots, WIDTH), bf16)]
        + [pltpu.VMEM((rows, WIDTH), bf16)] * 2
        + [pltpu.SemaphoreType.DMA((3,))],
        flops=6 * rows * slots * WIDTH,
    )


def spread_of(counts, image):
    parts = []
    start = 0
    slot = lax.broadcasted_iota(jnp.int32, (SLOTS, KEPT), 0)
    row = lax.broadcasted_iota(jnp.int32, (SLOTS, KEPT), 1)
    for s in range(RANGES):
        number = counts[image, s]
        parts.append(((row == slot + start) & (slot < number)).astype(f32))
        start = start + number
    return jnp.concatenate(parts, 0).astype(bf16)


def expand_body(images, extra, size, places, info, counts, *rest):
    pieces, (out, sums, held, sems) = rest[: len(places)], rest[len(places) :]
    half = size - extra
    copies = []
    for n, (k, at) in enumerate(places):
        row = pl.multiple_of((info[HEAD] ^ k) * size + at, 16)
        copies.append(pltpu.make_async_copy(pieces[n], held.at[pl.ds(row, pieces[n].shape[0])], sems.at[n]))
    finish(started(copies))
    parts = half // 64
    for i in range(images):
        spread = spread_of(counts, i)
        chunks = []
        for chunk in (2 * i, 2 * i + 1):
            row = (chunk // parts) * size + (chunk % parts) * 64
            chunks.append(held[row : row + 64, :])
        out[i] = dot(spread, jnp.concatenate(chunks, 0)).astype(bf16)
        if True:
            total = jnp.zeros((6, WIDTH), f32)
            for chunk in (2 * i, 2 * i + 1):
                base = (chunk // parts) * size + half
                block = held[base : base + extra, :].astype(f32)
                at = (chunk % parts) * 6
                total = total + block[at : at + 6]
            quarter = WIDTH // 4
            picked = total[:, :quarter]
            for k in range(1, 4):
                picked = jnp.where(info[HEAD] == k, total[:, k * quarter : (k + 1) * quarter], picked)
            sums[i] = picked


def expand(info, counts, size, pieces, images, slots, extra):
    return call(
        functools.partial(expand_body, images, extra, size, [(k, at) for _, k, at in pieces]),
        "expand_rows",
        [(info, SMEM), (counts, SMEM)] + [(p, ANY) for p, _, _ in pieces],
        [((images, slots, WIDTH), bf16, VMEM), ((images, 6, WIDTH // 4), f32, VMEM)],
        [pltpu.VMEM((4 * size, WIDTH), bf16), pltpu.SemaphoreType.DMA((len(pieces),))],
        flops=2 * images * slots * KEPT * WIDTH,
    )


def expand_all_body(images, info, counts, rows, out):
    for i in range(images):
        spread = spread_of(counts, i)
        out[i] = dot(spread, rows[i * KEPT : (i + 1) * KEPT, :]).astype(bf16)


def expand_all(info, counts, rows, images, slots):
    return call(
        functools.partial(expand_all_body, images),
        "expand_output",
        [(info, SMEM), (counts, SMEM), (rows, VMEM)],
        [((images, slots, WIDTH), bf16, VMEM)],
        flops=2 * images * slots * KEPT * WIDTH,
    )


def both_copies(own, other, target, sems):
    rows = target.shape[0] // 2
    return [
        pltpu.make_async_copy(ref, target.at[pl.ds(k * rows, rows)], sems.at[k]) for k, ref in enumerate((own, other))
    ]


def first_sum_body(mine, got, send):
    send[: mine.shape[0], :] = (mine[...].astype(f32) + got[...].astype(f32)).astype(send.dtype)
    if send.shape[0] > mine.shape[0]:
        send[mine.shape[0] :, :] = jnp.zeros((send.shape[0] - mine.shape[0], send.shape[1]), send.dtype)


def sum_rows(parts, kind=bf16, spare=0):
    own_send, own_keep, other_send, other_keep = parts
    got, got_keep = over_core(other_send), over_core(other_keep)
    rows, width = own_send.shape
    (send,) = call(first_sum_body, "first_sum", [(own_send, VMEM), (got, VMEM)], [((rows + spare, width), kind, VMEM)])
    return own_keep, got_keep, over_head(send, 1)


def relay_body(got, out):
    out[...] = got[...]


def relay_two_body(got, first, second):
    first[...] = got[: first.shape[0], :]
    second[...] = got[first.shape[0] :, :]


def relay_two(got):
    part = got.shape[0] // 32 * 16
    shapes = [(part, got.shape[1]), (got.shape[0] - part, got.shape[1])]
    return call(relay_two_body, "relay_last", [(got, VMEM)], [(shape, got.dtype, VMEM) for shape in shapes])


def relay(got, after=()):
    return call(relay_body, "relay", [(got, VMEM)], [(got.shape, got.dtype, VMEM)], after=after)[0]


def all_terms(terms, rows):
    total = terms[0][rows, :].astype(f32)
    for term in terms[1:]:
        total = total + term[rows, :].astype(f32)
    return total


def share_copies(info, pieces, target, sems):
    half = pieces[0].shape[0]
    copies = []
    for k in range(4):
        row = (k // 2) * 2 * half + (info[HALF] ^ (k % 2)) * half
        copies.append(
            pltpu.make_async_copy(pieces[k], target.at[pl.ds(pl.multiple_of(row, 64), half)], sems.at[k])
        )
    return copies


def split_halves(info, full, outs):
    half = outs[0].shape[0]
    for k in range(4):
        place = info[HALF] if k % 2 else 1 - info[HALF]
        outs[k][...] = full[pl.ds(pl.multiple_of((2 * (k // 2) + place) * half, 64), half), :].astype(bf16)


def head_mask():
    return lax.broadcasted_iota(jnp.int32, (KEPT, PAIRED), 1) < HEAD_DIM


def split_heads(values, mask):
    zero = jnp.zeros_like(values)
    return jnp.concatenate([jnp.where(mask, values, zero), jnp.where(mask, zero, values)], 0)


def sum_of_rows(ref, first):
    rows = ref[...].astype(f32)
    return rows[first : first + 1] + rows[first + 1 : first + 2] + rows[first + 2 : first + 3]


def attend_body(number, info, act, bias, w0, w1, w2, w3, weights, qkv, probs, mixed, sems):
    finish(started(piece_copies(info, (w0, w1, w2, w3), weights, sems)))
    mask = head_mask()
    bias = sum_of_rows(bias, 0)[:, :QKV]
    for rows in chunks_of(act.shape[0], 384):
        qkv[rows, :] = (dot(act[rows, :], weights[:, :QKV]) + bias).astype(bf16)
    for i in range(2 * number):
        rows = slice(i * KEPT, (i + 1) * KEPT)
        here = qkv[rows, :]
        q, k, v = (here[:, j * PAIRED : (j + 1) * PAIRED] for j in range(3))
        scores = dot_t(split_heads(q, mask), k) * score_scale
        raised = jnp.exp(scores - jnp.max(scores, -1, keepdims=True))
        p = raised / jnp.sum(raised, -1, keepdims=True)
        probs[i] = p
        low = p.astype(bf16)
        wide = jnp.concatenate([low[:KEPT], low[KEPT:]], 1)
        mixed[rows, :] = dot(wide, split_heads(v, mask)).astype(bf16)


def attend(info, act, bias, pieces, number):
    rows = 2 * number * KEPT
    return call(
        functools.partial(attend_body, number),
        "attend",
        [(info, SMEM), (act, VMEM), (bias, VMEM)] + [(p, ANY) for p in pieces],
        [
            ((WIDTH, QKV + PAIRED), bf16, VMEM),
            ((rows, QKV), bf16, VMEM),
            ((2 * number, 2 * KEPT, KEPT), f32, VMEM),
            ((rows, PAIRED), bf16, VMEM),
        ],
        [pltpu.SemaphoreType.DMA((8,))],
        flops=2 * rows * WIDTH * QKV,
    )


def project_body(info, near_w, far_w, near, far, *rest):
    outs, full = rest[:4], rest[4]
    wa = near_w[:, QKV:]
    wb = far_w[:, QKV:]
    for rows in chunks_of(near.shape[0], 384):
        full[rows, :] = (dot_t(near[rows, :], wa) + dot_t(far[rows, :], wb)).astype(bf16)
    split_halves(info, full, outs)


def halves_of(rows):
    return [((rows // 4, WIDTH), bf16, VMEM)] * 4


def project(info, near_w, far_w, near, far):
    rows = near.shape[0]
    return call(
        project_body,
        "project",
        [(info, SMEM), (near_w, VMEM), (far_w, VMEM), (near, VMEM), (far, VMEM)],
        halves_of(rows),
        [pltpu.VMEM((rows, WIDTH), bf16)],
        flops=4 * rows * WIDTH * PAIRED,
    )


def middle_body(number, info, modulation, bias_out, x_mine, *rest):
    terms, (hidden, attn, act) = rest[:-3], rest[-3:]
    half = x_mine.shape[0]
    parts = half // 64
    for t in range(parts):
        rows = slice(t * 64, (t + 1) * 64)
        mod = modulation[info[FIRST] + (info[HALF] * parts + t) // 2]
        a = all_terms(terms, rows) + bias_out[0:1, :]
        h = x_mine[rows, :].astype(f32) + mod[2:3] * a
        attn[rows, :] = a
        hidden[rows, :] = h
        normed, _ = normalize(h)
        act[rows, :] = (normed * (1.0 + mod[4:5]) + mod[3:4]).astype(bf16)


def middle(info, modulation, bias_out, x_mine, terms, number):
    half = x_mine.shape[0]
    return call(
        functools.partial(middle_body, number),
        "middle",
        [(info, SMEM), (modulation, VMEM), (bias_out, VMEM), (x_mine, VMEM)] + [(t, VMEM) for t in terms],
        [((half, WIDTH), f32, VMEM)] * 2 + [((half, WIDTH), bf16, VMEM)],
    )


def mlp_weights_body(relative, info, *refs):
    pieces, (up, down, held, sems) = refs[:4], refs[4:]
    finish(started(piece_copies(info, pieces, held, sems, None if relative else 0)))
    for i in range(8):
        rows = slice(i * SIDE, (i + 1) * SIDE)
        up[rows, :] = held[rows, :UP]
        down[rows, :] = held[rows, UP:]


def whole_body(info, whole, *refs):
    mlp_weights_body(False, info, *[whole.at[k] for k in range(4)], *refs)


def mlp_weights(info, pieces):
    relative = isinstance(pieces, list)
    arrays = pieces if relative else [pieces]
    return call(
        functools.partial(mlp_weights_body, True) if relative else whole_body,
        "mlp_weights",
        [(info, SMEM)] + [(p, ANY) for p in arrays],
        [((WIDTH, UP), bf16, VMEM)] * 2,
        [pltpu.VMEM((WIDTH, 2 * UP), bf16), pltpu.SemaphoreType.DMA((8,))],
    )


def smooth_both(u):
    c = 0.7978845608028654
    cube = 0.044715
    square = u * u
    t = jnp.tanh(c * u * (1.0 + cube * square))
    half_up = 0.5 * (1.0 + t)
    slope = half_up + 0.5 * u * (1.0 - t * t) * (c * (1.0 + 3.0 * cube * square))
    return u * half_up, slope


def mlp_body(number, info, near_bias, far_bias, own, other, near_up, near_down, far_up, far_down, s0, s1, s2, s3, *rest):
    act, f, du, g0, g1, g2, g3, db, dm, dm_sems, sems = rest
    copies = started(both_copies(own, other, dm, dm_sems))
    finish(copies + started(share_copies(info, (s0, s1, s2, s3), act, sems)))
    biases = [sum_of_rows(ref, 3) for ref in (near_bias, far_bias)]
    for rows in chunks_of(act.shape[0], 384):
        values, lows = [], []
        total = 0.0
        for g, (up, down) in enumerate(((near_up, near_down), (far_up, far_down))):
            u = dot(act[rows, :], up[...]) + biases[g]
            value, slope = smooth_both(u)
            low = (dot(dm[rows, :], down[...]) * slope).astype(bf16)
            total = total + dot_t(low, up[...])
            values.append(value.astype(bf16))
            lows.append(low)
        f[rows, :] = jnp.concatenate(values, 1)
        du[rows, :] = jnp.concatenate(lows, 1)
        db[rows, :] = total.astype(bf16)
    split_halves(info, db, (g0, g1, g2, g3))


def mlp(info, biases, own, other, near, far, pieces, number):
    rows = 2 * number * KEPT
    full = ((rows, WIDTH), bf16, VMEM)
    return call(
        functools.partial(mlp_body, number),
        "mlp",
        [(info, SMEM), (biases[0], VMEM), (biases[1], VMEM), (own, ANY), (other, ANY)]
        + [(a, VMEM) for a in (*near, *far)]
        + [(p, ANY) for p in pieces],
        [full] * 3 + halves_of(rows),
        [pltpu.VMEM((rows, WIDTH), bf16)] * 2 + [pltpu.SemaphoreType.DMA((2,)), pltpu.SemaphoreType.DMA((4,))],
        flops=6 * rows * WIDTH * WIDTH,
    )


def down_body(info, f, near_w, far_w, *rest):
    outs, full = rest[:4], rest[4]
    for rows in chunks_of(f.shape[0], 384):
        full[rows, :] = (dot_t(f[rows, :UP], near_w[...]) + dot_t(f[rows, UP:], far_w[...])).astype(bf16)
    split_halves(info, full, outs)


def down_rows(info, f, near_w, far_w):
    rows = f.shape[0]
    return call(
        down_body,
        "down",
        [(info, SMEM), (f, VMEM), (near_w, VMEM), (far_w, VMEM)],
        halves_of(rows),
        [pltpu.VMEM((rows, WIDTH), bf16)],
        flops=2 * rows * WIDTH * WIDTH,
    )


def two_rows(values):
    high = values.astype(bf16)
    return [high.astype(f32), values - high.astype(f32)]


def three_rows(values):
    high, rest = two_rows(values)
    return [high] + two_rows(rest)


def stacked(rows, count):
    width = rows[0].shape[1]
    place = lax.broadcasted_iota(jnp.int32, (count, width), 0)
    out = jnp.zeros((count, width), f32)
    for k, row in enumerate(rows):
        out = jnp.where(place == k, row, out)
    return out


def block_copies(strips, info, full, extra, outs, sems):
    copies = []

    def add(source, target):
        copies.append(pltpu.make_async_copy(source, target, sems.at[len(copies)]))

    if strips:
        moves = ((0, 0, (1, 3)), (1, 1, (2, 3)), (2, 0, (0, 2)), (3, 1, (0, 1)))
        for out, part, places in moves:
            for j, k in enumerate(places):
                row = pl.multiple_of((info[SUP] ^ k) * 288 + part * SIDE, 16)
                add(full.at[pl.ds(row, SIDE)], outs[out].at[j, pl.ds(0, SIDE)])
                if part:
                    add(extra, outs[out].at[j, pl.ds(SIDE, 16)])
    else:
        for k in range(4):
            add(full.at[pl.ds(k * 288, 288)], outs[k].at[pl.ds(0, 288)])
            add(extra, outs[k].at[pl.ds(288, 16)])
    return copies


def column_sums(ref):
    half = ref.shape[0] // 2
    first = jnp.sum(ref[:half, :].astype(f32), 0, keepdims=True)
    return first + jnp.sum(ref[half:, :].astype(f32), 0, keepdims=True)


def mlp_grads_body(strips, info, act, du, f, own, other, o0, o1, o2, o3, vectors, dm, full, dm_sems, sems):
    finish(started(both_copies(own, other, dm, dm_sems)))
    for part in (slice(0, 512), slice(512, WIDTH)):
        up = t_dot(act[:, part], du[...]).astype(bf16)
        down = t_dot(dm[:, part], f[...]).astype(bf16)
        for g in range(2):
            columns = slice(g * UP, (g + 1) * UP)
            full[g, part, :] = jnp.concatenate([up[:, columns], down[:, columns]], 1)
    if strips:
        moves = ((0, o0, (1, 3)), (1, o1, (2, 3)), (0, o2, (0, 2)), (1, o3, (0, 1)))
    else:
        moves = [(g, o, (2 * h, 2 * h + 1)) for g, h, o in ((0, 0, o0), (0, 1, o1), (1, 0, o2), (1, 1, o3))]
    copies = []
    for g, out, places in moves:
        for j, k in enumerate(places):
            row = pl.multiple_of((info[SUP] ^ k) * 288, 16)
            copies.append(pltpu.make_async_copy(full.at[g, pl.ds(row, 288)], out.at[j], sems.at[len(copies)]))
    started(copies)
    vectors[...] = stacked([column_sums(du), column_sums(dm)], 8)
    finish(copies)


def mlp_grads(info, act, du, f, own, other, strips):
    rows = act.shape[0]
    return call(
        functools.partial(mlp_grads_body, strips),
        "mlp_grads",
        [(info, SMEM), (act, VMEM), (du, VMEM), (f, VMEM), (own, ANY), (other, ANY)],
        [((2, 288, WIDTH), bf16, ANY)] * 4 + [((8, WIDTH), f32, VMEM)],
        [pltpu.VMEM((rows, WIDTH), bf16), pltpu.VMEM((2, WIDTH, WIDTH), bf16)]
        + [pltpu.SemaphoreType.DMA((2,)), pltpu.SemaphoreType.DMA((8,))],
        flops=4 * rows * WIDTH * WIDTH,
    )


def half_way_body(near_keep, near_got, far_keep, far_got, near, far, near_send, far_send):
    for keep, got, mine, send in ((near_keep, near_got, near, near_send), (far_keep, far_got, far, far_send)):
        mine[...] = keep[0].astype(f32) + got[0].astype(f32)
        send[...] = (keep[1].astype(f32) + got[1].astype(f32)).astype(bf16)


def half_way(keeps, gots, after):
    return call(
        half_way_body,
        "half_way",
        [(a, VMEM) for a in (keeps[0], gots[0], keeps[1], gots[1])],
        [((288, WIDTH), f32, VMEM)] * 2 + [((288, WIDTH), bf16, VMEM)] * 2,
        after=after,
    )


def mlp_join_body(near_mine, near_got, far_mine, far_got, near, far):
    near[...] = near_mine[...] + near_got[...].astype(f32)
    far[...] = (far_mine[...] + far_got[...].astype(f32)).astype(bf16)


def mlp_join(mines, gots):
    return call(
        mlp_join_body,
        "mlp_join",
        [(a, VMEM) for a in (mines[0], gots[0], mines[1], gots[1])],
        [((288, WIDTH), f32, VMEM), ((288, WIDTH), bf16, VMEM)],
    )


def output_body(number, info, modulation, bias_out, hidden, g_mine, *rest):
    terms, (out, sums) = rest[:-2], rest[-2:]
    half = hidden.shape[0]
    parts = half // 64
    for t in range(parts):
        rows = slice(t * 64, (t + 1) * 64)
        mod = modulation[info[FIRST] + (info[HALF] * parts + t) // 2]
        m = all_terms(terms, rows) + bias_out[1:2, :]
        value = (hidden[rows, :] + mod[5:6] * m).astype(bf16)
        out[rows, :] = value
        sums[t : t + 1, :] = jnp.sum(g_mine[rows, :].astype(f32) * m, 0, keepdims=True)


def output_rows(info, modulation, bias_out, hidden, g_mine, terms, number):
    half = hidden.shape[0]
    return call(
        functools.partial(output_body, number),
        "output_rows",
        [(info, SMEM), (modulation, VMEM), (bias_out, VMEM), (hidden, VMEM), (g_mine, VMEM)]
        + [(t, VMEM) for t in terms],
        [((half, WIDTH), bf16, VMEM), ((half // 64, WIDTH), f32, VMEM)],
    )


def back_middle_body(number, info, modulation, hidden, attn, g_mine, *rest):
    terms, (dh, dat, sums) = rest[:-3], rest[-3:]
    half = hidden.shape[0]
    parts = half // 64
    for t in range(parts):
        rows = slice(t * 64, (t + 1) * 64)
        mod = modulation[info[FIRST] + (info[HALF] * parts + t) // 2]
        db = all_terms(terms, rows)
        normed, inverse = normalize(hidden[rows, :])
        grad = g_mine[rows, :].astype(f32) + norm_back(db * (1.0 + mod[4:5]), normed, inverse)
        dh[rows, :] = grad
        dat[rows, :] = (mod[2:3] * grad).astype(bf16)
        sums[3 * t : 3 * t + 1, :] = jnp.sum(grad * attn[rows, :], 0, keepdims=True)
        sums[3 * t + 1 : 3 * t + 2, :] = jnp.sum(db, 0, keepdims=True)
        sums[3 * t + 2 : 3 * t + 3, :] = jnp.sum(db * normed, 0, keepdims=True)


def back_middle(info, modulation, hidden, attn, g_mine, terms, number):
    half = hidden.shape[0]
    return call(
        functools.partial(back_middle_body, number),
        "back_middle",
        [(info, SMEM), (modulation, VMEM), (hidden, VMEM), (attn, VMEM), (g_mine, VMEM)]
        + [(t, VMEM) for t in terms],
        [((half, WIDTH), f32, VMEM), ((half, WIDTH), bf16, VMEM), ((3 * (half // 64), WIDTH), f32, VMEM)],
    )


def attend_back_body(number, info, near_w, far_w, near_qkv, far_qkv, near_p, far_p, s0, s1, s2, s3, *rest):
    dat, near_grad, far_grad, g0, g1, g2, g3, da, near_do, far_do, sems = rest
    copies = started(share_copies(info, (s0, s1, s2, s3), dat, sems))
    mask = head_mask()
    near_out, far_out = near_w[:, QKV:], far_w[:, QKV:]
    finish(copies)
    for rows in chunks_of(dat.shape[0], 384):
        near_do[rows, :] = dot(dat[rows, :], near_out).astype(bf16)
        far_do[rows, :] = dot(dat[rows, :], far_out).astype(bf16)
    for i in range(2 * number):
        rows = slice(i * KEPT, (i + 1) * KEPT)
        for do, qkv, probs, out in ((near_do, near_qkv, near_p, near_grad), (far_do, far_qkv, far_p, far_grad)):
            here = qkv[rows, :]
            q, k, v = (here[:, j * PAIRED : (j + 1) * PAIRED] for j in range(3))
            p = probs[i]
            both = split_heads(do[rows, :], mask)
            dp = dot_t(both, v)
            ds = (p * (dp - jnp.sum(p * dp, -1, keepdims=True))).astype(bf16)
            wide = jnp.concatenate([ds[:KEPT], ds[KEPT:]], 1)
            dq = dot(wide, split_heads(k, mask)) * score_scale
            dk = t_dot(ds, split_heads(q, mask)) * score_scale
            dv = t_dot(p.astype(bf16), both)
            out[rows, :] = jnp.concatenate([dq, dk, dv], 1).astype(bf16)
    near_in, far_in = near_w[:, :QKV], far_w[:, :QKV]
    for rows in chunks_of(dat.shape[0], 384):
        da[rows, :] = (dot_t(near_grad[rows, :], near_in) + dot_t(far_grad[rows, :], far_in)).astype(bf16)
    split_halves(info, da, (g0, g1, g2, g3))


def attend_back(info, near, far, pieces, number):
    rows = 2 * number * KEPT
    return call(
        functools.partial(attend_back_body, number),
        "attend_back",
        [(info, SMEM)]
        + [(a, VMEM) for a in (near[0], far[0], near[1], far[1], near[2], far[2])]
        + [(p, ANY) for p in pieces],
        [((rows, WIDTH), bf16, VMEM)] + [((rows, QKV), bf16, VMEM)] * 2 + halves_of(rows),
        [pltpu.VMEM((rows, WIDTH), bf16)]
        + [pltpu.VMEM((rows, PAIRED), bf16)] * 2
        + [pltpu.SemaphoreType.DMA((4,))],
        flops=4 * rows * WIDTH * 576,
    )


def attn_grads_body(strips, info, act, dat, near_grad, far_grad, near_o, far_o, vectors, o0, o1, o2, o3, mixed, full, extra, sems):
    mixed[...] = jnp.concatenate([near_o[...], far_o[...]], 1)
    for part in (slice(0, 512), slice(512, WIDTH)):
        parts = [t_dot(act[:, part], grad[...]) for grad in (near_grad, far_grad)]
        parts.append(t_dot(dat[:, part], mixed[...]))
        full[part, :] = jnp.concatenate(parts, 1).astype(bf16)
    sums = jnp.concatenate(
        [column_sums(near_grad), column_sums(far_grad), jnp.zeros((1, 2 * PAIRED), f32)], 1
    )
    rows = (sums, column_sums(dat), vectors[0:1, :], vectors[1:2, :])
    extra[...] = stacked([part for row in rows for part in two_rows(row)], 16).astype(bf16)
    finish(started(block_copies(strips, info, full, extra, (o0, o1, o2, o3), sems)))


def attn_grads(info, act, dat, grads, near_o, far_o, vectors, strips):
    rows = dat.shape[0]
    return call(
        functools.partial(attn_grads_body, strips),
        "attn_grads",
        [(info, SMEM)] + [(a, VMEM) for a in (act, dat, *grads, near_o, far_o, vectors)],
        [((2, SIDE + 16 * (k % 2), WIDTH) if strips else (304, WIDTH), bf16, ANY) for k in range(4)],
        [
            pltpu.VMEM((rows, 2 * PAIRED), bf16),
            pltpu.VMEM((WIDTH, WIDTH), bf16),
            pltpu.VMEM((16, WIDTH), bf16),
            pltpu.SemaphoreType.DMA((12,)),
        ],
        flops=2 * rows * WIDTH * WIDTH,
    )


def last_rows_body(number, info, modulation, x_mine, dh, *rest):
    terms, (back_sums, gate_sums, out, sums) = rest[:-4], rest[-4:]
    half = x_mine.shape[0]
    parts = half // 64
    sums[...] = jnp.zeros_like(sums)
    for t in range(parts):
        rows = slice(t * 64, (t + 1) * 64)
        mod = modulation[info[FIRST] + (info[HALF] * parts + t) // 2]
        da = all_terms(terms, rows)
        normed, inverse = normalize(x_mine[rows, :].astype(f32))
        out[rows, :] = (dh[rows, :] + norm_back(da * (1.0 + mod[1:2]), normed, inverse)).astype(bf16)
        sums[6 * t : 6 * t + 1, :] = jnp.sum(da, 0, keepdims=True)
        sums[6 * t + 1 : 6 * t + 2, :] = jnp.sum(da * normed, 0, keepdims=True)
        sums[6 * t + 2 : 6 * t + 5, :] = back_sums[3 * t : 3 * t + 3, :]
        sums[6 * t + 5 : 6 * t + 6, :] = gate_sums[t : t + 1, :]
    out[half:, :] = sums[...].astype(bf16)


def gather_last(last):
    near, far = over_head(last, 1), over_head(last, 2)
    pieces = [(last, 0, 0), (near, 1, 0)]
    at = 0
    for part in relay_two(far):
        pieces += [(part, 2, at), (over_head(part, 1), 3, at)]
        at += part.shape[0]
    return pieces


def last_rows(info, modulation, x_mine, dh, terms, back_sums, gate_sums, number):
    half = x_mine.shape[0]
    extra = -(-6 * (half // 64) // 16) * 16
    (out,) = call(
        functools.partial(last_rows_body, number),
        "last_rows",
        [(info, SMEM), (modulation, VMEM), (x_mine, VMEM), (dh, VMEM)]
        + [(t, VMEM) for t in terms]
        + [(back_sums, VMEM), (gate_sums, VMEM)],
        [((half + extra, WIDTH), bf16, VMEM)],
        [pltpu.VMEM((extra, WIDTH), f32)],
        cost=0,
    )
    return out, extra


def attn_half_body(keep_p, got_p, keep_q, got_q, mine_p, mine_q, send_p, send_q):
    for keep, got, mine, send in ((keep_p, got_p, mine_p, send_p), (keep_q, got_q, mine_q, send_q)):
        for j, out in ((0, mine), (1, send)):
            out[:SIDE, :] = (keep[j, :SIDE, :].astype(f32) + got[j, :SIDE, :].astype(f32)).astype(out.dtype)
            if keep.shape[1] > SIDE:
                extra = keep[j, SIDE:, :].astype(f32) + got[j, SIDE:, :].astype(f32)
                rows = [part for k in range(4) for part in two_rows(extra[2 * k : 2 * k + 1] + extra[2 * k + 1 : 2 * k + 2])]
                out[SIDE:, :] = stacked(rows, 16).astype(bf16).astype(out.dtype)


def attn_half(keeps, gots):
    shapes = [(SIDE, WIDTH), (SIDE + 16, WIDTH)]
    return call(
        attn_half_body,
        "attn_half",
        [(a, VMEM) for a in (keeps[0], gots[0], keeps[1], gots[1])],
        [(shape, kind, VMEM) for kind in (f32, bf16) for shape in shapes],
    )


def join_body(mine_p, got_p, mine_q, got_q, near, far, vectors):
    cut = 2 * QKV + PAIRED
    for at, mine, got in ((0, mine_p, got_p), (SIDE, mine_q, got_q)):
        total = mine[:SIDE, :] + got[:SIDE, :].astype(f32)
        near[at : at + SIDE, :] = jnp.concatenate([total[:, :QKV], total[:, 2 * QKV : cut]], 1)
        far[at : at + SIDE, :] = jnp.concatenate([total[:, QKV : 2 * QKV], total[:, cut:]], 1).astype(bf16)
    extra = mine_q[SIDE:, :] + got_q[SIDE:, :].astype(f32)
    qkv, dat, up, dm = (extra[2 * k : 2 * k + 1] + extra[2 * k + 1 : 2 * k + 2] for k in range(4))
    pad = lambda row: jnp.concatenate([row, jnp.zeros((1, UP - QKV), f32)], 1)
    rows = two_rows(pad(qkv[:, QKV : 2 * QKV])) + two_rows(up[:, UP:])
    both = [two_rows(dat), two_rows(dm)]
    rows += [part[:, c : c + UP] for pair in both for part in pair for c in (0, UP)]
    far[288:304, :] = stacked(rows, 16).astype(bf16)
    low = lambda value: value.astype(bf16).astype(f32)
    wide = lambda row: jnp.concatenate([row, jnp.zeros((1, WIDTH - UP), f32)], 1)
    vectors[...] = stacked(
        [wide(pad(qkv[:, :QKV])), wide(up[:, :UP])] + [low(pair[0]) + low(pair[1]) for pair in both], 8
    )


def join(mines, gots):
    return call(
        join_body,
        "attn_join",
        [(a, VMEM) for a in (mines[0], gots[0], mines[1], gots[1])],
        [((288, UP), f32, VMEM), ((304, UP), bf16, VMEM), ((8, WIDTH), f32, VMEM)],
    )


def strip_rows(info, near, got, keep, send):
    mine = pl.ds(pl.multiple_of(info[CORE] * SIDE, 16), SIDE)
    theirs = pl.ds(pl.multiple_of((1 - info[CORE]) * SIDE, 16), SIDE)
    keep[...] = near[mine, :] + got[mine, :].astype(f32)
    send[:SIDE, :] = (near[theirs, :] + got[theirs, :].astype(f32)).astype(bf16)


def mlp_strip(info, near, got):
    width = near.shape[1]
    return call(
        strip_rows,
        "mlp_strip",
        [(info, SMEM), (near, VMEM), (got, VMEM)],
        [((SIDE, width), f32, VMEM), ((SIDE, width), bf16, VMEM)],
    )


def attn_strip_body(info, near, vectors, got, keep, send, total):
    strip_rows(info, near, got, keep, send)
    extra = got[288:304, :].astype(f32)
    low = lambda value: value.astype(bf16).astype(f32)
    wide = lambda row: jnp.concatenate([row, jnp.zeros((1, WIDTH - UP), f32)], 1)
    rows, totals = [], []
    for k in range(2):
        pair = two_rows(vectors[k : k + 1, :UP] + extra[2 * k : 2 * k + 1] + extra[2 * k + 1 : 2 * k + 2])
        rows += pair
        totals.append(wide(low(pair[0]) + low(pair[1])))
    for k in range(2):
        at = 4 + 4 * k
        row = jnp.concatenate([extra[at + j : at + j + 1] + extra[at + 2 + j : at + 3 + j] for j in range(2)], 1)
        totals.append(vectors[2 + k : 3 + k, :] + row)
    send[SIDE:, :] = stacked(rows, 16).astype(bf16)
    total[...] = stacked(totals, 8)


def attn_strip(info, near, vectors, got):
    width = near.shape[1]
    return call(
        attn_strip_body,
        "attn_strip",
        [(info, SMEM), (near, VMEM), (vectors, VMEM), (got, VMEM)],
        [((SIDE, width), f32, VMEM), ((SIDE + 16, width), bf16, VMEM), ((8, WIDTH), f32, VMEM)],
    )


def shampoo_body(wide, chained, info, keep, got, left, right, left_root, right_root, master, *rest):
    out_g, out_l, out_r, out_m = rest[4:] if chained else rest
    core = info[CORE]
    for step in range(4 if wide else 2):

        @pl.when(pl.program_id(0) == step)
        def _(step=step):
            for j in range(4):
                column, half = (4 * (step // 2) + j, step % 2) if wide else (2 * step + j // 2, j % 2)
                columns = slice(column * SIDE, (column + 1) * SIDE)
                value = jnp.where(core == half, keep[:, columns], got[:SIDE, columns].astype(f32))
                out_g[j] = value
                low = value.astype(bf16)
                out_l[j] = decay_rate * left[j] + (1.0 - decay_rate) * dot_t(low, low)
                out_r[j] = decay_rate * right[j] + (1.0 - decay_rate) * t_dot(low, low)
                first = dot(left_root[j].astype(bf16), low).astype(bf16)
                out_m[j] = master[j] - weight_rate * dot(first, right_root[j].astype(bf16))


def shampoo(info, keep, got, states, previous, wide):
    first = 2 if wide else 0
    tiles = pl.BlockSpec((4, SIDE, SIDE), lambda i: (first + i, 0, 0))
    whole = lambda a: pl.BlockSpec(a.shape, lambda i: (0, 0))
    inputs = [(info, SMEM), (keep, whole(keep)), (got, whole(got))] + [(s, tiles) for s in states]
    aliases = None
    if previous is not None:
        aliases = {len(inputs) + k: k for k in range(4)}
        inputs += [(p, ANY) for p in previous]
    return call(
        functools.partial(shampoo_body, wide, previous is not None),
        "shampoo",
        inputs,
        [(states[0].shape, f32, tiles)] * 4,
        aliases=aliases,
        grid=(4 if wide else 2,),
    )


def heads_of(qkv, up):
    rows = []
    for j in range(2):
        rows.append(
            jnp.concatenate(
                [
                    qkv[:, j * HEAD_DIM : (j + 1) * HEAD_DIM],
                    qkv[:, 2 * PAIRED + j * HEAD_DIM : 2 * PAIRED + (j + 1) * HEAD_DIM],
                    up[:, j * 288 : (j + 1) * 288],
                ],
                1,
            )
        )
    return rows


def bias_body(info, total, got, b_in, s_in, b_out, s_out, g_in, m_in, n_in, g_out, m_out, n_out):
    there = got[SIDE : SIDE + 16, :].astype(f32)
    mine = heads_of(total[0:1, :QKV], total[1:2, :UP])
    theirs = heads_of((there[0:1] + there[1:2])[:, :QKV], there[2:3] + there[3:4])
    zero = info[CORE] == 0
    rows = [jnp.where(zero, a, b) for a, b in zip(mine, theirs)]
    rows += [jnp.where(zero, b, a) for a, b in zip(mine, theirs)]
    for grad, base, square, g_ref, m_ref, n_ref in (
        (stacked(rows, 4), b_in, s_in, g_in, m_in, n_in),
        (total[2:4, :], b_out, s_out, g_out, m_out, n_out),
    ):
        new = decay_rate * square[...] + (1.0 - decay_rate) * grad * grad
        g_ref[...] = grad
        m_ref[...] = new
        n_ref[...] = base[...] - bias_rate * grad / (jnp.sqrt(new) + root_epsilon)


def bias_step(info, total, got, bias_in, bias_in_sq, bias_out, bias_out_sq):
    arrays = [total, got, bias_in, bias_in_sq, bias_out, bias_out_sq]
    return call(
        bias_body,
        "bias_step",
        [(info, SMEM)] + [(a, VMEM) for a in arrays],
        [(bias_in.shape, f32, VMEM)] * 3 + [(bias_out.shape, f32, VMEM)] * 3,
    )


def pass_body(far, block, rows):
    size = block.shape[0]
    block[...] = far[:size, :]
    rows[...] = far[size:, :]


def pass_on(far, after):
    width = far.shape[1]
    return call(
        pass_body,
        "pass_on",
        [(far, VMEM)],
        [((far.shape[0] - 16, width), bf16, VMEM), ((16, width), bf16, VMEM)],
        after=after,
    )


def finish_whole(attn_blocks, mlp_blocks, states, biases, core, head):
    left_stat, right_stat, left_root, right_root, master = states
    bias_in, bias_in_sq, bias_out, bias_out_sq = biases
    far_of = lambda v: over_head(v, 2)

    def halves(near):
        both = lax.all_gather(near.astype(bf16), "core").astype(f32)
        return [part.reshape(8, SIDE, -1, SIDE).transpose(2, 0, 1, 3) for part in (both[0], both[1])]

    full = jnp.concatenate([b[:288] for b in attn_blocks], 0)
    near, far = (
        jnp.concatenate([full[:, a : a + QKV], full[:, b : b + PAIRED]], 1) for a, b in ((0, 864), (432, 1008))
    )
    a0, a1 = halves(near.astype(f32) + far_of(far).astype(f32))
    near, far = (jnp.concatenate(mlp_blocks[2 * g : 2 * g + 2], 0).reshape(WIDTH, WIDTH) for g in range(2))
    m0, m1 = halves(near.astype(f32) + far_of(far).astype(f32))
    attn = jnp.stack([a0, a1], 1).reshape(8, 8, SIDE, SIDE)
    tiles = jnp.concatenate([attn, m0[:4], m1[:4], m0[4:], m1[4:]], 0)
    tiles = tiles.transpose(1, 0, 2, 3).reshape(192, SIDE, SIDE)
    tiles = lax.psum_scatter(tiles, "sup", scatter_dimension=0, tiled=True)
    count = master.shape[0]
    grad = lax.dynamic_slice_in_dim(tiles, core * count, count, 0)
    low = grad.astype(bf16)
    product = lambda spec, a, b: jnp.einsum(spec, a.astype(bf16), b.astype(bf16), preferred_element_type=f32)
    left_new = decay_rate * left_stat + (1.0 - decay_rate) * product("kab,kcb->kac", low, low)
    right_new = decay_rate * right_stat + (1.0 - decay_rate) * product("kba,kbc->kac", low, low)
    step = product("kab,kbc->kac", product("kab,kbc->kac", left_root, low), right_root)
    master_new = master - weight_rate * step
    attn_rows = attn_blocks[0][288:304].astype(f32)
    rows = [attn_rows[2 * k] + attn_rows[2 * k + 1] for k in range(4)]
    vector = lax.psum(jnp.stack(rows, 0), "sup")
    qkv, dat, up, dm = vector[0][: 2 * QKV], vector[1], vector[2], vector[3]
    rows = jnp.stack([dat, dm], 0)
    swap = lax.psum(rows, HEAD_AXES) * 0.5
    qkv = qkv[:QKV] + far_of(qkv[QKV:])
    up = up[:UP] + far_of(up[UP:])
    parts = [jnp.concatenate(heads_of(qkv[None], up[None]), 0)]
    grad_in = lax.all_gather(parts[0], "core", axis=0, tiled=True)
    out = [grad, left_new, right_new, master_new]
    for g, b, s in ((grad_in, bias_in, bias_in_sq), (swap, bias_out, bias_out_sq)):
        new = decay_rate * s + (1.0 - decay_rate) * g * g
        out += [g, new, b - bias_rate * g / (jnp.sqrt(new) + root_epsilon)]
    return out


def on_device(
    tokens,
    cotangent,
    modulation,
    counts,
    master,
    left_stat,
    right_stat,
    left_root,
    right_root,
    bias_in,
    bias_in_sq,
    bias_out,
    bias_out_sq,
):
    images, slots, _ = tokens.shape
    core = lax.axis_index("core")
    head = lax.axis_index(HEAD_AXES)
    number = images // 2
    strips = master.shape[0] == 24
    place = lax.axis_index("sup") if strips else 0
    order = core if strips else 0
    info = jnp.stack(
        [jnp.asarray(v, jnp.int32) for v in (place, order, core, head, head % 2, (head // 2) * number, head // 2, 0)]
    )
    LAST[0] = None
    attn_mine, attn_other, bias_mine, mlp_mine, mlp_other = pack(
        info, master if strips else jnp.zeros((24, SIDE, SIDE), f32), bias_in
    )
    small = small_rows(counts, modulation)
    far_tokens, far_small = over_core(tokens), over_core(small)
    if strips:
        mlp_block = jnp.concatenate([mlp_mine, over_core(mlp_other)], 0)
        mlp_near = lax.all_gather(mlp_block, "sup")
        block = jnp.concatenate([attn_mine, over_core(attn_other), bias_mine], 0)
        far_block = over_head(block, 2)
        attn_near = gather_pieces(block)
    else:
        (attn_near, attn_far), (mlp_near, mlp_far) = whole_pieces(master, core)
        far_block = jnp.concatenate([attn_far[0], over_head(bias_mine, 2)], 0)
    act, dm_own, x_mine, g_mine = kept_rows(info, small, tokens, cotangent, far_small, far_tokens, number)
    dm_other = over_core(dm_own)
    if strips:
        mlp_far = over_head(relay(mlp_block, (far_block,)), 2)
    far_block, bias_far = pass_on(far_block, attn_near[1:])
    if strips:
        attn_far = gather_pieces(far_block)
    near = attend(info, act, bias_mine, attn_near, number)
    far = attend(info, act, bias_far, attn_far, number)
    if strips:
        mlp_far = lax.all_gather(relay(mlp_far), "sup")
    terms = sum_rows(project(info, near[0], far[0], near[3], far[3]))
    w_near = mlp_weights(info, mlp_near)
    hidden, attn, act_mine = middle(info, modulation, bias_out, x_mine, terms, number)
    act_far = over_head(act_mine, 1)
    w_far = mlp_weights(info, mlp_far)
    act_far = relay(act_far)
    pieces = (act_mine, act_far, over_core(act_mine), over_core(act_far))
    act_two, f, du, *db_parts = mlp(info, (bias_mine, bias_far), dm_own, dm_other, w_near, w_far, pieces, number)
    db_terms = sum_rows(db_parts)
    mlp_parts = down_rows(info, f, w_near[1], w_far[1])
    dh, dat_mine, back_sums = back_middle(info, modulation, hidden, attn, g_mine, db_terms, number)
    dat_far = over_head(dat_mine, 1)
    mlp_terms = sum_rows(mlp_parts)
    *mlp_blocks, vectors = mlp_grads(info, act_two, du, f, dm_own, dm_other, strips)
    if strips:
        gots = [over_sup(mlp_blocks[0], 1), over_sup(mlp_blocks[1], 2)]
    dat_far = relay(dat_far)
    output_mine, gate_sums = output_rows(info, modulation, bias_out, hidden, g_mine, mlp_terms, number)
    output_all = lax.all_gather(output_mine, HEAD_AXES, axis=0, tiled=True)
    dat_pieces = (dat_mine, dat_far, over_core(dat_mine), over_core(dat_far))
    dat, near_grad, far_grad, *da_parts = attend_back(info, near, far, dat_pieces, number)
    da_terms = sum_rows(da_parts, spare=0)
    if strips:
        near_mine, far_mine, near_send, far_send = half_way(mlp_blocks[2:], gots, (da_terms[1],))
        gots = [over_sup(near_send, 2), over_sup(far_send, 1)]
    attn_blocks = attn_grads(info, act, dat, (near_grad, far_grad), near[3], far[3], vectors, strips)
    last, extra = last_rows(info, modulation, x_mine, dh, da_terms, back_sums, gate_sums, number)
    half = x_mine.shape[0]

    states = (left_stat, right_stat, left_root, right_root, master)
    biases = (bias_in, bias_in_sq, bias_out, bias_out_sq)
    if strips:
        mlp_near_sum, mlp_far_sum = mlp_join((near_mine, far_mine), gots)
        mlp_far_got = over_head(mlp_far_sum, 2)
        attn_gots = [over_sup(attn_blocks[0], 1), over_sup(attn_blocks[1], 2)]
        mine_p, mine_q, send_p, send_q = attn_half(attn_blocks[2:], attn_gots)
        attn_gots = [over_sup(send_p, 2), over_sup(send_q, 1)]
        near_sum, far_sum, sums = join((mine_p, mine_q), attn_gots)
        far_got = over_head(far_sum, 2)
        last_pieces = gather_last(last)
        (output,) = expand_all(info, counts, output_all, images, slots)
        keep, send, total = attn_strip(info, near_sum, sums, far_got)
        got = over_core(send)
        mlp_keep, mlp_send = mlp_strip(info, mlp_near_sum, mlp_far_got)
        mlp_got = over_core(mlp_send)
        previous = shampoo(info, keep, got, states, None, False)
        grad_tokens, grad_modulation = expand(info, counts, half + extra, last_pieces, images, slots, extra)
        steps = bias_step(info, total, got, *biases)
        weights = shampoo(info, mlp_keep, mlp_got, states, previous, True)
        tail = list(weights) + list(steps)
    else:
        last_pieces = gather_last(last)
        grad_tokens, grad_modulation = expand(info, counts, half + extra, last_pieces, images, slots, extra)
        (output,) = expand_all(info, counts, output_all, images, slots)
        tail = finish_whole(attn_blocks, mlp_blocks, states, biases, core, head)
    return (output, grad_tokens, grad_modulation, *tail)


def solution(mesh):
    devices = mesh.devices
    inner = Mesh(
        devices.reshape(devices.shape[0] // 2, 2, 2, devices.shape[1] // 2), ("sup", "core", *HEAD_AXES)
    )
    seq = ("sup", "core")
    tile = P(("sup", "core", *HEAD_AXES), None, None)
    rows = P(seq, None, None)
    return jax.shard_map(
        on_device,
        mesh=inner,
        in_specs=(rows, rows, rows, P(seq, None), tile, tile, tile, tile, tile)
        + (P(HEAD_AXES, None), P(HEAD_AXES, None), P(), P()),
        out_specs=(rows, rows, P(seq, None, HEAD_AXES), tile, tile, tile, tile)
        + (P(HEAD_AXES, None),) * 3
        + (P(),) * 3,
        check_vma=False,
    )
```

```python
import functools

import jax
import jax.numpy as jnp
from jax import lax
from jax.experimental import pallas as pl
from jax.experimental.pallas import tpu as pltpu
from jax.sharding import Mesh, PartitionSpec as P

HEADS = 16
HEAD_DIM = 72
KEPT = 128
SIDE = 144
RANGES = 8
SLOTS = 24
WIDTH = 1152
QKV = 432
PAIRED = 144
UP = 576

norm_epsilon = 1e-06
decay_rate = 0.5
weight_rate = 0.3
bias_rate = 0.1
root_epsilon = 1e-08
score_scale = HEAD_DIM ** (-0.5)
bf16 = jnp.bfloat16
f32 = jnp.float32
CORE_SWAP = [(0, 1), (1, 0)]
HEAD_AXES = ("hp", "hq")

SUP, ORDER, CORE, HEAD, HALF, FIRST, GROUP = range(7)
ANY = pl.BlockSpec(memory_space=pl.ANY)
VMEM = pl.BlockSpec(memory_space=pltpu.VMEM)
SMEM = pl.BlockSpec(memory_space=pltpu.SMEM)


def dot(a, b):
    return lax.dot_general(a, b, (((1,), (0,)), ((), ())), preferred_element_type=f32)


def dot_t(a, b):
    return lax.dot_general(a, b, (((1,), (1,)), ((), ())), preferred_element_type=f32)


def t_dot(a, b):
    return lax.dot_general(a, b, (((0,), (0,)), ((), ())), preferred_element_type=f32)


def normalize(values):
    center = jnp.mean(values, -1, keepdims=True)
    centered = values - center
    inverse = lax.rsqrt(jnp.mean(centered * centered, -1, keepdims=True) + norm_epsilon)
    return (centered * inverse, inverse)


def norm_back(grad_in, normed, inverse):
    inner = jnp.mean(grad_in * normed, -1, keepdims=True)
    return inverse * (grad_in - jnp.mean(grad_in, -1, keepdims=True) - normed * inner)


def over_both(values):
    pairs = [(i, i ^ 5) for i in range(8)]
    return lax.ppermute(values, ("core", "hp", "hq"), pairs)


def over_core(values):
    return lax.ppermute(values, "core", CORE_SWAP)


def over_head(values, offset):
    return lax.ppermute(values, HEAD_AXES, [(i, i ^ offset) for i in range(4)])


def over_sup(values, offset):
    return lax.ppermute(values, "sup", [(i, i ^ offset) for i in range(4)])


def shaped(shape, dtype):
    return jax.ShapeDtypeStruct(shape, dtype)


LAST = [None]
VMEM_MIB = dict(mlp=32, mlp_grads=28, attend_back=26, down=20, kept_rows=20, attn_grads=24)
TIMES = dict(last_rows=10, relay_last=5, expand_rows=3, back_middle=10)
COST = 0.02


def call(body, name, inputs, outputs, scratch=(), flops=0, aliases=None, after=(), cost=0, grid=()):
    inputs = list(inputs)
    count = len(inputs)
    if LAST[0] is not None and all(LAST[0] is not array for array, _ in inputs):
        inputs.append((LAST[0], ANY))
    inputs += [(a, ANY) for a in after]
    arrays = [array for array, _ in inputs]
    shapes = [shaped(shape, dtype) for shape, dtype, _ in outputs]

    size = sum(a.size * a.dtype.itemsize for a in arrays[:count] + shapes)

    def ordered(*refs):
        return body(*refs[:count], *refs[len(arrays) :])

    results = pl.pallas_call(
        ordered,
        name=name,
        grid=grid,
        out_shape=shapes,
        in_specs=[spec for _, spec in inputs],
        out_specs=[spec for _, _, spec in outputs],
        scratch_shapes=list(scratch),
        input_output_aliases=aliases or {},
        cost_estimate=pl.CostEstimate(flops=int(1.0e9 * TIMES.get(name, 0.02)), bytes_accessed=0, transcendentals=0),
        compiler_params=pltpu.CompilerParams(vmem_limit_bytes=VMEM_MIB.get(name, 16) * 1024 * 1024),
    )(*arrays)
    LAST[0] = min(results, key=lambda a: a.size * a.dtype.itemsize)
    return results


def chunks_of(rows, size):
    return [slice(at, min(at + size, rows)) for at in range(0, rows, size)]


def started(copies):
    for copy in copies:
        copy.start()
    return copies


def finish(copies):
    for copy in copies:
        copy.wait()


def pack_body(info, master, bias, mine, other, rows, mlp_mine, mlp_other, held, sems):
    copies = started(
        [pltpu.make_async_copy(master.at[pl.ds(8 * k, 8)], held.at[pl.ds(8 * k, 8)], sems.at[k]) for k in range(3)]
    )
    core = info[CORE]
    heads = [jnp.where(core == 0, bias[j : j + 1, :], bias[j + 2 : j + 3, :]) for j in range(2)]
    both = lambda a, b: jnp.concatenate([heads[0][:, a:b], heads[1][:, a:b]], 1)
    blank = jnp.zeros((1, PAIRED), f32)
    first = jnp.concatenate([both(0, HEAD_DIM), blank, both(HEAD_DIM, 2 * HEAD_DIM), blank], 1)
    rows[...] = stacked(three_rows(first) + three_rows(both(2 * HEAD_DIM, QKV)), 16).astype(bf16)
    copies[0].wait()
    for out, half in ((mine, core), (other, 1 - core)):
        out[...] = jnp.concatenate([held[2 * k + half].astype(bf16) for k in range(4)], 1)
    finish(copies[1:])
    for out, half in ((mlp_mine, core), (mlp_other, 1 - core)):
        out[...] = jnp.concatenate(
            [held[8 + 8 * w + 4 * half + k].astype(bf16) for w in range(2) for k in range(4)], 1
        )


def pack(info, master, bias_in):
    outs = lambda width: [((SIDE, width), bf16, VMEM)] * 2
    return call(
        pack_body,
        "pack",
        [(info, SMEM), (master, ANY), (bias_in, VMEM)],
        outs(4 * SIDE) + [((16, 4 * SIDE), bf16, VMEM)] + outs(8 * SIDE),
        [pltpu.VMEM((24, SIDE, SIDE), f32), pltpu.SemaphoreType.DMA((3,))],
    )


def piece_copies(info, pieces, target, sems, sup=None):
    copies = []
    sup = info[SUP] if sup is None else sup
    for k in range(4):
        for j in range(2):
            row = ((sup ^ k) * 2 + (info[ORDER] ^ j)) * SIDE
            copies.append(
                pltpu.make_async_copy(
                    pieces[k].at[pl.ds(j * SIDE, SIDE)],
                    target.at[pl.ds(pl.multiple_of(row, 16), SIDE)],
                    sems.at[2 * k + j],
                )
            )
    return copies


def gather_pieces(block):
    return [block] + [over_sup(block, k) for k in (1, 2, 3)]


def whole_pieces(master, core):
    tiles = lax.all_gather(master.astype(bf16), ("sup", "core"), axis=0, tiled=True)
    slab = tiles.reshape(8, 24, SIDE, SIDE).transpose(1, 0, 2, 3).reshape(24, 8 * SIDE, SIDE)
    take = lambda k: lax.dynamic_index_in_dim(slab, k, 0, False)
    attn = jnp.concatenate([take(2 * k + core) for k in range(4)], 1)
    mlp = jnp.concatenate([take(8 + 8 * w + 4 * core + k) for w in range(2) for k in range(4)], 1)
    out = []
    far = over_head(attn, 2)
    pieces = [[part[288 * k : 288 * k + 288] for k in range(4)] for part in (attn, far)]
    return pieces, [p.reshape(4, 288, 2 * UP) for p in (mlp, over_head(mlp, 2))]


def later_body(mine, got, out):
    out[: mine.shape[0], :] = mine[...]
    out[mine.shape[0] :, :] = got[...]


def copies_body(mine, *rest):
    out = rest[-1]
    for k in range(out.shape[0]):
        out[k, : mine.shape[0], :] = mine[...]
        if len(rest) > 1:
            out[k, mine.shape[0] :, :] = rest[0][...]


def copies_of(parts, count):
    rows = sum(p.shape[0] for p in parts)
    return call(
        copies_body, "copies", [(p, VMEM) for p in parts], [((count, rows, parts[0].shape[1]), bf16, VMEM)]
    )[0]


def to_all(values, axis):
    return lax.all_to_all(values, axis, 0, 0)


def later_block(mine, got, after=()):
    rows = mine.shape[0] + got.shape[0]
    return call(
        later_body, "later_block", [(mine, VMEM), (got, VMEM)], [((rows, mine.shape[1]), bf16, VMEM)], after=after
    )[0]


def small_body(info, counts, modulation, tokens, out, part, sem):
    images = out.shape[0]
    copies = started([pltpu.make_async_copy(tokens.at[pl.ds(info[FIRST], part.shape[0])], part, sem)])
    out[:, :6, :] = modulation[...]
    place = lax.broadcasted_iota(jnp.int32, (2, WIDTH), 1)
    for i in range(images):
        row = jnp.zeros((2, WIDTH), f32)
        for s in range(RANGES):
            row = jnp.where(place == s, counts[i, s].astype(f32), row)
        out[i, 6:8, :] = row
    finish(copies)


def small_rows(info, counts, modulation, tokens):
    shape = (modulation.shape[0], 8, WIDTH)
    part = (tokens.shape[0] // 2, *tokens.shape[1:])
    return call(
        small_body,
        "small_rows",
        [(info, SMEM), (counts, SMEM), (modulation, VMEM), (tokens, ANY)],
        [(shape, f32, VMEM), (part, bf16, VMEM)],
        [pltpu.SemaphoreType.DMA],
    )


def kept_target_of(row, slot):
    target = jnp.full(slot.shape, -1.0, f32)
    start = jnp.zeros((1, 1), f32)
    for s in range(RANGES):
        number = row[:, s : s + 1]
        place = slot - s * SLOTS
        target = jnp.where((place >= 0) & (place < number), place + start, target)
        start = start + number
    return target


def rows_body(number, info, small, tokens, cotangent, far_small, far_tokens, act, dm, x_mine, g_mine, tok, cot, x_own, g_own, sems):
    first = info[FIRST]
    copies = started(
        [
            pltpu.make_async_copy(tokens.at[pl.ds(first, number)], tok.at[pl.ds(0, number)], sems.at[0]),
            pltpu.make_async_copy(far_tokens, tok.at[pl.ds(number, number)], sems.at[1]),
            pltpu.make_async_copy(cotangent.at[pl.ds(first, number)], cot, sems.at[2]),
        ]
    )
    finish(copies)
    slots = tok.shape[1]
    slot = lax.broadcasted_iota(jnp.int32, (1, slots), 1).astype(f32)
    place = lax.broadcasted_iota(jnp.int32, (KEPT, slots), 0).astype(f32)
    for i in range(2 * number):
        mod = (small if i < number else far_small)[first + i % number]
        select = (kept_target_of(mod[6:7], slot) == place).astype(f32).astype(bf16)
        rows = slice(i * KEPT, (i + 1) * KEPT)
        x = dot(select, tok[i])
        normed, _ = normalize(x)
        act[rows, :] = (normed * (1.0 + mod[1:2]) + mod[0:1]).astype(bf16)
        if i < number:
            x_own[rows, :] = x.astype(bf16)
            g = dot(select, cot[i])
            g_own[rows, :] = g.astype(bf16)
            dm[rows, :] = (mod[5:6] * g).astype(bf16)
    half = x_mine.shape[0]
    mine = pl.ds(pl.multiple_of(info[HALF] * half, 64), half)
    x_mine[...] = x_own[mine, :]
    g_mine[...] = g_own[mine, :]


def kept_rows(info, small, tokens, cotangent, far_small, far_tokens, number):
    slots = tokens.shape[1]
    rows = number * KEPT
    half = rows // 2
    return call(
        functools.partial(rows_body, number),
        "kept_rows",
        [(info, SMEM), (small, VMEM), (tokens, ANY), (cotangent, ANY), (far_small, VMEM), (far_tokens, ANY)],
        [((2 * rows, WIDTH), bf16, VMEM), ((rows, WIDTH), bf16, VMEM)] + [((half, WIDTH), bf16, VMEM)] * 2,
        [pltpu.VMEM((2 * number, slots, WIDTH), bf16), pltpu.VMEM((number, slots, WIDTH), bf16)]
        + [pltpu.VMEM((rows, WIDTH), bf16)] * 2
        + [pltpu.SemaphoreType.DMA((3,))],
        flops=6 * rows * slots * WIDTH,
    )


def spread_of(counts, image):
    parts = []
    start = 0
    slot = lax.broadcasted_iota(jnp.int32, (SLOTS, KEPT), 0)
    row = lax.broadcasted_iota(jnp.int32, (SLOTS, KEPT), 1)
    for s in range(RANGES):
        number = counts[image, s]
        parts.append(((row == slot + start) & (slot < number)).astype(f32))
        start = start + number
    return jnp.concatenate(parts, 0).astype(bf16)


def expand_body(images, extra, size, places, info, counts, *rest):
    pieces, (out, sums, held, sems) = rest[: len(places)], rest[len(places) :]
    half = size - extra
    copies = []
    for n, (k, at) in enumerate(places):
        row = pl.multiple_of((info[HEAD] ^ k) * size + at, 16)
        copies.append(pltpu.make_async_copy(pieces[n], held.at[pl.ds(row, pieces[n].shape[0])], sems.at[n]))
    finish(started(copies))
    parts = half // 64
    for i in range(images):
        spread = spread_of(counts, i)
        chunks = []
        for chunk in (2 * i, 2 * i + 1):
            row = (chunk // parts) * size + (chunk % parts) * 64
            chunks.append(held[row : row + 64, :])
        out[i] = dot(spread, jnp.concatenate(chunks, 0)).astype(bf16)
        if True:
            total = jnp.zeros((6, WIDTH), f32)
            for chunk in (2 * i, 2 * i + 1):
                base = (chunk // parts) * size + half
                block = held[base : base + extra, :].astype(f32)
                at = (chunk % parts) * 6
                total = total + block[at : at + 6]
            quarter = WIDTH // 4
            picked = total[:, :quarter]
            for k in range(1, 4):
                picked = jnp.where(info[HEAD] == k, total[:, k * quarter : (k + 1) * quarter], picked)
            sums[i] = picked


def expand(info, counts, size, pieces, images, slots, extra):
    return call(
        functools.partial(expand_body, images, extra, size, [(k, at) for _, k, at in pieces]),
        "expand_rows",
        [(info, SMEM), (counts, SMEM)] + [(p, ANY) for p, _, _ in pieces],
        [((images, slots, WIDTH), bf16, VMEM), ((images, 6, WIDTH // 4), f32, VMEM)],
        [pltpu.VMEM((4 * size, WIDTH), bf16), pltpu.SemaphoreType.DMA((len(pieces),))],
        flops=2 * images * slots * KEPT * WIDTH,
    )


def expand_all_body(images, info, counts, rows, out):
    for i in range(images):
        spread = spread_of(counts, i)
        out[i] = dot(spread, rows[i * KEPT : (i + 1) * KEPT, :]).astype(bf16)


def expand_all(info, counts, rows, images, slots):
    return call(
        functools.partial(expand_all_body, images),
        "expand_output",
        [(info, SMEM), (counts, SMEM), (rows, VMEM)],
        [((images, slots, WIDTH), bf16, VMEM)],
        flops=2 * images * slots * KEPT * WIDTH,
    )


def both_copies(own, other, target, sems):
    rows = target.shape[0] // 2
    return [
        pltpu.make_async_copy(ref, target.at[pl.ds(k * rows, rows)], sems.at[k]) for k, ref in enumerate((own, other))
    ]


def first_sum_body(mine, got, send):
    send[: mine.shape[0], :] = (mine[...].astype(f32) + got[...].astype(f32)).astype(send.dtype)
    if send.shape[0] > mine.shape[0]:
        send[mine.shape[0] :, :] = jnp.zeros((send.shape[0] - mine.shape[0], send.shape[1]), send.dtype)


def sum_rows(parts, kind=bf16, spare=0):
    own_send, own_keep, other_send, other_keep = parts
    got, got_keep = over_core(other_send), over_core(other_keep)
    rows, width = own_send.shape
    (send,) = call(first_sum_body, "first_sum", [(own_send, VMEM), (got, VMEM)], [((rows + spare, width), kind, VMEM)])
    return own_keep, got_keep, over_head(send, 1)


def relay_body(got, out):
    out[...] = got[...]


def relay_two_body(got, first, second):
    first[...] = got[: first.shape[0], :]
    second[...] = got[first.shape[0] :, :]


def relay_two(got):
    part = got.shape[0] // 32 * 16
    shapes = [(part, got.shape[1]), (got.shape[0] - part, got.shape[1])]
    return call(relay_two_body, "relay_last", [(got, VMEM)], [(shape, got.dtype, VMEM) for shape in shapes])


def relay(got, after=()):
    return call(relay_body, "relay", [(got, VMEM)], [(got.shape, got.dtype, VMEM)], after=after)[0]


def all_terms(terms, rows):
    total = terms[0][rows, :].astype(f32)
    for term in terms[1:]:
        total = total + term[rows, :].astype(f32)
    return total


def share_copies(info, pieces, target, sems):
    half = pieces[0].shape[0]
    copies = []
    for k in range(4):
        row = (k // 2) * 2 * half + (info[HALF] ^ (k % 2)) * half
        copies.append(
            pltpu.make_async_copy(pieces[k], target.at[pl.ds(pl.multiple_of(row, 64), half)], sems.at[k])
        )
    return copies


def split_halves(info, full, outs):
    half = outs[0].shape[0]
    for k in range(4):
        place = info[HALF] if k % 2 else 1 - info[HALF]
        outs[k][...] = full[pl.ds(pl.multiple_of((2 * (k // 2) + place) * half, 64), half), :].astype(bf16)


def head_mask():
    return lax.broadcasted_iota(jnp.int32, (KEPT, PAIRED), 1) < HEAD_DIM


def split_heads(values, mask):
    zero = jnp.zeros_like(values)
    return jnp.concatenate([jnp.where(mask, values, zero), jnp.where(mask, zero, values)], 0)


def sum_of_rows(ref, first):
    rows = ref[...].astype(f32)
    return rows[first : first + 1] + rows[first + 1 : first + 2] + rows[first + 2 : first + 3]


def attend_body(number, info, act, bias, w0, w1, w2, w3, weights, qkv, probs, mixed, sems):
    finish(started(piece_copies(info, (w0, w1, w2, w3), weights, sems)))
    mask = head_mask()
    bias = sum_of_rows(bias, 0)[:, :QKV]
    for rows in chunks_of(act.shape[0], 384):
        qkv[rows, :] = (dot(act[rows, :], weights[:, :QKV]) + bias).astype(bf16)
    for i in range(2 * number):
        rows = slice(i * KEPT, (i + 1) * KEPT)
        here = qkv[rows, :]
        q, k, v = (here[:, j * PAIRED : (j + 1) * PAIRED] for j in range(3))
        scores = dot_t(split_heads(q, mask), k) * score_scale
        raised = jnp.exp(scores - jnp.max(scores, -1, keepdims=True))
        p = raised / jnp.sum(raised, -1, keepdims=True)
        probs[i] = p
        low = p.astype(bf16)
        wide = jnp.concatenate([low[:KEPT], low[KEPT:]], 1)
        mixed[rows, :] = dot(wide, split_heads(v, mask)).astype(bf16)


def attend(info, act, bias, pieces, number):
    rows = 2 * number * KEPT
    return call(
        functools.partial(attend_body, number),
        "attend",
        [(info, SMEM), (act, VMEM), (bias, VMEM)] + [(p, ANY) for p in pieces],
        [
            ((WIDTH, QKV + PAIRED), bf16, VMEM),
            ((rows, QKV), bf16, VMEM),
            ((2 * number, 2 * KEPT, KEPT), f32, VMEM),
            ((rows, PAIRED), bf16, VMEM),
        ],
        [pltpu.SemaphoreType.DMA((8,))],
        flops=2 * rows * WIDTH * QKV,
    )


def project_body(info, near_w, far_w, near, far, *rest):
    outs, full = rest[:4], rest[4]
    wa = near_w[:, QKV:]
    wb = far_w[:, QKV:]
    for rows in chunks_of(near.shape[0], 384):
        full[rows, :] = (dot_t(near[rows, :], wa) + dot_t(far[rows, :], wb)).astype(bf16)
    split_halves(info, full, outs)


def halves_of(rows):
    return [((rows // 4, WIDTH), bf16, VMEM)] * 4


def project(info, near_w, far_w, near, far):
    rows = near.shape[0]
    return call(
        project_body,
        "project",
        [(info, SMEM), (near_w, VMEM), (far_w, VMEM), (near, VMEM), (far, VMEM)],
        halves_of(rows),
        [pltpu.VMEM((rows, WIDTH), bf16)],
        flops=4 * rows * WIDTH * PAIRED,
    )


def middle_body(number, info, modulation, bias_out, x_mine, *rest):
    terms, (hidden, attn, act) = rest[:-3], rest[-3:]
    half = x_mine.shape[0]
    parts = half // 64
    for t in range(parts):
        rows = slice(t * 64, (t + 1) * 64)
        mod = modulation[info[FIRST] + (info[HALF] * parts + t) // 2]
        a = all_terms(terms, rows) + bias_out[0:1, :]
        h = x_mine[rows, :].astype(f32) + mod[2:3] * a
        attn[rows, :] = a
        hidden[rows, :] = h
        normed, _ = normalize(h)
        act[rows, :] = (normed * (1.0 + mod[4:5]) + mod[3:4]).astype(bf16)


def middle(info, modulation, bias_out, x_mine, terms, number):
    half = x_mine.shape[0]
    return call(
        functools.partial(middle_body, number),
        "middle",
        [(info, SMEM), (modulation, VMEM), (bias_out, VMEM), (x_mine, VMEM)] + [(t, VMEM) for t in terms],
        [((half, WIDTH), f32, VMEM)] * 2 + [((half, WIDTH), bf16, VMEM)],
    )


def mlp_weights_body(relative, info, *refs):
    pieces, (up, down, held, sems) = refs[:4], refs[4:]
    finish(started(piece_copies(info, pieces, held, sems, None if relative else 0)))
    for i in range(8):
        rows = slice(i * SIDE, (i + 1) * SIDE)
        up[rows, :] = held[rows, :UP]
        down[rows, :] = held[rows, UP:]


def whole_body(info, whole, *refs):
    mlp_weights_body(False, info, *[whole.at[k] for k in range(4)], *refs)


def mlp_weights(info, pieces):
    relative = isinstance(pieces, list)
    arrays = pieces if relative else [pieces]
    return call(
        functools.partial(mlp_weights_body, True) if relative else whole_body,
        "mlp_weights",
        [(info, SMEM)] + [(p, ANY) for p in arrays],
        [((WIDTH, UP), bf16, VMEM)] * 2,
        [pltpu.VMEM((WIDTH, 2 * UP), bf16), pltpu.SemaphoreType.DMA((8,))],
    )


def smooth_both(u):
    c = 0.7978845608028654
    cube = 0.044715
    square = u * u
    t = jnp.tanh(c * u * (1.0 + cube * square))
    half_up = 0.5 * (1.0 + t)
    slope = half_up + 0.5 * u * (1.0 - t * t) * (c * (1.0 + 3.0 * cube * square))
    return u * half_up, slope


def mlp_body(number, info, near_bias, far_bias, own, other, near_up, near_down, far_up, far_down, s0, s1, s2, s3, *rest):
    act, f, du, g0, g1, g2, g3, db, dm, dm_sems, sems = rest
    copies = started(both_copies(own, other, dm, dm_sems))
    finish(copies + started(share_copies(info, (s0, s1, s2, s3), act, sems)))
    biases = [sum_of_rows(ref, 3) for ref in (near_bias, far_bias)]
    for rows in chunks_of(act.shape[0], 384):
        values, lows = [], []
        total = 0.0
        for g, (up, down) in enumerate(((near_up, near_down), (far_up, far_down))):
            u = dot(act[rows, :], up[...]) + biases[g]
            value, slope = smooth_both(u)
            low = (dot(dm[rows, :], down[...]) * slope).astype(bf16)
            total = total + dot_t(low, up[...])
            values.append(value.astype(bf16))
            lows.append(low)
        f[rows, :] = jnp.concatenate(values, 1)
        du[rows, :] = jnp.concatenate(lows, 1)
        db[rows, :] = total.astype(bf16)
    split_halves(info, db, (g0, g1, g2, g3))


def mlp(info, biases, own, other, near, far, pieces, number):
    rows = 2 * number * KEPT
    full = ((rows, WIDTH), bf16, VMEM)
    return call(
        functools.partial(mlp_body, number),
        "mlp",
        [(info, SMEM), (biases[0], VMEM), (biases[1], VMEM), (own, ANY), (other, ANY)]
        + [(a, VMEM) for a in (*near, *far)]
        + [(p, ANY) for p in pieces],
        [full] * 3 + halves_of(rows),
        [pltpu.VMEM((rows, WIDTH), bf16)] * 2 + [pltpu.SemaphoreType.DMA((2,)), pltpu.SemaphoreType.DMA((4,))],
        flops=6 * rows * WIDTH * WIDTH,
    )


def down_body(info, f, near_w, far_w, *rest):
    outs, full = rest[:4], rest[4]
    for rows in chunks_of(f.shape[0], 384):
        full[rows, :] = (dot_t(f[rows, :UP], near_w[...]) + dot_t(f[rows, UP:], far_w[...])).astype(bf16)
    split_halves(info, full, outs)


def down_rows(info, f, near_w, far_w):
    rows = f.shape[0]
    return call(
        down_body,
        "down",
        [(info, SMEM), (f, VMEM), (near_w, VMEM), (far_w, VMEM)],
        halves_of(rows),
        [pltpu.VMEM((rows, WIDTH), bf16)],
        flops=2 * rows * WIDTH * WIDTH,
    )


def two_rows(values):
    high = values.astype(bf16)
    return [high.astype(f32), values - high.astype(f32)]


def three_rows(values):
    high, rest = two_rows(values)
    return [high] + two_rows(rest)


def stacked(rows, count):
    width = rows[0].shape[1]
    place = lax.broadcasted_iota(jnp.int32, (count, width), 0)
    out = jnp.zeros((count, width), f32)
    for k, row in enumerate(rows):
        out = jnp.where(place == k, row, out)
    return out


def block_copies(strips, info, full, extra, outs, sems):
    copies = []

    def add(source, target):
        copies.append(pltpu.make_async_copy(source, target, sems.at[len(copies)]))

    if strips:
        moves = ((0, 0, (1, 3)), (1, 1, (2, 3)), (2, 0, (0, 2)), (3, 1, (0, 1)))
        for out, part, places in moves:
            for j, k in enumerate(places):
                row = pl.multiple_of((info[SUP] ^ k) * 288 + part * SIDE, 16)
                add(full.at[pl.ds(row, SIDE)], outs[out].at[j, pl.ds(0, SIDE)])
                if part:
                    add(extra, outs[out].at[j, pl.ds(SIDE, 16)])
    else:
        for k in range(4):
            add(full.at[pl.ds(k * 288, 288)], outs[k].at[pl.ds(0, 288)])
            add(extra, outs[k].at[pl.ds(288, 16)])
    return copies


def column_sums(ref):
    half = ref.shape[0] // 2
    first = jnp.sum(ref[:half, :].astype(f32), 0, keepdims=True)
    return first + jnp.sum(ref[half:, :].astype(f32), 0, keepdims=True)


def mlp_grads_body(strips, info, act, du, f, own, other, o0, o1, o2, o3, vectors, dm, full, dm_sems, sems):
    finish(started(both_copies(own, other, dm, dm_sems)))
    for part in (slice(0, 512), slice(512, WIDTH)):
        up = t_dot(act[:, part], du[...]).astype(bf16)
        down = t_dot(dm[:, part], f[...]).astype(bf16)
        for g in range(2):
            columns = slice(g * UP, (g + 1) * UP)
            full[g, part, :] = jnp.concatenate([up[:, columns], down[:, columns]], 1)
    if strips:
        moves = ((0, o0, (1, 3)), (1, o1, (2, 3)), (0, o2, (0, 2)), (1, o3, (0, 1)))
    else:
        moves = [(g, o, (2 * h, 2 * h + 1)) for g, h, o in ((0, 0, o0), (0, 1, o1), (1, 0, o2), (1, 1, o3))]
    copies = []
    for g, out, places in moves:
        for j, k in enumerate(places):
            row = pl.multiple_of((info[SUP] ^ k) * 288, 16)
            copies.append(pltpu.make_async_copy(full.at[g, pl.ds(row, 288)], out.at[j], sems.at[len(copies)]))
    started(copies)
    vectors[...] = stacked([column_sums(du), column_sums(dm)], 8)
    finish(copies)


def mlp_grads(info, act, du, f, own, other, strips):
    rows = act.shape[0]
    return call(
        functools.partial(mlp_grads_body, strips),
        "mlp_grads",
        [(info, SMEM), (act, VMEM), (du, VMEM), (f, VMEM), (own, ANY), (other, ANY)],
        [((2, 288, WIDTH), bf16, ANY)] * 4 + [((8, WIDTH), f32, VMEM)],
        [pltpu.VMEM((rows, WIDTH), bf16), pltpu.VMEM((2, WIDTH, WIDTH), bf16)]
        + [pltpu.SemaphoreType.DMA((2,)), pltpu.SemaphoreType.DMA((8,))],
        flops=4 * rows * WIDTH * WIDTH,
    )


def half_way_body(near_keep, near_got, far_keep, far_got, near, far, near_send, far_send):
    for keep, got, mine, send in ((near_keep, near_got, near, near_send), (far_keep, far_got, far, far_send)):
        mine[...] = keep[0].astype(f32) + got[0].astype(f32)
        send[...] = (keep[1].astype(f32) + got[1].astype(f32)).astype(bf16)


def half_way(keeps, gots, after):
    return call(
        half_way_body,
        "half_way",
        [(a, VMEM) for a in (keeps[0], gots[0], keeps[1], gots[1])],
        [((288, WIDTH), f32, VMEM)] * 2 + [((288, WIDTH), bf16, VMEM)] * 2,
        after=after,
    )


def mlp_join_body(near_mine, near_got, far_mine, far_got, near, far):
    near[...] = near_mine[...] + near_got[...].astype(f32)
    far[...] = (far_mine[...] + far_got[...].astype(f32)).astype(bf16)


def mlp_join(mines, gots):
    return call(
        mlp_join_body,
        "mlp_join",
        [(a, VMEM) for a in (mines[0], gots[0], mines[1], gots[1])],
        [((288, WIDTH), f32, VMEM), ((288, WIDTH), bf16, VMEM)],
    )


def output_body(number, info, modulation, bias_out, hidden, g_mine, *rest):
    terms, (out, sums) = rest[:-2], rest[-2:]
    half = hidden.shape[0]
    parts = half // 64
    for t in range(parts):
        rows = slice(t * 64, (t + 1) * 64)
        mod = modulation[info[FIRST] + (info[HALF] * parts + t) // 2]
        m = all_terms(terms, rows) + bias_out[1:2, :]
        value = (hidden[rows, :] + mod[5:6] * m).astype(bf16)
        out[rows, :] = value
        sums[t : t + 1, :] = jnp.sum(g_mine[rows, :].astype(f32) * m, 0, keepdims=True)


def output_rows(info, modulation, bias_out, hidden, g_mine, terms, number):
    half = hidden.shape[0]
    return call(
        functools.partial(output_body, number),
        "output_rows",
        [(info, SMEM), (modulation, VMEM), (bias_out, VMEM), (hidden, VMEM), (g_mine, VMEM)]
        + [(t, VMEM) for t in terms],
        [((half, WIDTH), bf16, VMEM), ((half // 64, WIDTH), f32, VMEM)],
    )


def back_middle_body(number, info, modulation, hidden, attn, g_mine, *rest):
    terms, (dh, dat, sums) = rest[:-3], rest[-3:]
    half = hidden.shape[0]
    parts = half // 64
    for t in range(parts):
        rows = slice(t * 64, (t + 1) * 64)
        mod = modulation[info[FIRST] + (info[HALF] * parts + t) // 2]
        db = all_terms(terms, rows)
        normed, inverse = normalize(hidden[rows, :])
        grad = g_mine[rows, :].astype(f32) + norm_back(db * (1.0 + mod[4:5]), normed, inverse)
        dh[rows, :] = grad
        dat[rows, :] = (mod[2:3] * grad).astype(bf16)
        sums[3 * t : 3 * t + 1, :] = jnp.sum(grad * attn[rows, :], 0, keepdims=True)
        sums[3 * t + 1 : 3 * t + 2, :] = jnp.sum(db, 0, keepdims=True)
        sums[3 * t + 2 : 3 * t + 3, :] = jnp.sum(db * normed, 0, keepdims=True)


def back_middle(info, modulation, hidden, attn, g_mine, terms, number):
    half = hidden.shape[0]
    return call(
        functools.partial(back_middle_body, number),
        "back_middle",
        [(info, SMEM), (modulation, VMEM), (hidden, VMEM), (attn, VMEM), (g_mine, VMEM)]
        + [(t, VMEM) for t in terms],
        [((half, WIDTH), f32, VMEM), ((half, WIDTH), bf16, VMEM), ((3 * (half // 64), WIDTH), f32, VMEM)],
    )


def attend_back_body(number, info, near_w, far_w, near_qkv, far_qkv, near_p, far_p, s0, s1, s2, s3, *rest):
    dat, near_grad, far_grad, g0, g1, g2, g3, da, near_do, far_do, sems = rest
    copies = started(share_copies(info, (s0, s1, s2, s3), dat, sems))
    mask = head_mask()
    near_out, far_out = near_w[:, QKV:], far_w[:, QKV:]
    finish(copies)
    for rows in chunks_of(dat.shape[0], 384):
        near_do[rows, :] = dot(dat[rows, :], near_out).astype(bf16)
        far_do[rows, :] = dot(dat[rows, :], far_out).astype(bf16)
    for i in range(2 * number):
        rows = slice(i * KEPT, (i + 1) * KEPT)
        for do, qkv, probs, out in ((near_do, near_qkv, near_p, near_grad), (far_do, far_qkv, far_p, far_grad)):
            here = qkv[rows, :]
            q, k, v = (here[:, j * PAIRED : (j + 1) * PAIRED] for j in range(3))
            p = probs[i]
            both = split_heads(do[rows, :], mask)
            dp = dot_t(both, v)
            ds = (p * (dp - jnp.sum(p * dp, -1, keepdims=True))).astype(bf16)
            wide = jnp.concatenate([ds[:KEPT], ds[KEPT:]], 1)
            dq = dot(wide, split_heads(k, mask)) * score_scale
            dk = t_dot(ds, split_heads(q, mask)) * score_scale
            dv = t_dot(p.astype(bf16), both)
            out[rows, :] = jnp.concatenate([dq, dk, dv], 1).astype(bf16)
    near_in, far_in = near_w[:, :QKV], far_w[:, :QKV]
    for rows in chunks_of(dat.shape[0], 384):
        da[rows, :] = (dot_t(near_grad[rows, :], near_in) + dot_t(far_grad[rows, :], far_in)).astype(bf16)
    split_halves(info, da, (g0, g1, g2, g3))


def attend_back(info, near, far, pieces, number):
    rows = 2 * number * KEPT
    return call(
        functools.partial(attend_back_body, number),
        "attend_back",
        [(info, SMEM)]
        + [(a, VMEM) for a in (near[0], far[0], near[1], far[1], near[2], far[2])]
        + [(p, ANY) for p in pieces],
        [((rows, WIDTH), bf16, VMEM)] + [((rows, QKV), bf16, VMEM)] * 2 + halves_of(rows),
        [pltpu.VMEM((rows, WIDTH), bf16)]
        + [pltpu.VMEM((rows, PAIRED), bf16)] * 2
        + [pltpu.SemaphoreType.DMA((4,))],
        flops=4 * rows * WIDTH * 576,
    )


def attn_grads_body(strips, info, act, dat, near_grad, far_grad, near_o, far_o, vectors, o0, o1, o2, o3, mixed, full, extra, sems):
    mixed[...] = jnp.concatenate([near_o[...], far_o[...]], 1)
    for part in (slice(0, 512), slice(512, WIDTH)):
        parts = [t_dot(act[:, part], grad[...]) for grad in (near_grad, far_grad)]
        parts.append(t_dot(dat[:, part], mixed[...]))
        full[part, :] = jnp.concatenate(parts, 1).astype(bf16)
    sums = jnp.concatenate(
        [column_sums(near_grad), column_sums(far_grad), jnp.zeros((1, 2 * PAIRED), f32)], 1
    )
    rows = (sums, column_sums(dat), vectors[0:1, :], vectors[1:2, :])
    extra[...] = stacked([part for row in rows for part in two_rows(row)], 16).astype(bf16)
    finish(started(block_copies(strips, info, full, extra, (o0, o1, o2, o3), sems)))


def attn_grads(info, act, dat, grads, near_o, far_o, vectors, strips):
    rows = dat.shape[0]
    return call(
        functools.partial(attn_grads_body, strips),
        "attn_grads",
        [(info, SMEM)] + [(a, VMEM) for a in (act, dat, *grads, near_o, far_o, vectors)],
        [((2, SIDE + 16 * (k % 2), WIDTH) if strips else (304, WIDTH), bf16, ANY) for k in range(4)],
        [
            pltpu.VMEM((rows, 2 * PAIRED), bf16),
            pltpu.VMEM((WIDTH, WIDTH), bf16),
            pltpu.VMEM((16, WIDTH), bf16),
            pltpu.SemaphoreType.DMA((12,)),
        ],
        flops=2 * rows * WIDTH * WIDTH,
    )


def last_rows_body(number, info, modulation, x_mine, dh, *rest):
    terms, (back_sums, gate_sums, out, sums) = rest[:-4], rest[-4:]
    half = x_mine.shape[0]
    parts = half // 64
    sums[...] = jnp.zeros_like(sums)
    for t in range(parts):
        rows = slice(t * 64, (t + 1) * 64)
        mod = modulation[info[FIRST] + (info[HALF] * parts + t) // 2]
        da = all_terms(terms, rows)
        normed, inverse = normalize(x_mine[rows, :].astype(f32))
        out[rows, :] = (dh[rows, :] + norm_back(da * (1.0 + mod[1:2]), normed, inverse)).astype(bf16)
        sums[6 * t : 6 * t + 1, :] = jnp.sum(da, 0, keepdims=True)
        sums[6 * t + 1 : 6 * t + 2, :] = jnp.sum(da * normed, 0, keepdims=True)
        sums[6 * t + 2 : 6 * t + 5, :] = back_sums[3 * t : 3 * t + 3, :]
        sums[6 * t + 5 : 6 * t + 6, :] = gate_sums[t : t + 1, :]
    out[half:, :] = sums[...].astype(bf16)


def gather_last(last):
    near, far = over_head(last, 1), over_head(last, 2)
    pieces = [(last, 0, 0), (near, 1, 0)]
    at = 0
    for part in relay_two(far):
        pieces += [(part, 2, at), (over_head(part, 1), 3, at)]
        at += part.shape[0]
    return pieces


def last_rows(info, modulation, x_mine, dh, terms, back_sums, gate_sums, number):
    half = x_mine.shape[0]
    extra = -(-6 * (half // 64) // 16) * 16
    (out,) = call(
        functools.partial(last_rows_body, number),
        "last_rows",
        [(info, SMEM), (modulation, VMEM), (x_mine, VMEM), (dh, VMEM)]
        + [(t, VMEM) for t in terms]
        + [(back_sums, VMEM), (gate_sums, VMEM)],
        [((half + extra, WIDTH), bf16, VMEM)],
        [pltpu.VMEM((extra, WIDTH), f32)],
        cost=0,
    )
    return out, extra


def attn_half_body(keep_p, got_p, keep_q, got_q, mine_p, mine_q, send_p, send_q):
    for keep, got, mine, send in ((keep_p, got_p, mine_p, send_p), (keep_q, got_q, mine_q, send_q)):
        for j, out in ((0, mine), (1, send)):
            out[:SIDE, :] = (keep[j, :SIDE, :].astype(f32) + got[j, :SIDE, :].astype(f32)).astype(out.dtype)
            if keep.shape[1] > SIDE:
                extra = keep[j, SIDE:, :].astype(f32) + got[j, SIDE:, :].astype(f32)
                rows = [part for k in range(4) for part in two_rows(extra[2 * k : 2 * k + 1] + extra[2 * k + 1 : 2 * k + 2])]
                out[SIDE:, :] = stacked(rows, 16).astype(bf16).astype(out.dtype)


def attn_half(keeps, gots):
    shapes = [(SIDE, WIDTH), (SIDE + 16, WIDTH)]
    return call(
        attn_half_body,
        "attn_half",
        [(a, VMEM) for a in (keeps[0], gots[0], keeps[1], gots[1])],
        [(shape, kind, VMEM) for kind in (f32, bf16) for shape in shapes],
    )


def join_body(mine_p, got_p, mine_q, got_q, near, far, vectors):
    cut = 2 * QKV + PAIRED
    for at, mine, got in ((0, mine_p, got_p), (SIDE, mine_q, got_q)):
        total = mine[:SIDE, :] + got[:SIDE, :].astype(f32)
        near[at : at + SIDE, :] = jnp.concatenate([total[:, :QKV], total[:, 2 * QKV : cut]], 1)
        far[at : at + SIDE, :] = jnp.concatenate([total[:, QKV : 2 * QKV], total[:, cut:]], 1).astype(bf16)
    extra = mine_q[SIDE:, :] + got_q[SIDE:, :].astype(f32)
    qkv, dat, up, dm = (extra[2 * k : 2 * k + 1] + extra[2 * k + 1 : 2 * k + 2] for k in range(4))
    pad = lambda row: jnp.concatenate([row, jnp.zeros((1, UP - QKV), f32)], 1)
    rows = two_rows(pad(qkv[:, QKV : 2 * QKV])) + two_rows(up[:, UP:])
    both = [two_rows(dat), two_rows(dm)]
    rows += [part[:, c : c + UP] for pair in both for part in pair for c in (0, UP)]
    far[288:304, :] = stacked(rows, 16).astype(bf16)
    low = lambda value: value.astype(bf16).astype(f32)
    wide = lambda row: jnp.concatenate([row, jnp.zeros((1, WIDTH - UP), f32)], 1)
    vectors[...] = stacked(
        [wide(pad(qkv[:, :QKV])), wide(up[:, :UP])] + [low(pair[0]) + low(pair[1]) for pair in both], 8
    )


def join(mines, gots):
    return call(
        join_body,
        "attn_join",
        [(a, VMEM) for a in (mines[0], gots[0], mines[1], gots[1])],
        [((288, UP), f32, VMEM), ((304, UP), bf16, VMEM), ((8, WIDTH), f32, VMEM)],
    )


def strip_rows(info, near, got, keep, send):
    mine = pl.ds(pl.multiple_of(info[CORE] * SIDE, 16), SIDE)
    theirs = pl.ds(pl.multiple_of((1 - info[CORE]) * SIDE, 16), SIDE)
    keep[...] = near[mine, :] + got[mine, :].astype(f32)
    send[:SIDE, :] = (near[theirs, :] + got[theirs, :].astype(f32)).astype(bf16)


def mlp_strip(info, near, got):
    width = near.shape[1]
    return call(
        strip_rows,
        "mlp_strip",
        [(info, SMEM), (near, VMEM), (got, VMEM)],
        [((SIDE, width), f32, VMEM), ((SIDE, width), bf16, VMEM)],
    )


def attn_strip_body(info, near, vectors, got, keep, send, total):
    strip_rows(info, near, got, keep, send)
    extra = got[288:304, :].astype(f32)
    low = lambda value: value.astype(bf16).astype(f32)
    wide = lambda row: jnp.concatenate([row, jnp.zeros((1, WIDTH - UP), f32)], 1)
    rows, totals = [], []
    for k in range(2):
        pair = two_rows(vectors[k : k + 1, :UP] + extra[2 * k : 2 * k + 1] + extra[2 * k + 1 : 2 * k + 2])
        rows += pair
        totals.append(wide(low(pair[0]) + low(pair[1])))
    for k in range(2):
        at = 4 + 4 * k
        row = jnp.concatenate([extra[at + j : at + j + 1] + extra[at + 2 + j : at + 3 + j] for j in range(2)], 1)
        totals.append(vectors[2 + k : 3 + k, :] + row)
    send[SIDE:, :] = stacked(rows, 16).astype(bf16)
    total[...] = stacked(totals, 8)


def attn_strip(info, near, vectors, got):
    width = near.shape[1]
    return call(
        attn_strip_body,
        "attn_strip",
        [(info, SMEM), (near, VMEM), (vectors, VMEM), (got, VMEM)],
        [((SIDE, width), f32, VMEM), ((SIDE + 16, width), bf16, VMEM), ((8, WIDTH), f32, VMEM)],
    )


def shampoo_body(wide, chained, info, keep, got, left, right, left_root, right_root, master, *rest):
    out_g, out_l, out_r, out_m = rest[4:] if chained else rest
    core = info[CORE]
    for step in range(4 if wide else 2):

        @pl.when(pl.program_id(0) == step)
        def _(step=step):
            for j in range(4):
                column, half = (4 * (step // 2) + j, step % 2) if wide else (2 * step + j // 2, j % 2)
                columns = slice(column * SIDE, (column + 1) * SIDE)
                value = jnp.where(core == half, keep[:, columns], got[:SIDE, columns].astype(f32))
                out_g[j] = value
                low = value.astype(bf16)
                out_l[j] = decay_rate * left[j] + (1.0 - decay_rate) * dot_t(low, low)
                out_r[j] = decay_rate * right[j] + (1.0 - decay_rate) * t_dot(low, low)
                first = dot(left_root[j].astype(bf16), low).astype(bf16)
                out_m[j] = master[j] - weight_rate * dot(first, right_root[j].astype(bf16))


def shampoo(info, keep, got, states, previous, wide):
    first = 2 if wide else 0
    tiles = pl.BlockSpec((4, SIDE, SIDE), lambda i: (first + i, 0, 0))
    whole = lambda a: pl.BlockSpec(a.shape, lambda i: (0, 0))
    inputs = [(info, SMEM), (keep, whole(keep)), (got, whole(got))] + [(s, tiles) for s in states]
    aliases = None
    if previous is not None:
        aliases = {len(inputs) + k: k for k in range(4)}
        inputs += [(p, ANY) for p in previous]
    return call(
        functools.partial(shampoo_body, wide, previous is not None),
        "shampoo",
        inputs,
        [(states[0].shape, f32, tiles)] * 4,
        aliases=aliases,
        grid=(4 if wide else 2,),
    )


def heads_of(qkv, up):
    rows = []
    for j in range(2):
        rows.append(
            jnp.concatenate(
                [
                    qkv[:, j * HEAD_DIM : (j + 1) * HEAD_DIM],
                    qkv[:, 2 * PAIRED + j * HEAD_DIM : 2 * PAIRED + (j + 1) * HEAD_DIM],
                    up[:, j * 288 : (j + 1) * 288],
                ],
                1,
            )
        )
    return rows


def bias_body(info, total, got, b_in, s_in, b_out, s_out, g_in, m_in, n_in, g_out, m_out, n_out):
    there = got[SIDE : SIDE + 16, :].astype(f32)
    mine = heads_of(total[0:1, :QKV], total[1:2, :UP])
    theirs = heads_of((there[0:1] + there[1:2])[:, :QKV], there[2:3] + there[3:4])
    zero = info[CORE] == 0
    rows = [jnp.where(zero, a, b) for a, b in zip(mine, theirs)]
    rows += [jnp.where(zero, b, a) for a, b in zip(mine, theirs)]
    for grad, base, square, g_ref, m_ref, n_ref in (
        (stacked(rows, 4), b_in, s_in, g_in, m_in, n_in),
        (total[2:4, :], b_out, s_out, g_out, m_out, n_out),
    ):
        new = decay_rate * square[...] + (1.0 - decay_rate) * grad * grad
        g_ref[...] = grad
        m_ref[...] = new
        n_ref[...] = base[...] - bias_rate * grad / (jnp.sqrt(new) + root_epsilon)


def bias_step(info, total, got, bias_in, bias_in_sq, bias_out, bias_out_sq):
    arrays = [total, got, bias_in, bias_in_sq, bias_out, bias_out_sq]
    return call(
        bias_body,
        "bias_step",
        [(info, SMEM)] + [(a, VMEM) for a in arrays],
        [(bias_in.shape, f32, VMEM)] * 3 + [(bias_out.shape, f32, VMEM)] * 3,
    )


def pass_body(far, block, rows):
    size = block.shape[0]
    block[...] = far[:size, :]
    rows[...] = far[size:, :]


def pass_on(far, after):
    width = far.shape[1]
    return call(
        pass_body,
        "pass_on",
        [(far, VMEM)],
        [((far.shape[0] - 16, width), bf16, VMEM), ((16, width), bf16, VMEM)],
        after=after,
    )


def finish_whole(attn_blocks, mlp_blocks, states, biases, core, head):
    left_stat, right_stat, left_root, right_root, master = states
    bias_in, bias_in_sq, bias_out, bias_out_sq = biases
    far_of = lambda v: over_head(v, 2)

    def halves(near):
        both = lax.all_gather(near.astype(bf16), "core").astype(f32)
        return [part.reshape(8, SIDE, -1, SIDE).transpose(2, 0, 1, 3) for part in (both[0], both[1])]

    full = jnp.concatenate([b[:288] for b in attn_blocks], 0)
    near, far = (
        jnp.concatenate([full[:, a : a + QKV], full[:, b : b + PAIRED]], 1) for a, b in ((0, 864), (432, 1008))
    )
    a0, a1 = halves(near.astype(f32) + far_of(far).astype(f32))
    near, far = (jnp.concatenate(mlp_blocks[2 * g : 2 * g + 2], 0).reshape(WIDTH, WIDTH) for g in range(2))
    m0, m1 = halves(near.astype(f32) + far_of(far).astype(f32))
    attn = jnp.stack([a0, a1], 1).reshape(8, 8, SIDE, SIDE)
    tiles = jnp.concatenate([attn, m0[:4], m1[:4], m0[4:], m1[4:]], 0)
    tiles = tiles.transpose(1, 0, 2, 3).reshape(192, SIDE, SIDE)
    tiles = lax.psum_scatter(tiles, "sup", scatter_dimension=0, tiled=True)
    count = master.shape[0]
    grad = lax.dynamic_slice_in_dim(tiles, core * count, count, 0)
    low = grad.astype(bf16)
    product = lambda spec, a, b: jnp.einsum(spec, a.astype(bf16), b.astype(bf16), preferred_element_type=f32)
    left_new = decay_rate * left_stat + (1.0 - decay_rate) * product("kab,kcb->kac", low, low)
    right_new = decay_rate * right_stat + (1.0 - decay_rate) * product("kba,kbc->kac", low, low)
    step = product("kab,kbc->kac", product("kab,kbc->kac", left_root, low), right_root)
    master_new = master - weight_rate * step
    attn_rows = attn_blocks[0][288:304].astype(f32)
    rows = [attn_rows[2 * k] + attn_rows[2 * k + 1] for k in range(4)]
    vector = lax.psum(jnp.stack(rows, 0), "sup")
    qkv, dat, up, dm = vector[0][: 2 * QKV], vector[1], vector[2], vector[3]
    rows = jnp.stack([dat, dm], 0)
    swap = lax.psum(rows, HEAD_AXES) * 0.5
    qkv = qkv[:QKV] + far_of(qkv[QKV:])
    up = up[:UP] + far_of(up[UP:])
    parts = [jnp.concatenate(heads_of(qkv[None], up[None]), 0)]
    grad_in = lax.all_gather(parts[0], "core", axis=0, tiled=True)
    out = [grad, left_new, right_new, master_new]
    for g, b, s in ((grad_in, bias_in, bias_in_sq), (swap, bias_out, bias_out_sq)):
        new = decay_rate * s + (1.0 - decay_rate) * g * g
        out += [g, new, b - bias_rate * g / (jnp.sqrt(new) + root_epsilon)]
    return out


def on_device(
    tokens,
    cotangent,
    modulation,
    counts,
    master,
    left_stat,
    right_stat,
    left_root,
    right_root,
    bias_in,
    bias_in_sq,
    bias_out,
    bias_out_sq,
):
    images, slots, _ = tokens.shape
    core = lax.axis_index("core")
    head = lax.axis_index(HEAD_AXES)
    number = images // 2
    strips = master.shape[0] == 24
    place = lax.axis_index("sup") if strips else 0
    order = core if strips else 0
    info = jnp.stack(
        [jnp.asarray(v, jnp.int32) for v in (place, order, core, head, head % 2, (head // 2) * number, head // 2, 0)]
    )
    LAST[0] = None
    attn_mine, attn_other, bias_mine, mlp_mine, mlp_other = pack(
        info, master if strips else jnp.zeros((24, SIDE, SIDE), f32), bias_in
    )
    small, part = small_rows(info, counts, modulation, tokens)
    far_tokens, far_small = over_core(part), over_core(small)
    if strips:
        mlp_block = jnp.concatenate([mlp_mine, over_core(mlp_other)], 0)
        mlp_near = lax.all_gather(mlp_block, "sup")
        block = jnp.concatenate([attn_mine, over_core(attn_other), bias_mine], 0)
        far_block = over_head(block, 2)
        attn_near = gather_pieces(block)
    else:
        (attn_near, attn_far), (mlp_near, mlp_far) = whole_pieces(master, core)
        far_block = jnp.concatenate([attn_far[0], over_head(bias_mine, 2)], 0)
    act, dm_own, x_mine, g_mine = kept_rows(info, small, tokens, cotangent, far_small, far_tokens, number)
    dm_other = over_core(dm_own)
    if strips:
        mlp_far = over_head(relay(mlp_block, (far_block,)), 2)
    far_block, bias_far = pass_on(far_block, attn_near[1:])
    if strips:
        attn_far = gather_pieces(far_block)
    near = attend(info, act, bias_mine, attn_near, number)
    far = attend(info, act, bias_far, attn_far, number)
    if strips:
        mlp_far = lax.all_gather(relay(mlp_far), "sup")
    terms = sum_rows(project(info, near[0], far[0], near[3], far[3]))
    w_near = mlp_weights(info, mlp_near)
    hidden, attn, act_mine = middle(info, modulation, bias_out, x_mine, terms, number)
    act_far = over_head(act_mine, 1)
    w_far = mlp_weights(info, mlp_far)
    act_far = relay(act_far)
    pieces = (act_mine, act_far, over_core(act_mine), over_core(act_far))
    act_two, f, du, *db_parts = mlp(info, (bias_mine, bias_far), dm_own, dm_other, w_near, w_far, pieces, number)
    db_terms = sum_rows(db_parts)
    mlp_parts = down_rows(info, f, w_near[1], w_far[1])
    dh, dat_mine, back_sums = back_middle(info, modulation, hidden, attn, g_mine, db_terms, number)
    dat_far = over_head(dat_mine, 1)
    mlp_terms = sum_rows(mlp_parts)
    *mlp_blocks, vectors = mlp_grads(info, act_two, du, f, dm_own, dm_other, strips)
    if strips:
        gots = [over_sup(mlp_blocks[0], 1), over_sup(mlp_blocks[1], 2)]
    dat_far = relay(dat_far)
    output_mine, gate_sums = output_rows(info, modulation, bias_out, hidden, g_mine, mlp_terms, number)
    output_all = lax.all_gather(output_mine, HEAD_AXES, axis=0, tiled=True)
    dat_pieces = (dat_mine, dat_far, over_core(dat_mine), over_core(dat_far))
    dat, near_grad, far_grad, *da_parts = attend_back(info, near, far, dat_pieces, number)
    da_terms = sum_rows(da_parts, spare=0)
    if strips:
        near_mine, far_mine, near_send, far_send = half_way(mlp_blocks[2:], gots, (da_terms[1],))
        gots = [over_sup(near_send, 2), over_sup(far_send, 1)]
    attn_blocks = attn_grads(info, act, dat, (near_grad, far_grad), near[3], far[3], vectors, strips)
    last, extra = last_rows(info, modulation, x_mine, dh, da_terms, back_sums, gate_sums, number)
    half = x_mine.shape[0]

    states = (left_stat, right_stat, left_root, right_root, master)
    biases = (bias_in, bias_in_sq, bias_out, bias_out_sq)
    if strips:
        mlp_near_sum, mlp_far_sum = mlp_join((near_mine, far_mine), gots)
        mlp_far_got = over_head(mlp_far_sum, 2)
        (output,) = expand_all(info, counts, output_all, images, slots)
        attn_gots = [over_sup(attn_blocks[0], 1), over_sup(attn_blocks[1], 2)]
        mine_p, mine_q, send_p, send_q = attn_half(attn_blocks[2:], attn_gots)
        attn_gots = [over_sup(send_p, 2), over_sup(send_q, 1)]
        near_sum, far_sum, sums = join((mine_p, mine_q), attn_gots)
        far_got = over_head(far_sum, 2)
        last_pieces = gather_last(last)
        mlp_keep, mlp_send = mlp_strip(info, mlp_near_sum, mlp_far_got)
        mlp_got = over_core(mlp_send)
        previous = shampoo(info, mlp_keep, mlp_got, states, None, True)
        keep, send, total = attn_strip(info, near_sum, sums, far_got)
        got = over_core(send)
        grad_tokens, grad_modulation = expand(info, counts, half + extra, last_pieces, images, slots, extra)
        weights = shampoo(info, keep, got, states, previous, False)
        steps = bias_step(info, total, got, *biases)
        tail = list(weights) + list(steps)
    else:
        last_pieces = gather_last(last)
        grad_tokens, grad_modulation = expand(info, counts, half + extra, last_pieces, images, slots, extra)
        (output,) = expand_all(info, counts, output_all, images, slots)
        tail = finish_whole(attn_blocks, mlp_blocks, states, biases, core, head)
    return (output, grad_tokens, grad_modulation, *tail)


def solution(mesh):
    devices = mesh.devices
    inner = Mesh(
        devices.reshape(devices.shape[0] // 2, 2, 2, devices.shape[1] // 2), ("sup", "core", *HEAD_AXES)
    )
    seq = ("sup", "core")
    tile = P(("sup", "core", *HEAD_AXES), None, None)
    rows = P(seq, None, None)
    return jax.shard_map(
        on_device,
        mesh=inner,
        in_specs=(rows, rows, rows, P(seq, None), tile, tile, tile, tile, tile)
        + (P(HEAD_AXES, None), P(HEAD_AXES, None), P(), P()),
        out_specs=(rows, rows, P(seq, None, HEAD_AXES), tile, tile, tile, tile)
        + (P(HEAD_AXES, None),) * 3
        + (P(),) * 3,
        check_vma=False,
    )
```

```python
import functools

import jax
import jax.numpy as jnp
from jax import lax
from jax.experimental import pallas as pl
from jax.experimental.pallas import tpu as pltpu
from jax.sharding import Mesh, PartitionSpec as P

HEADS = 16
HEAD_DIM = 72
KEPT = 128
SIDE = 144
RANGES = 8
SLOTS = 24
WIDTH = 1152
QKV = 432
PAIRED = 144
UP = 576

norm_epsilon = 1e-06
decay_rate = 0.5
weight_rate = 0.3
bias_rate = 0.1
root_epsilon = 1e-08
score_scale = HEAD_DIM ** (-0.5)
bf16 = jnp.bfloat16
f32 = jnp.float32
CORE_SWAP = [(0, 1), (1, 0)]
HEAD_AXES = ("hp", "hq")

SUP, ORDER, CORE, HEAD, HALF, FIRST, GROUP = range(7)
ANY = pl.BlockSpec(memory_space=pl.ANY)
VMEM = pl.BlockSpec(memory_space=pltpu.VMEM)
SMEM = pl.BlockSpec(memory_space=pltpu.SMEM)


def dot(a, b):
    return lax.dot_general(a, b, (((1,), (0,)), ((), ())), preferred_element_type=f32)


def dot_t(a, b):
    return lax.dot_general(a, b, (((1,), (1,)), ((), ())), preferred_element_type=f32)


def t_dot(a, b):
    return lax.dot_general(a, b, (((0,), (0,)), ((), ())), preferred_element_type=f32)


def normalize(values):
    center = jnp.mean(values, -1, keepdims=True)
    centered = values - center
    inverse = lax.rsqrt(jnp.mean(centered * centered, -1, keepdims=True) + norm_epsilon)
    return (centered * inverse, inverse)


def norm_back(grad_in, normed, inverse):
    inner = jnp.mean(grad_in * normed, -1, keepdims=True)
    return inverse * (grad_in - jnp.mean(grad_in, -1, keepdims=True) - normed * inner)


def over_both(values):
    pairs = [(i, i ^ 5) for i in range(8)]
    return lax.ppermute(values, ("core", "hp", "hq"), pairs)


def over_core(values):
    return lax.ppermute(values, "core", CORE_SWAP)


def over_head(values, offset):
    return lax.ppermute(values, HEAD_AXES, [(i, i ^ offset) for i in range(4)])


def over_sup(values, offset):
    return lax.ppermute(values, "sup", [(i, i ^ offset) for i in range(4)])


def shaped(shape, dtype):
    return jax.ShapeDtypeStruct(shape, dtype)


LAST = [None]
VMEM_MIB = dict(mlp=32, mlp_grads=28, attend_back=26, down=20, kept_rows=20, attn_grads=24)
TIMES = dict(last_rows=10, relay_dat=3, relay_last=5, expand_rows=3, back_middle=10)
COST = 0.02


def call(body, name, inputs, outputs, scratch=(), flops=0, aliases=None, after=(), cost=0, grid=()):
    inputs = list(inputs)
    count = len(inputs)
    if LAST[0] is not None and all(LAST[0] is not array for array, _ in inputs):
        inputs.append((LAST[0], ANY))
    inputs += [(a, ANY) for a in after]
    arrays = [array for array, _ in inputs]
    shapes = [shaped(shape, dtype) for shape, dtype, _ in outputs]

    size = sum(a.size * a.dtype.itemsize for a in arrays[:count] + shapes)

    def ordered(*refs):
        return body(*refs[:count], *refs[len(arrays) :])

    results = pl.pallas_call(
        ordered,
        name=name,
        grid=grid,
        out_shape=shapes,
        in_specs=[spec for _, spec in inputs],
        out_specs=[spec for _, _, spec in outputs],
        scratch_shapes=list(scratch),
        input_output_aliases=aliases or {},
        cost_estimate=pl.CostEstimate(flops=int(1.0e9 * TIMES.get(name, 0.02)), bytes_accessed=0, transcendentals=0),
        compiler_params=pltpu.CompilerParams(vmem_limit_bytes=VMEM_MIB.get(name, 16) * 1024 * 1024),
    )(*arrays)
    LAST[0] = min(results, key=lambda a: a.size * a.dtype.itemsize)
    return results


def chunks_of(rows, size):
    return [slice(at, min(at + size, rows)) for at in range(0, rows, size)]


def started(copies):
    for copy in copies:
        copy.start()
    return copies


def finish(copies):
    for copy in copies:
        copy.wait()


def pack_body(info, master, bias, mine, rows, mlp_mine, other, held, sems):
    copies = started(
        [pltpu.make_async_copy(master.at[pl.ds(8 * k, 8)], held.at[pl.ds(8 * k, 8)], sems.at[k]) for k in range(3)]
    )
    core = info[CORE]
    heads = [jnp.where(core == 0, bias[j : j + 1, :], bias[j + 2 : j + 3, :]) for j in range(2)]
    both = lambda a, b: jnp.concatenate([heads[0][:, a:b], heads[1][:, a:b]], 1)
    blank = jnp.zeros((1, PAIRED), f32)
    first = jnp.concatenate([both(0, HEAD_DIM), blank, both(HEAD_DIM, 2 * HEAD_DIM), blank], 1)
    rows[...] = stacked(three_rows(first) + three_rows(both(2 * HEAD_DIM, QKV)), 16).astype(bf16)
    copies[0].wait()
    attn = lambda half: jnp.concatenate([held[2 * k + half].astype(bf16) for k in range(4)], 1)
    mine[...] = attn(core)
    part = attn(1 - core)
    other[SIDE:, :] = jnp.concatenate([part[: SIDE // 2], part[SIDE // 2 :]], 1)
    finish(copies[1:])
    mlp = lambda half: jnp.concatenate(
        [held[8 + 8 * w + 4 * half + k].astype(bf16) for w in range(2) for k in range(4)], 1
    )
    mlp_mine[...] = mlp(core)
    other[:SIDE, :] = mlp(1 - core)


def pack(info, master, bias_in):
    return call(
        pack_body,
        "pack",
        [(info, SMEM), (master, ANY), (bias_in, VMEM)],
        [
            ((SIDE, 4 * SIDE), bf16, VMEM),
            ((16, 4 * SIDE), bf16, VMEM),
            ((SIDE, 8 * SIDE), bf16, VMEM),
            ((3 * SIDE // 2, 8 * SIDE), bf16, VMEM),
        ],
        [pltpu.VMEM((24, SIDE, SIDE), f32), pltpu.SemaphoreType.DMA((3,))],
    )


def blocks_body(mine, rows, mlp_mine, got, block, mlp_block):
    block[:SIDE, :] = mine[...]
    part = got[SIDE:, :]
    block[SIDE : 2 * SIDE, :] = jnp.concatenate([part[:, : 4 * SIDE], part[:, 4 * SIDE :]], 0)
    block[2 * SIDE :, :] = rows[...]
    mlp_block[:SIDE, :] = mlp_mine[...]
    mlp_block[SIDE:, :] = got[:SIDE, :]


def blocks_of(mine, rows, mlp_mine, got):
    return call(
        blocks_body,
        "blocks",
        [(a, VMEM) for a in (mine, rows, mlp_mine, got)],
        [((2 * SIDE + 16, 4 * SIDE), bf16, VMEM), ((2 * SIDE, 8 * SIDE), bf16, VMEM)],
    )


def piece_copies(info, pieces, target, sems, sup=None):
    copies = []
    sup = info[SUP] if sup is None else sup
    for k in range(4):
        for j in range(2):
            row = ((sup ^ k) * 2 + (info[ORDER] ^ j)) * SIDE
            copies.append(
                pltpu.make_async_copy(
                    pieces[k].at[pl.ds(j * SIDE, SIDE)],
                    target.at[pl.ds(pl.multiple_of(row, 16), SIDE)],
                    sems.at[2 * k + j],
                )
            )
    return copies


def gather_pieces(block):
    return [block] + [over_sup(block, k) for k in (1, 2, 3)]


def whole_pieces(master, core):
    tiles = lax.all_gather(master.astype(bf16), ("sup", "core"), axis=0, tiled=True)
    slab = tiles.reshape(8, 24, SIDE, SIDE).transpose(1, 0, 2, 3).reshape(24, 8 * SIDE, SIDE)
    take = lambda k: lax.dynamic_index_in_dim(slab, k, 0, False)
    attn = jnp.concatenate([take(2 * k + core) for k in range(4)], 1)
    mlp = jnp.concatenate([take(8 + 8 * w + 4 * core + k) for w in range(2) for k in range(4)], 1)
    out = []
    far = over_head(attn, 2)
    pieces = [[part[288 * k : 288 * k + 288] for k in range(4)] for part in (attn, far)]
    return pieces, [p.reshape(4, 288, 2 * UP) for p in (mlp, over_head(mlp, 2))]


def later_body(mine, got, out):
    out[: mine.shape[0], :] = mine[...]
    out[mine.shape[0] :, :] = got[...]


def copies_body(mine, *rest):
    out = rest[-1]
    for k in range(out.shape[0]):
        out[k, : mine.shape[0], :] = mine[...]
        if len(rest) > 1:
            out[k, mine.shape[0] :, :] = rest[0][...]


def copies_of(parts, count):
    rows = sum(p.shape[0] for p in parts)
    return call(
        copies_body, "copies", [(p, VMEM) for p in parts], [((count, rows, parts[0].shape[1]), bf16, VMEM)]
    )[0]


def to_all(values, axis):
    return lax.all_to_all(values, axis, 0, 0)


def later_block(mine, got, after=()):
    rows = mine.shape[0] + got.shape[0]
    return call(
        later_body, "later_block", [(mine, VMEM), (got, VMEM)], [((rows, mine.shape[1]), bf16, VMEM)], after=after
    )[0]


def small_body(info, counts, modulation, tokens, out, part, sem):
    images = out.shape[0]
    copies = started([pltpu.make_async_copy(tokens.at[pl.ds(info[FIRST], part.shape[0])], part, sem)])
    out[:, :6, :] = modulation[...]
    place = lax.broadcasted_iota(jnp.int32, (2, WIDTH), 1)
    for i in range(images):
        row = jnp.zeros((2, WIDTH), f32)
        for s in range(RANGES):
            row = jnp.where(place == s, counts[i, s].astype(f32), row)
        out[i, 6:8, :] = row
    finish(copies)


def small_rows(info, counts, modulation, tokens):
    shape = (modulation.shape[0], 8, WIDTH)
    part = (tokens.shape[0] // 2, *tokens.shape[1:])
    return call(
        small_body,
        "small_rows",
        [(info, SMEM), (counts, SMEM), (modulation, VMEM), (tokens, ANY)],
        [(shape, f32, VMEM), (part, bf16, VMEM)],
        [pltpu.SemaphoreType.DMA],
    )


def kept_target_of(row, slot):
    target = jnp.full(slot.shape, -1.0, f32)
    start = jnp.zeros((1, 1), f32)
    for s in range(RANGES):
        number = row[:, s : s + 1]
        place = slot - s * SLOTS
        target = jnp.where((place >= 0) & (place < number), place + start, target)
        start = start + number
    return target


def rows_body(number, info, small, tokens, cotangent, far_small, far_tokens, act, dm, x_mine, g_mine, tok, cot, x_own, g_own, sems):
    first = info[FIRST]
    copies = started(
        [
            pltpu.make_async_copy(tokens.at[pl.ds(first, number)], tok.at[pl.ds(0, number)], sems.at[0]),
            pltpu.make_async_copy(far_tokens, tok.at[pl.ds(number, number)], sems.at[1]),
            pltpu.make_async_copy(cotangent.at[pl.ds(first, number)], cot, sems.at[2]),
        ]
    )
    finish(copies)
    slots = tok.shape[1]
    slot = lax.broadcasted_iota(jnp.int32, (1, slots), 1).astype(f32)
    place = lax.broadcasted_iota(jnp.int32, (KEPT, slots), 0).astype(f32)
    for i in range(2 * number):
        mod = (small if i < number else far_small)[first + i % number]
        select = (kept_target_of(mod[6:7], slot) == place).astype(f32).astype(bf16)
        rows = slice(i * KEPT, (i + 1) * KEPT)
        x = dot(select, tok[i])
        normed, _ = normalize(x)
        act[rows, :] = (normed * (1.0 + mod[1:2]) + mod[0:1]).astype(bf16)
        if i < number:
            x_own[rows, :] = x.astype(bf16)
            g = dot(select, cot[i])
            g_own[rows, :] = g.astype(bf16)
            dm[rows, :] = (mod[5:6] * g).astype(bf16)
    half = x_mine.shape[0]
    mine = pl.ds(pl.multiple_of(info[HALF] * half, 64), half)
    x_mine[...] = x_own[mine, :]
    g_mine[...] = g_own[mine, :]


def kept_rows(info, small, tokens, cotangent, far_small, far_tokens, number):
    slots = tokens.shape[1]
    rows = number * KEPT
    half = rows // 2
    return call(
        functools.partial(rows_body, number),
        "kept_rows",
        [(info, SMEM), (small, VMEM), (tokens, ANY), (cotangent, ANY), (far_small, VMEM), (far_tokens, ANY)],
        [((2 * rows, WIDTH), bf16, VMEM), ((rows, WIDTH), bf16, VMEM)] + [((half, WIDTH), bf16, VMEM)] * 2,
        [pltpu.VMEM((2 * number, slots, WIDTH), bf16), pltpu.VMEM((number, slots, WIDTH), bf16)]
        + [pltpu.VMEM((rows, WIDTH), bf16)] * 2
        + [pltpu.SemaphoreType.DMA((3,))],
        flops=6 * rows * slots * WIDTH,
    )


def spread_of(counts, image):
    parts = []
    start = 0
    slot = lax.broadcasted_iota(jnp.int32, (SLOTS, KEPT), 0)
    row = lax.broadcasted_iota(jnp.int32, (SLOTS, KEPT), 1)
    for s in range(RANGES):
        number = counts[image, s]
        parts.append(((row == slot + start) & (slot < number)).astype(f32))
        start = start + number
    return jnp.concatenate(parts, 0).astype(bf16)


def expand_body(images, extra, size, places, info, counts, *rest):
    pieces, (out, sums, held, sems) = rest[: len(places)], rest[len(places) :]
    half = size - extra
    copies = []
    for n, (k, at) in enumerate(places):
        row = pl.multiple_of((info[HEAD] ^ k) * size + at, 16)
        copies.append(pltpu.make_async_copy(pieces[n], held.at[pl.ds(row, pieces[n].shape[0])], sems.at[n]))
    finish(started(copies))
    parts = half // 64
    for i in range(images):
        spread = spread_of(counts, i)
        chunks = []
        for chunk in (2 * i, 2 * i + 1):
            row = (chunk // parts) * size + (chunk % parts) * 64
            chunks.append(held[row : row + 64, :])
        out[i] = dot(spread, jnp.concatenate(chunks, 0)).astype(bf16)
        if True:
            total = jnp.zeros((6, WIDTH), f32)
            for chunk in (2 * i, 2 * i + 1):
                base = (chunk // parts) * size + half
                block = held[base : base + extra, :].astype(f32)
                at = (chunk % parts) * 6
                total = total + block[at : at + 6]
            quarter = WIDTH // 4
            picked = total[:, :quarter]
            for k in range(1, 4):
                picked = jnp.where(info[HEAD] == k, total[:, k * quarter : (k + 1) * quarter], picked)
            sums[i] = picked


def expand(info, counts, size, pieces, images, slots, extra):
    return call(
        functools.partial(expand_body, images, extra, size, [(k, at) for _, k, at in pieces]),
        "expand_rows",
        [(info, SMEM), (counts, SMEM)] + [(p, ANY) for p, _, _ in pieces],
        [((images, slots, WIDTH), bf16, VMEM), ((images, 6, WIDTH // 4), f32, VMEM)],
        [pltpu.VMEM((4 * size, WIDTH), bf16), pltpu.SemaphoreType.DMA((len(pieces),))],
        flops=2 * images * slots * KEPT * WIDTH,
    )


def expand_all_body(images, info, counts, rows, out):
    for i in range(images):
        spread = spread_of(counts, i)
        out[i] = dot(spread, rows[i * KEPT : (i + 1) * KEPT, :]).astype(bf16)


def expand_all(info, counts, rows, images, slots):
    return call(
        functools.partial(expand_all_body, images),
        "expand_output",
        [(info, SMEM), (counts, SMEM), (rows, VMEM)],
        [((images, slots, WIDTH), bf16, VMEM)],
        flops=2 * images * slots * KEPT * WIDTH,
    )


def both_copies(own, other, target, sems):
    rows = target.shape[0] // 2
    return [
        pltpu.make_async_copy(ref, target.at[pl.ds(k * rows, rows)], sems.at[k]) for k, ref in enumerate((own, other))
    ]


def first_sum_body(mine, got, send):
    send[: mine.shape[0], :] = (mine[...].astype(f32) + got[...].astype(f32)).astype(send.dtype)
    if send.shape[0] > mine.shape[0]:
        send[mine.shape[0] :, :] = jnp.zeros((send.shape[0] - mine.shape[0], send.shape[1]), send.dtype)


def sum_rows(parts, kind=bf16, spare=0):
    own_send, own_keep, other_send, other_keep = parts
    got, got_keep = over_core(other_send), over_core(other_keep)
    rows, width = own_send.shape
    (send,) = call(first_sum_body, "first_sum", [(own_send, VMEM), (got, VMEM)], [((rows + spare, width), kind, VMEM)])
    return own_keep, got_keep, over_head(send, 1)


def relay_body(got, out):
    out[...] = got[...]


def relay_two_body(got, held, first, second, later):
    later[...] = held[...]
    first[...] = got[: first.shape[0], :]
    second[...] = got[first.shape[0] :, :]


def relay_two(got, held):
    part = got.shape[0] // 32 * 16
    shapes = [(part, got.shape[1]), (got.shape[0] - part, got.shape[1])]
    shapes.append(held.shape)
    return call(
        relay_two_body, "relay_last", [(got, VMEM), (held, VMEM)], [(shape, bf16, VMEM) for shape in shapes]
    )


def relay(got, after=(), name="relay"):
    return call(relay_body, name, [(got, VMEM)], [(got.shape, got.dtype, VMEM)], after=after)[0]


def all_terms(terms, rows):
    total = terms[0][rows, :].astype(f32)
    for term in terms[1:]:
        total = total + term[rows, :].astype(f32)
    return total


def share_copies(info, pieces, target, sems):
    half = pieces[0].shape[0]
    copies = []
    for k in range(4):
        row = (k // 2) * 2 * half + (info[HALF] ^ (k % 2)) * half
        copies.append(
            pltpu.make_async_copy(pieces[k], target.at[pl.ds(pl.multiple_of(row, 64), half)], sems.at[k])
        )
    return copies


def split_halves(info, full, outs):
    half = outs[0].shape[0]
    for k in range(4):
        place = info[HALF] if k % 2 else 1 - info[HALF]
        outs[k][...] = full[pl.ds(pl.multiple_of((2 * (k // 2) + place) * half, 64), half), :].astype(bf16)


def head_mask():
    return lax.broadcasted_iota(jnp.int32, (KEPT, PAIRED), 1) < HEAD_DIM


def split_heads(values, mask):
    zero = jnp.zeros_like(values)
    return jnp.concatenate([jnp.where(mask, values, zero), jnp.where(mask, zero, values)], 0)


def sum_of_rows(ref, first):
    rows = ref[...].astype(f32)
    return rows[first : first + 1] + rows[first + 1 : first + 2] + rows[first + 2 : first + 3]


def attend_body(number, info, act, bias, w0, w1, w2, w3, weights, qkv, probs, mixed, sems):
    finish(started(piece_copies(info, (w0, w1, w2, w3), weights, sems)))
    mask = head_mask()
    bias = sum_of_rows(bias, 0)[:, :QKV]
    for rows in chunks_of(act.shape[0], 384):
        qkv[rows, :] = (dot(act[rows, :], weights[:, :QKV]) + bias).astype(bf16)
    for i in range(2 * number):
        rows = slice(i * KEPT, (i + 1) * KEPT)
        here = qkv[rows, :]
        q, k, v = (here[:, j * PAIRED : (j + 1) * PAIRED] for j in range(3))
        scores = dot_t(split_heads(q, mask), k) * score_scale
        raised = jnp.exp(scores - jnp.max(scores, -1, keepdims=True))
        p = raised / jnp.sum(raised, -1, keepdims=True)
        low = p.astype(bf16)
        probs[i] = low
        wide = jnp.concatenate([low[:KEPT], low[KEPT:]], 1)
        mixed[rows, :] = dot(wide, split_heads(v, mask)).astype(bf16)


def attend(info, act, bias, pieces, number):
    rows = 2 * number * KEPT
    return call(
        functools.partial(attend_body, number),
        "attend",
        [(info, SMEM), (act, VMEM), (bias, VMEM)] + [(p, ANY) for p in pieces],
        [
            ((WIDTH, QKV + PAIRED), bf16, VMEM),
            ((rows, QKV), bf16, VMEM),
            ((2 * number, 2 * KEPT, KEPT), bf16, VMEM),
            ((rows, PAIRED), bf16, VMEM),
        ],
        [pltpu.SemaphoreType.DMA((8,))],
        flops=2 * rows * WIDTH * QKV,
    )


def project_body(info, near_w, far_w, near, far, *rest):
    outs, full = rest[:4], rest[4]
    wa = near_w[:, QKV:]
    wb = far_w[:, QKV:]
    for rows in chunks_of(near.shape[0], 384):
        full[rows, :] = (dot_t(near[rows, :], wa) + dot_t(far[rows, :], wb)).astype(bf16)
    split_halves(info, full, outs)


def halves_of(rows):
    return [((rows // 4, WIDTH), bf16, VMEM)] * 4


def project(info, near_w, far_w, near, far):
    rows = near.shape[0]
    return call(
        project_body,
        "project",
        [(info, SMEM), (near_w, VMEM), (far_w, VMEM), (near, VMEM), (far, VMEM)],
        halves_of(rows),
        [pltpu.VMEM((rows, WIDTH), bf16)],
        flops=4 * rows * WIDTH * PAIRED,
    )


def middle_body(number, info, modulation, bias_out, x_mine, *rest):
    terms, (hidden, attn, act) = rest[:-3], rest[-3:]
    half = x_mine.shape[0]
    parts = half // 64
    for t in range(parts):
        rows = slice(t * 64, (t + 1) * 64)
        mod = modulation[info[FIRST] + (info[HALF] * parts + t) // 2]
        a = all_terms(terms, rows) + bias_out[0:1, :]
        h = x_mine[rows, :].astype(f32) + mod[2:3] * a
        attn[rows, :] = a
        hidden[rows, :] = h
        normed, _ = normalize(h)
        act[rows, :] = (normed * (1.0 + mod[4:5]) + mod[3:4]).astype(bf16)


def middle(info, modulation, bias_out, x_mine, terms, number):
    half = x_mine.shape[0]
    return call(
        functools.partial(middle_body, number),
        "middle",
        [(info, SMEM), (modulation, VMEM), (bias_out, VMEM), (x_mine, VMEM)] + [(t, VMEM) for t in terms],
        [((half, WIDTH), f32, VMEM)] * 2 + [((half, WIDTH), bf16, VMEM)],
    )


def mlp_weights_body(relative, info, *refs):
    pieces, (up, down, held, sems) = refs[:4], refs[4:]
    finish(started(piece_copies(info, pieces, held, sems, None if relative else 0)))
    for i in range(8):
        rows = slice(i * SIDE, (i + 1) * SIDE)
        up[rows, :] = held[rows, :UP]
        down[rows, :] = held[rows, UP:]


def whole_body(info, whole, *refs):
    mlp_weights_body(False, info, *[whole.at[k] for k in range(4)], *refs)


def mlp_weights(info, pieces):
    relative = isinstance(pieces, list)
    arrays = pieces if relative else [pieces]
    return call(
        functools.partial(mlp_weights_body, True) if relative else whole_body,
        "mlp_weights",
        [(info, SMEM)] + [(p, ANY) for p in arrays],
        [((WIDTH, UP), bf16, VMEM)] * 2,
        [pltpu.VMEM((WIDTH, 2 * UP), bf16), pltpu.SemaphoreType.DMA((8,))],
    )


def smooth_both(u):
    c = 0.7978845608028654
    cube = 0.044715
    square = u * u
    t = jnp.tanh(c * u * (1.0 + cube * square))
    half_up = 0.5 * (1.0 + t)
    slope = half_up + 0.5 * u * (1.0 - t * t) * (c * (1.0 + 3.0 * cube * square))
    return u * half_up, slope


def mlp_body(number, info, near_bias, far_bias, own, other, near_up, near_down, far_up, far_down, s0, s1, s2, s3, *rest):
    act, f, du, g0, g1, g2, g3, db, dm, dm_sems, sems = rest
    copies = started(both_copies(own, other, dm, dm_sems))
    finish(copies + started(share_copies(info, (s0, s1, s2, s3), act, sems)))
    biases = [sum_of_rows(ref, 3) for ref in (near_bias, far_bias)]
    for rows in chunks_of(act.shape[0], 384):
        values, lows = [], []
        total = 0.0
        for g, (up, down) in enumerate(((near_up, near_down), (far_up, far_down))):
            u = dot(act[rows, :], up[...]) + biases[g]
            value, slope = smooth_both(u)
            low = (dot(dm[rows, :], down[...]) * slope).astype(bf16)
            total = total + dot_t(low, up[...])
            values.append(value.astype(bf16))
            lows.append(low)
        f[rows, :] = jnp.concatenate(values, 1)
        du[rows, :] = jnp.concatenate(lows, 1)
        db[rows, :] = total.astype(bf16)
    split_halves(info, db, (g0, g1, g2, g3))


def mlp(info, biases, own, other, near, far, pieces, number):
    rows = 2 * number * KEPT
    full = ((rows, WIDTH), bf16, VMEM)
    return call(
        functools.partial(mlp_body, number),
        "mlp",
        [(info, SMEM), (biases[0], VMEM), (biases[1], VMEM), (own, ANY), (other, ANY)]
        + [(a, VMEM) for a in (*near, *far)]
        + [(p, ANY) for p in pieces],
        [full] * 3 + halves_of(rows),
        [pltpu.VMEM((rows, WIDTH), bf16)] * 2 + [pltpu.SemaphoreType.DMA((2,)), pltpu.SemaphoreType.DMA((4,))],
        flops=6 * rows * WIDTH * WIDTH,
    )


def down_body(info, f, near_w, far_w, *rest):
    outs, full = rest[:4], rest[4]
    for rows in chunks_of(f.shape[0], 384):
        full[rows, :] = (dot_t(f[rows, :UP], near_w[...]) + dot_t(f[rows, UP:], far_w[...])).astype(bf16)
    split_halves(info, full, outs)


def down_rows(info, f, near_w, far_w):
    rows = f.shape[0]
    return call(
        down_body,
        "down",
        [(info, SMEM), (f, VMEM), (near_w, VMEM), (far_w, VMEM)],
        halves_of(rows),
        [pltpu.VMEM((rows, WIDTH), bf16)],
        flops=2 * rows * WIDTH * WIDTH,
    )


def two_rows(values):
    high = values.astype(bf16)
    return [high.astype(f32), values - high.astype(f32)]


def three_rows(values):
    high, rest = two_rows(values)
    return [high] + two_rows(rest)


def stacked(rows, count):
    width = rows[0].shape[1]
    place = lax.broadcasted_iota(jnp.int32, (count, width), 0)
    out = jnp.zeros((count, width), f32)
    for k, row in enumerate(rows):
        out = jnp.where(place == k, row, out)
    return out


def block_copies(strips, info, full, extra, outs, sems):
    copies = []

    def add(source, target):
        copies.append(pltpu.make_async_copy(source, target, sems.at[len(copies)]))

    if strips:
        moves = ((0, 0, (1, 3)), (1, 1, (2, 3)), (2, 0, (0, 2)), (3, 1, (0, 1)))
        for out, part, places in moves:
            for j, k in enumerate(places):
                row = pl.multiple_of((info[SUP] ^ k) * 288 + part * SIDE, 16)
                add(full.at[pl.ds(row, SIDE)], outs[out].at[j, pl.ds(0, SIDE)])
                if part:
                    add(extra, outs[out].at[j, pl.ds(SIDE, 16)])
    else:
        for k in range(4):
            add(full.at[pl.ds(k * 288, 288)], outs[k].at[pl.ds(0, 288)])
            add(extra, outs[k].at[pl.ds(288, 16)])
    return copies


def column_sums(ref):
    half = ref.shape[0] // 2
    first = jnp.sum(ref[:half, :].astype(f32), 0, keepdims=True)
    return first + jnp.sum(ref[half:, :].astype(f32), 0, keepdims=True)


def mlp_grads_body(strips, info, act, du, f, own, other, o0, o1, o2, o3, vectors, dm, full, dm_sems, sems):
    finish(started(both_copies(own, other, dm, dm_sems)))
    for part in (slice(0, 512), slice(512, WIDTH)):
        up = t_dot(act[:, part], du[...]).astype(bf16)
        down = t_dot(dm[:, part], f[...]).astype(bf16)
        for g in range(2):
            columns = slice(g * UP, (g + 1) * UP)
            full[g, part, :] = jnp.concatenate([up[:, columns], down[:, columns]], 1)
    if strips:
        moves = ((0, o0, (1, 3)), (1, o1, (2, 3)), (0, o2, (0, 2)), (1, o3, (0, 1)))
    else:
        moves = [(g, o, (2 * h, 2 * h + 1)) for g, h, o in ((0, 0, o0), (0, 1, o1), (1, 0, o2), (1, 1, o3))]
    copies = []
    for g, out, places in moves:
        for j, k in enumerate(places):
            row = pl.multiple_of((info[SUP] ^ k) * 288, 16)
            copies.append(pltpu.make_async_copy(full.at[g, pl.ds(row, 288)], out.at[j], sems.at[len(copies)]))
    started(copies)
    vectors[...] = stacked([column_sums(du), column_sums(dm)], 8)
    finish(copies)


def mlp_grads(info, act, du, f, own, other, strips):
    rows = act.shape[0]
    return call(
        functools.partial(mlp_grads_body, strips),
        "mlp_grads",
        [(info, SMEM), (act, VMEM), (du, VMEM), (f, VMEM), (own, ANY), (other, ANY)],
        [((2, 288, WIDTH), bf16, ANY)] * 4 + [((8, WIDTH), f32, VMEM)],
        [pltpu.VMEM((rows, WIDTH), bf16), pltpu.VMEM((2, WIDTH, WIDTH), bf16)]
        + [pltpu.SemaphoreType.DMA((2,)), pltpu.SemaphoreType.DMA((8,))],
        flops=4 * rows * WIDTH * WIDTH,
    )


def half_way_body(near_keep, near_got, far_keep, far_got, near, far, near_send, far_send):
    for keep, got, mine, send in ((near_keep, near_got, near, near_send), (far_keep, far_got, far, far_send)):
        mine[...] = keep[0].astype(f32) + got[0].astype(f32)
        send[...] = (keep[1].astype(f32) + got[1].astype(f32)).astype(bf16)


def half_way(keeps, gots, after):
    return call(
        half_way_body,
        "half_way",
        [(a, VMEM) for a in (keeps[0], gots[0], keeps[1], gots[1])],
        [((288, WIDTH), f32, VMEM)] * 2 + [((288, WIDTH), bf16, VMEM)] * 2,
        after=after,
    )


def mlp_join_body(near_mine, near_got, far_mine, far_got, near, far):
    near[...] = near_mine[...] + near_got[...].astype(f32)
    far[...] = (far_mine[...] + far_got[...].astype(f32)).astype(bf16)


def mlp_join(mines, gots):
    return call(
        mlp_join_body,
        "mlp_join",
        [(a, VMEM) for a in (mines[0], gots[0], mines[1], gots[1])],
        [((288, WIDTH), f32, VMEM), ((288, WIDTH), bf16, VMEM)],
    )


def output_body(number, info, modulation, bias_out, hidden, g_mine, *rest):
    terms, (out, sums) = rest[:-2], rest[-2:]
    half = hidden.shape[0]
    parts = half // 64
    for t in range(parts):
        rows = slice(t * 64, (t + 1) * 64)
        mod = modulation[info[FIRST] + (info[HALF] * parts + t) // 2]
        m = all_terms(terms, rows) + bias_out[1:2, :]
        value = (hidden[rows, :] + mod[5:6] * m).astype(bf16)
        out[rows, :] = value
        sums[t : t + 1, :] = jnp.sum(g_mine[rows, :].astype(f32) * m, 0, keepdims=True)


def output_rows(info, modulation, bias_out, hidden, g_mine, terms, number):
    half = hidden.shape[0]
    return call(
        functools.partial(output_body, number),
        "output_rows",
        [(info, SMEM), (modulation, VMEM), (bias_out, VMEM), (hidden, VMEM), (g_mine, VMEM)]
        + [(t, VMEM) for t in terms],
        [((half, WIDTH), bf16, VMEM), ((half // 64, WIDTH), f32, VMEM)],
    )


def back_middle_body(number, info, modulation, hidden, attn, g_mine, *rest):
    terms, (dh, dat, sums) = rest[:-3], rest[-3:]
    half = hidden.shape[0]
    parts = half // 64
    for t in range(parts):
        rows = slice(t * 64, (t + 1) * 64)
        mod = modulation[info[FIRST] + (info[HALF] * parts + t) // 2]
        db = all_terms(terms, rows)
        normed, inverse = normalize(hidden[rows, :])
        grad = g_mine[rows, :].astype(f32) + norm_back(db * (1.0 + mod[4:5]), normed, inverse)
        dh[rows, :] = grad
        dat[rows, :] = (mod[2:3] * grad).astype(bf16)
        sums[3 * t : 3 * t + 1, :] = jnp.sum(grad * attn[rows, :], 0, keepdims=True)
        sums[3 * t + 1 : 3 * t + 2, :] = jnp.sum(db, 0, keepdims=True)
        sums[3 * t + 2 : 3 * t + 3, :] = jnp.sum(db * normed, 0, keepdims=True)


def back_middle(info, modulation, hidden, attn, g_mine, terms, number):
    half = hidden.shape[0]
    return call(
        functools.partial(back_middle_body, number),
        "back_middle",
        [(info, SMEM), (modulation, VMEM), (hidden, VMEM), (attn, VMEM), (g_mine, VMEM)]
        + [(t, VMEM) for t in terms],
        [((half, WIDTH), f32, VMEM), ((half, WIDTH), bf16, VMEM), ((3 * (half // 64), WIDTH), f32, VMEM)],
    )


def attend_back_body(number, info, near_w, far_w, near_qkv, far_qkv, near_p, far_p, s0, s1, s2, s3, *rest):
    dat, near_grad, far_grad, g0, g1, g2, g3, da, near_do, far_do, sems = rest
    copies = started(share_copies(info, (s0, s1, s2, s3), dat, sems))
    mask = head_mask()
    near_out, far_out = near_w[:, QKV:], far_w[:, QKV:]
    finish(copies)
    for rows in chunks_of(dat.shape[0], 384):
        near_do[rows, :] = dot(dat[rows, :], near_out).astype(bf16)
        far_do[rows, :] = dot(dat[rows, :], far_out).astype(bf16)
    for i in range(2 * number):
        rows = slice(i * KEPT, (i + 1) * KEPT)
        for do, qkv, probs, out in ((near_do, near_qkv, near_p, near_grad), (far_do, far_qkv, far_p, far_grad)):
            here = qkv[rows, :]
            q, k, v = (here[:, j * PAIRED : (j + 1) * PAIRED] for j in range(3))
            low = probs[i]
            p = low.astype(f32)
            both = split_heads(do[rows, :], mask)
            dp = dot_t(both, v)
            ds = (p * (dp - jnp.sum(p * dp, -1, keepdims=True))).astype(bf16)
            wide = jnp.concatenate([ds[:KEPT], ds[KEPT:]], 1)
            dq = dot(wide, split_heads(k, mask)) * score_scale
            dk = t_dot(ds, split_heads(q, mask)) * score_scale
            dv = t_dot(low, both)
            out[rows, :] = jnp.concatenate([dq, dk, dv], 1).astype(bf16)
    near_in, far_in = near_w[:, :QKV], far_w[:, :QKV]
    for rows in chunks_of(dat.shape[0], 384):
        da[rows, :] = (dot_t(near_grad[rows, :], near_in) + dot_t(far_grad[rows, :], far_in)).astype(bf16)
    split_halves(info, da, (g0, g1, g2, g3))


def attend_back(info, near, far, pieces, number):
    rows = 2 * number * KEPT
    return call(
        functools.partial(attend_back_body, number),
        "attend_back",
        [(info, SMEM)]
        + [(a, VMEM) for a in (near[0], far[0], near[1], far[1], near[2], far[2])]
        + [(p, ANY) for p in pieces],
        [((rows, WIDTH), bf16, VMEM)] + [((rows, QKV), bf16, VMEM)] * 2 + halves_of(rows),
        [pltpu.VMEM((rows, WIDTH), bf16)]
        + [pltpu.VMEM((rows, PAIRED), bf16)] * 2
        + [pltpu.SemaphoreType.DMA((4,))],
        flops=4 * rows * WIDTH * 576,
    )


def attn_grads_body(strips, info, act, dat, near_grad, far_grad, near_o, far_o, vectors, o0, o1, o2, o3, mixed, full, extra, sems):
    mixed[...] = jnp.concatenate([near_o[...], far_o[...]], 1)
    for part in (slice(0, 512), slice(512, WIDTH)):
        parts = [t_dot(act[:, part], grad[...]) for grad in (near_grad, far_grad)]
        parts.append(t_dot(dat[:, part], mixed[...]))
        full[part, :] = jnp.concatenate(parts, 1).astype(bf16)
    sums = jnp.concatenate(
        [column_sums(near_grad), column_sums(far_grad), jnp.zeros((1, 2 * PAIRED), f32)], 1
    )
    rows = (sums, column_sums(dat), vectors[0:1, :], vectors[1:2, :])
    extra[...] = stacked([part for row in rows for part in two_rows(row)], 16).astype(bf16)
    finish(started(block_copies(strips, info, full, extra, (o0, o1, o2, o3), sems)))


def attn_grads(info, act, dat, grads, near_o, far_o, vectors, strips):
    rows = dat.shape[0]
    return call(
        functools.partial(attn_grads_body, strips),
        "attn_grads",
        [(info, SMEM)] + [(a, VMEM) for a in (act, dat, *grads, near_o, far_o, vectors)],
        [((2, SIDE + 16 * (k % 2), WIDTH) if strips else (304, WIDTH), bf16, ANY) for k in range(4)],
        [
            pltpu.VMEM((rows, 2 * PAIRED), bf16),
            pltpu.VMEM((WIDTH, WIDTH), bf16),
            pltpu.VMEM((16, WIDTH), bf16),
            pltpu.SemaphoreType.DMA((12,)),
        ],
        flops=2 * rows * WIDTH * WIDTH,
    )


def last_rows_body(number, info, modulation, x_mine, dh, *rest):
    terms, (back_sums, gate_sums, out, sums) = rest[:-4], rest[-4:]
    half = x_mine.shape[0]
    parts = half // 64
    sums[...] = jnp.zeros_like(sums)
    for t in range(parts):
        rows = slice(t * 64, (t + 1) * 64)
        mod = modulation[info[FIRST] + (info[HALF] * parts + t) // 2]
        da = all_terms(terms, rows)
        normed, inverse = normalize(x_mine[rows, :].astype(f32))
        out[rows, :] = (dh[rows, :] + norm_back(da * (1.0 + mod[1:2]), normed, inverse)).astype(bf16)
        sums[6 * t : 6 * t + 1, :] = jnp.sum(da, 0, keepdims=True)
        sums[6 * t + 1 : 6 * t + 2, :] = jnp.sum(da * normed, 0, keepdims=True)
        sums[6 * t + 2 : 6 * t + 5, :] = back_sums[3 * t : 3 * t + 3, :]
        sums[6 * t + 5 : 6 * t + 6, :] = gate_sums[t : t + 1, :]
    out[half:, :] = sums[...].astype(bf16)


def gather_last(last, held):
    near, far = over_head(last, 1), over_head(last, 2)
    pieces = [(last, 0, 0), (near, 1, 0)]
    at = 0
    *parts, later = relay_two(far, held)
    for part in parts:
        pieces += [(part, 2, at), (over_head(part, 1), 3, at)]
        at += part.shape[0]
    return pieces, later


def last_rows(info, modulation, x_mine, dh, terms, back_sums, gate_sums, number):
    half = x_mine.shape[0]
    extra = -(-6 * (half // 64) // 16) * 16
    (out,) = call(
        functools.partial(last_rows_body, number),
        "last_rows",
        [(info, SMEM), (modulation, VMEM), (x_mine, VMEM), (dh, VMEM)]
        + [(t, VMEM) for t in terms]
        + [(back_sums, VMEM), (gate_sums, VMEM)],
        [((half + extra, WIDTH), bf16, VMEM)],
        [pltpu.VMEM((extra, WIDTH), f32)],
        cost=0,
    )
    return out, extra


def attn_half_body(keep_p, got_p, keep_q, got_q, mine_p, mine_q, send_p, send_q):
    for keep, got, mine, send in ((keep_p, got_p, mine_p, send_p), (keep_q, got_q, mine_q, send_q)):
        for j, out in ((0, mine), (1, send)):
            out[:SIDE, :] = (keep[j, :SIDE, :].astype(f32) + got[j, :SIDE, :].astype(f32)).astype(out.dtype)
            if keep.shape[1] > SIDE:
                extra = keep[j, SIDE:, :].astype(f32) + got[j, SIDE:, :].astype(f32)
                rows = [part for k in range(4) for part in two_rows(extra[2 * k : 2 * k + 1] + extra[2 * k + 1 : 2 * k + 2])]
                out[SIDE:, :] = stacked(rows, 16).astype(bf16).astype(out.dtype)


def attn_half(keeps, gots):
    shapes = [(SIDE, WIDTH), (SIDE + 16, WIDTH)]
    return call(
        attn_half_body,
        "attn_half",
        [(a, VMEM) for a in (keeps[0], gots[0], keeps[1], gots[1])],
        [(shape, kind, VMEM) for kind in (f32, bf16) for shape in shapes],
    )


def join_body(mine_p, got_p, mine_q, got_q, near, far, vectors):
    cut = 2 * QKV + PAIRED
    for at, mine, got in ((0, mine_p, got_p), (SIDE, mine_q, got_q)):
        total = mine[:SIDE, :] + got[:SIDE, :].astype(f32)
        near[at : at + SIDE, :] = jnp.concatenate([total[:, :QKV], total[:, 2 * QKV : cut]], 1)
        far[at : at + SIDE, :] = jnp.concatenate([total[:, QKV : 2 * QKV], total[:, cut:]], 1).astype(bf16)
    extra = mine_q[SIDE:, :] + got_q[SIDE:, :].astype(f32)
    qkv, dat, up, dm = (extra[2 * k : 2 * k + 1] + extra[2 * k + 1 : 2 * k + 2] for k in range(4))
    pad = lambda row: jnp.concatenate([row, jnp.zeros((1, UP - QKV), f32)], 1)
    rows = two_rows(pad(qkv[:, QKV : 2 * QKV])) + two_rows(up[:, UP:])
    both = [two_rows(dat), two_rows(dm)]
    rows += [part[:, c : c + UP] for pair in both for part in pair for c in (0, UP)]
    far[288:304, :] = stacked(rows, 16).astype(bf16)
    low = lambda value: value.astype(bf16).astype(f32)
    wide = lambda row: jnp.concatenate([row, jnp.zeros((1, WIDTH - UP), f32)], 1)
    vectors[...] = stacked(
        [wide(pad(qkv[:, :QKV])), wide(up[:, :UP])] + [low(pair[0]) + low(pair[1]) for pair in both], 8
    )


def join(mines, gots):
    return call(
        join_body,
        "attn_join",
        [(a, VMEM) for a in (mines[0], gots[0], mines[1], gots[1])],
        [((288, UP), f32, VMEM), ((304, UP), bf16, VMEM), ((8, WIDTH), f32, VMEM)],
    )


def strip_rows(info, near, got, keep, send):
    mine = pl.ds(pl.multiple_of(info[CORE] * SIDE, 16), SIDE)
    theirs = pl.ds(pl.multiple_of((1 - info[CORE]) * SIDE, 16), SIDE)
    keep[...] = near[mine, :] + got[mine, :].astype(f32)
    send[:SIDE, :] = (near[theirs, :] + got[theirs, :].astype(f32)).astype(bf16)


def mlp_strip(info, near, got):
    width = near.shape[1]
    return call(
        strip_rows,
        "mlp_strip",
        [(info, SMEM), (near, VMEM), (got, VMEM)],
        [((SIDE, width), f32, VMEM), ((SIDE, width), bf16, VMEM)],
    )


def attn_strip_body(info, near, vectors, got, keep, send, total):
    strip_rows(info, near, got, keep, send)
    extra = got[288:304, :].astype(f32)
    low = lambda value: value.astype(bf16).astype(f32)
    wide = lambda row: jnp.concatenate([row, jnp.zeros((1, WIDTH - UP), f32)], 1)
    rows, totals = [], []
    for k in range(2):
        pair = two_rows(vectors[k : k + 1, :UP] + extra[2 * k : 2 * k + 1] + extra[2 * k + 1 : 2 * k + 2])
        rows += pair
        totals.append(wide(low(pair[0]) + low(pair[1])))
    for k in range(2):
        at = 4 + 4 * k
        row = jnp.concatenate([extra[at + j : at + j + 1] + extra[at + 2 + j : at + 3 + j] for j in range(2)], 1)
        totals.append(vectors[2 + k : 3 + k, :] + row)
    send[SIDE:, :] = stacked(rows, 16).astype(bf16)
    total[...] = stacked(totals, 8)


def attn_strip(info, near, vectors, got):
    width = near.shape[1]
    return call(
        attn_strip_body,
        "attn_strip",
        [(info, SMEM), (near, VMEM), (vectors, VMEM), (got, VMEM)],
        [((SIDE, width), f32, VMEM), ((SIDE + 16, width), bf16, VMEM), ((8, WIDTH), f32, VMEM)],
    )


def shampoo_body(wide, chained, info, keep, got, left, right, left_root, right_root, master, *rest):
    out_g, out_l, out_r, out_m = rest[4:] if chained else rest
    core = info[CORE]
    for step in range(4 if wide else 2):

        @pl.when(pl.program_id(0) == step)
        def _(step=step):
            for j in range(4):
                column, half = (4 * (step // 2) + j, step % 2) if wide else (2 * step + j // 2, j % 2)
                columns = slice(column * SIDE, (column + 1) * SIDE)
                value = jnp.where(core == half, keep[:, columns], got[:SIDE, columns].astype(f32))
                out_g[j] = value
                low = value.astype(bf16)
                out_l[j] = decay_rate * left[j] + (1.0 - decay_rate) * dot_t(low, low)
                out_r[j] = decay_rate * right[j] + (1.0 - decay_rate) * t_dot(low, low)
                first = dot(left_root[j].astype(bf16), low).astype(bf16)
                out_m[j] = master[j] - weight_rate * dot(first, right_root[j].astype(bf16))


def shampoo(info, keep, got, states, previous, wide):
    first = 2 if wide else 0
    tiles = pl.BlockSpec((4, SIDE, SIDE), lambda i: (first + i, 0, 0))
    whole = lambda a: pl.BlockSpec(a.shape, lambda i: (0, 0))
    inputs = [(info, SMEM), (keep, whole(keep)), (got, whole(got))] + [(s, tiles) for s in states]
    aliases = None
    if previous is not None:
        aliases = {len(inputs) + k: k for k in range(4)}
        inputs += [(p, ANY) for p in previous]
    return call(
        functools.partial(shampoo_body, wide, previous is not None),
        "shampoo",
        inputs,
        [(states[0].shape, f32, tiles)] * 4,
        aliases=aliases,
        grid=(4 if wide else 2,),
    )


def heads_of(qkv, up):
    rows = []
    for j in range(2):
        rows.append(
            jnp.concatenate(
                [
                    qkv[:, j * HEAD_DIM : (j + 1) * HEAD_DIM],
                    qkv[:, 2 * PAIRED + j * HEAD_DIM : 2 * PAIRED + (j + 1) * HEAD_DIM],
                    up[:, j * 288 : (j + 1) * 288],
                ],
                1,
            )
        )
    return rows


def bias_body(info, total, got, b_in, s_in, b_out, s_out, g_in, m_in, n_in, g_out, m_out, n_out):
    there = got[SIDE : SIDE + 16, :].astype(f32)
    mine = heads_of(total[0:1, :QKV], total[1:2, :UP])
    theirs = heads_of((there[0:1] + there[1:2])[:, :QKV], there[2:3] + there[3:4])
    zero = info[CORE] == 0
    rows = [jnp.where(zero, a, b) for a, b in zip(mine, theirs)]
    rows += [jnp.where(zero, b, a) for a, b in zip(mine, theirs)]
    for grad, base, square, g_ref, m_ref, n_ref in (
        (stacked(rows, 4), b_in, s_in, g_in, m_in, n_in),
        (total[2:4, :], b_out, s_out, g_out, m_out, n_out),
    ):
        new = decay_rate * square[...] + (1.0 - decay_rate) * grad * grad
        g_ref[...] = grad
        m_ref[...] = new
        n_ref[...] = base[...] - bias_rate * grad / (jnp.sqrt(new) + root_epsilon)


def bias_step(info, total, got, bias_in, bias_in_sq, bias_out, bias_out_sq):
    arrays = [total, got, bias_in, bias_in_sq, bias_out, bias_out_sq]
    return call(
        bias_body,
        "bias_step",
        [(info, SMEM)] + [(a, VMEM) for a in arrays],
        [(bias_in.shape, f32, VMEM)] * 3 + [(bias_out.shape, f32, VMEM)] * 3,
    )


def pass_body(far, block, rows):
    size = block.shape[0]
    block[...] = far[:size, :]
    rows[...] = far[size:, :]


def pass_on(far, after):
    width = far.shape[1]
    return call(
        pass_body,
        "pass_on",
        [(far, VMEM)],
        [((far.shape[0] - 16, width), bf16, VMEM), ((16, width), bf16, VMEM)],
        after=after,
    )


def finish_whole(attn_blocks, mlp_blocks, states, biases, core, head):
    left_stat, right_stat, left_root, right_root, master = states
    bias_in, bias_in_sq, bias_out, bias_out_sq = biases
    far_of = lambda v: over_head(v, 2)

    def halves(near):
        both = lax.all_gather(near.astype(bf16), "core").astype(f32)
        return [part.reshape(8, SIDE, -1, SIDE).transpose(2, 0, 1, 3) for part in (both[0], both[1])]

    full = jnp.concatenate([b[:288] for b in attn_blocks], 0)
    near, far = (
        jnp.concatenate([full[:, a : a + QKV], full[:, b : b + PAIRED]], 1) for a, b in ((0, 864), (432, 1008))
    )
    a0, a1 = halves(near.astype(f32) + far_of(far).astype(f32))
    near, far = (jnp.concatenate(mlp_blocks[2 * g : 2 * g + 2], 0).reshape(WIDTH, WIDTH) for g in range(2))
    m0, m1 = halves(near.astype(f32) + far_of(far).astype(f32))
    attn = jnp.stack([a0, a1], 1).reshape(8, 8, SIDE, SIDE)
    tiles = jnp.concatenate([attn, m0[:4], m1[:4], m0[4:], m1[4:]], 0)
    tiles = tiles.transpose(1, 0, 2, 3).reshape(192, SIDE, SIDE)
    tiles = lax.psum_scatter(tiles, "sup", scatter_dimension=0, tiled=True)
    count = master.shape[0]
    grad = lax.dynamic_slice_in_dim(tiles, core * count, count, 0)
    low = grad.astype(bf16)
    product = lambda spec, a, b: jnp.einsum(spec, a.astype(bf16), b.astype(bf16), preferred_element_type=f32)
    left_new = decay_rate * left_stat + (1.0 - decay_rate) * product("kab,kcb->kac", low, low)
    right_new = decay_rate * right_stat + (1.0 - decay_rate) * product("kba,kbc->kac", low, low)
    step = product("kab,kbc->kac", product("kab,kbc->kac", left_root, low), right_root)
    master_new = master - weight_rate * step
    attn_rows = attn_blocks[0][288:304].astype(f32)
    rows = [attn_rows[2 * k] + attn_rows[2 * k + 1] for k in range(4)]
    vector = lax.psum(jnp.stack(rows, 0), "sup")
    qkv, dat, up, dm = vector[0][: 2 * QKV], vector[1], vector[2], vector[3]
    rows = jnp.stack([dat, dm], 0)
    swap = lax.psum(rows, HEAD_AXES) * 0.5
    qkv = qkv[:QKV] + far_of(qkv[QKV:])
    up = up[:UP] + far_of(up[UP:])
    parts = [jnp.concatenate(heads_of(qkv[None], up[None]), 0)]
    grad_in = lax.all_gather(parts[0], "core", axis=0, tiled=True)
    out = [grad, left_new, right_new, master_new]
    for g, b, s in ((grad_in, bias_in, bias_in_sq), (swap, bias_out, bias_out_sq)):
        new = decay_rate * s + (1.0 - decay_rate) * g * g
        out += [g, new, b - bias_rate * g / (jnp.sqrt(new) + root_epsilon)]
    return out


def on_device(
    tokens,
    cotangent,
    modulation,
    counts,
    master,
    left_stat,
    right_stat,
    left_root,
    right_root,
    bias_in,
    bias_in_sq,
    bias_out,
    bias_out_sq,
):
    images, slots, _ = tokens.shape
    core = lax.axis_index("core")
    head = lax.axis_index(HEAD_AXES)
    number = images // 2
    strips = master.shape[0] == 24
    place = lax.axis_index("sup") if strips else 0
    order = core if strips else 0
    info = jnp.stack(
        [jnp.asarray(v, jnp.int32) for v in (place, order, core, head, head % 2, (head // 2) * number, head // 2, 0)]
    )
    LAST[0] = None
    attn_mine, bias_mine, mlp_mine, strips_other = pack(
        info, master if strips else jnp.zeros((24, SIDE, SIDE), f32), bias_in
    )
    if strips:
        block, mlp_block = blocks_of(attn_mine, bias_mine, mlp_mine, over_core(strips_other))
    small, part = small_rows(info, counts, modulation, tokens)
    far_tokens, far_small = over_core(part), over_core(small)
    if strips:
        mlp_near = lax.all_gather(mlp_block, "sup")
        far_block = over_head(block, 2)
        attn_near = gather_pieces(block)
    else:
        (attn_near, attn_far), (mlp_near, mlp_far) = whole_pieces(master, core)
        far_block = jnp.concatenate([attn_far[0], over_head(bias_mine, 2)], 0)
    act, dm_own, x_mine, g_mine = kept_rows(info, small, tokens, cotangent, far_small, far_tokens, number)
    dm_other = over_core(dm_own)
    if strips:
        mlp_far = over_head(relay(mlp_block, (far_block,)), 2)
    far_block, bias_far = pass_on(far_block, attn_near[1:])
    if strips:
        attn_far = gather_pieces(far_block)
    near = attend(info, act, bias_mine, attn_near, number)
    far = attend(info, act, bias_far, attn_far, number)
    if strips:
        mlp_far = lax.all_gather(relay(mlp_far), "sup")
    terms = sum_rows(project(info, near[0], far[0], near[3], far[3]))
    w_near = mlp_weights(info, mlp_near)
    hidden, attn, act_mine = middle(info, modulation, bias_out, x_mine, terms, number)
    act_far = over_head(act_mine, 1)
    w_far = mlp_weights(info, mlp_far)
    act_far = relay(act_far)
    pieces = (act_mine, act_far, over_core(act_mine), over_core(act_far))
    act_two, f, du, *db_parts = mlp(info, (bias_mine, bias_far), dm_own, dm_other, w_near, w_far, pieces, number)
    db_terms = sum_rows(db_parts, spare=32)
    mlp_parts = down_rows(info, f, w_near[1], w_far[1])
    mlp_terms = sum_rows(mlp_parts)
    dh, dat_mine, back_sums = back_middle(info, modulation, hidden, attn, g_mine, db_terms, number)
    dat_far = over_head(dat_mine, 1)
    *mlp_blocks, vectors = mlp_grads(info, act_two, du, f, dm_own, dm_other, strips)
    if strips:
        gots = [over_sup(mlp_blocks[0], 1), over_sup(mlp_blocks[1], 2)]
    output_mine, gate_sums = output_rows(info, modulation, bias_out, hidden, g_mine, mlp_terms, number)
    output_all = lax.all_gather(output_mine, HEAD_AXES, axis=0, tiled=True)
    dat_far = relay(dat_far, name="relay_dat")
    dat_pieces = (dat_mine, dat_far, over_core(dat_mine), over_core(dat_far))
    dat, near_grad, far_grad, *da_parts = attend_back(info, near, far, dat_pieces, number)
    da_terms = sum_rows(da_parts, spare=0)
    if strips:
        near_mine, far_mine, near_send, far_send = half_way(mlp_blocks[2:], gots, (da_terms[1],))
        gots = [over_sup(near_send, 2), over_sup(far_send, 1)]
    attn_blocks = attn_grads(info, act, dat, (near_grad, far_grad), near[3], far[3], vectors, strips)
    last, extra = last_rows(info, modulation, x_mine, dh, da_terms, back_sums, gate_sums, number)
    half = x_mine.shape[0]

    states = (left_stat, right_stat, left_root, right_root, master)
    biases = (bias_in, bias_in_sq, bias_out, bias_out_sq)
    if strips:
        mlp_near_sum, mlp_far_sum = mlp_join((near_mine, far_mine), gots)
        (output,) = expand_all(info, counts, output_all, images, slots)
        attn_gots = [over_sup(attn_blocks[0], 1), over_sup(attn_blocks[1], 2)]
        mine_p, mine_q, send_p, send_q = attn_half(attn_blocks[2:], attn_gots)
        attn_gots = [over_sup(send_p, 2), over_sup(send_q, 1)]
        near_sum, far_sum, sums = join((mine_p, mine_q), attn_gots)
        far_got = over_head(far_sum, 2)
        last_pieces, mlp_far_sum = gather_last(last, mlp_far_sum)
        mlp_far_got = over_head(mlp_far_sum, 2)
        keep, send, total = attn_strip(info, near_sum, sums, far_got)
        got = over_core(send)
        previous = shampoo(info, keep, got, states, None, False)
        grad_tokens, grad_modulation = expand(info, counts, half + extra, last_pieces, images, slots, extra)
        steps = bias_step(info, total, got, *biases)
        mlp_keep, mlp_send = mlp_strip(info, mlp_near_sum, mlp_far_got)
        mlp_got = over_core(mlp_send)
        weights = shampoo(info, mlp_keep, mlp_got, states, previous, True)
        tail = list(weights) + list(steps)
    else:
        last_pieces, _ = gather_last(last, act_mine)
        grad_tokens, grad_modulation = expand(info, counts, half + extra, last_pieces, images, slots, extra)
        (output,) = expand_all(info, counts, output_all, images, slots)
        tail = finish_whole(attn_blocks, mlp_blocks, states, biases, core, head)
    return (output, grad_tokens, grad_modulation, *tail)


def solution(mesh):
    devices = mesh.devices
    inner = Mesh(
        devices.reshape(devices.shape[0] // 2, 2, 2, devices.shape[1] // 2), ("sup", "core", *HEAD_AXES)
    )
    seq = ("sup", "core")
    tile = P(("sup", "core", *HEAD_AXES), None, None)
    rows = P(seq, None, None)
    return jax.shard_map(
        on_device,
        mesh=inner,
        in_specs=(rows, rows, rows, P(seq, None), tile, tile, tile, tile, tile)
        + (P(HEAD_AXES, None), P(HEAD_AXES, None), P(), P()),
        out_specs=(rows, rows, P(seq, None, HEAD_AXES), tile, tile, tile, tile)
        + (P(HEAD_AXES, None),) * 3
        + (P(),) * 3,
        check_vma=False,
    )
```

```python
import functools

import jax
import jax.numpy as jnp
from jax import lax
from jax.experimental import pallas as pl
from jax.experimental.pallas import tpu as pltpu
from jax.sharding import Mesh, PartitionSpec as P

HEADS = 16
HEAD_DIM = 72
KEPT = 128
SIDE = 144
RANGES = 8
SLOTS = 24
WIDTH = 1152
QKV = 432
PAIRED = 144
UP = 576

norm_epsilon = 1e-06
decay_rate = 0.5
weight_rate = 0.3
bias_rate = 0.1
root_epsilon = 1e-08
score_scale = HEAD_DIM ** (-0.5)
bf16 = jnp.bfloat16
f32 = jnp.float32
CORE_SWAP = [(0, 1), (1, 0)]
HEAD_AXES = ("hp", "hq")

SUP, ORDER, CORE, HEAD, HALF, FIRST, GROUP = range(7)
ANY = pl.BlockSpec(memory_space=pl.ANY)
VMEM = pl.BlockSpec(memory_space=pltpu.VMEM)
SMEM = pl.BlockSpec(memory_space=pltpu.SMEM)


def dot(a, b):
    return lax.dot_general(a, b, (((1,), (0,)), ((), ())), preferred_element_type=f32)


def dot_t(a, b):
    return lax.dot_general(a, b, (((1,), (1,)), ((), ())), preferred_element_type=f32)


def t_dot(a, b):
    return lax.dot_general(a, b, (((0,), (0,)), ((), ())), preferred_element_type=f32)


def normalize(values):
    center = jnp.mean(values, -1, keepdims=True)
    centered = values - center
    inverse = lax.rsqrt(jnp.mean(centered * centered, -1, keepdims=True) + norm_epsilon)
    return (centered * inverse, inverse)


def norm_back(grad_in, normed, inverse):
    inner = jnp.mean(grad_in * normed, -1, keepdims=True)
    return inverse * (grad_in - jnp.mean(grad_in, -1, keepdims=True) - normed * inner)


def over_both(values):
    pairs = [(i, i ^ 5) for i in range(8)]
    return lax.ppermute(values, ("core", "hp", "hq"), pairs)


def over_core(values):
    return lax.ppermute(values, "core", CORE_SWAP)


def over_head(values, offset):
    return lax.ppermute(values, HEAD_AXES, [(i, i ^ offset) for i in range(4)])


def over_sup(values, offset):
    return lax.ppermute(values, "sup", [(i, i ^ offset) for i in range(4)])


def shaped(shape, dtype):
    return jax.ShapeDtypeStruct(shape, dtype)


LAST = [None]
VMEM_MIB = dict(mlp=32, mlp_grads=28, attend_back=26, down=20, kept_rows=20, attn_grads=24)
TIMES = dict(last_rows=10, relay_dat=3, relay_last=5, expand_rows=3, back_middle=10)
COST = 0.02


def call(body, name, inputs, outputs, scratch=(), flops=0, aliases=None, after=(), cost=0, grid=()):
    inputs = list(inputs)
    count = len(inputs)
    if LAST[0] is not None and all(LAST[0] is not array for array, _ in inputs):
        inputs.append((LAST[0], ANY))
    inputs += [(a, ANY) for a in after]
    arrays = [array for array, _ in inputs]
    shapes = [shaped(shape, dtype) for shape, dtype, _ in outputs]

    size = sum(a.size * a.dtype.itemsize for a in arrays[:count] + shapes)

    def ordered(*refs):
        return body(*refs[:count], *refs[len(arrays) :])

    results = pl.pallas_call(
        ordered,
        name=name,
        grid=grid,
        out_shape=shapes,
        in_specs=[spec for _, spec in inputs],
        out_specs=[spec for _, _, spec in outputs],
        scratch_shapes=list(scratch),
        input_output_aliases=aliases or {},
        cost_estimate=pl.CostEstimate(flops=int(1.0e9 * TIMES.get(name, 0.02)), bytes_accessed=0, transcendentals=0),
        compiler_params=pltpu.CompilerParams(vmem_limit_bytes=VMEM_MIB.get(name, 16) * 1024 * 1024),
    )(*arrays)
    LAST[0] = min(results, key=lambda a: a.size * a.dtype.itemsize)
    return results


def chunks_of(rows, size):
    return [slice(at, min(at + size, rows)) for at in range(0, rows, size)]


def started(copies):
    for copy in copies:
        copy.start()
    return copies


def finish(copies):
    for copy in copies:
        copy.wait()


def pack_body(info, master, bias, mine, rows, mlp_mine, other, held, sems):
    copies = started(
        [pltpu.make_async_copy(master.at[pl.ds(8 * k, 8)], held.at[pl.ds(8 * k, 8)], sems.at[k]) for k in range(3)]
    )
    core = info[CORE]
    heads = [jnp.where(core == 0, bias[j : j + 1, :], bias[j + 2 : j + 3, :]) for j in range(2)]
    both = lambda a, b: jnp.concatenate([heads[0][:, a:b], heads[1][:, a:b]], 1)
    blank = jnp.zeros((1, PAIRED), f32)
    first = jnp.concatenate([both(0, HEAD_DIM), blank, both(HEAD_DIM, 2 * HEAD_DIM), blank], 1)
    rows[...] = stacked(three_rows(first) + three_rows(both(2 * HEAD_DIM, QKV)), 16).astype(bf16)
    copies[0].wait()
    attn = lambda half: jnp.concatenate([held[2 * k + half].astype(bf16) for k in range(4)], 1)
    mine[...] = attn(core)
    part = attn(1 - core)
    other[SIDE:, :] = jnp.concatenate([part[: SIDE // 2], part[SIDE // 2 :]], 1)
    finish(copies[1:])
    mlp = lambda half: jnp.concatenate(
        [held[8 + 8 * w + 4 * half + k].astype(bf16) for w in range(2) for k in range(4)], 1
    )
    mlp_mine[...] = mlp(core)
    other[:SIDE, :] = mlp(1 - core)


def pack(info, master, bias_in):
    return call(
        pack_body,
        "pack",
        [(info, SMEM), (master, ANY), (bias_in, VMEM)],
        [
            ((SIDE, 4 * SIDE), bf16, VMEM),
            ((16, 4 * SIDE), bf16, VMEM),
            ((SIDE, 8 * SIDE), bf16, VMEM),
            ((3 * SIDE // 2, 8 * SIDE), bf16, VMEM),
        ],
        [pltpu.VMEM((24, SIDE, SIDE), f32), pltpu.SemaphoreType.DMA((3,))],
    )


def blocks_body(mine, rows, mlp_mine, got, block, mlp_block):
    block[:SIDE, :] = mine[...]
    part = got[SIDE:, :]
    block[SIDE : 2 * SIDE, :] = jnp.concatenate([part[:, : 4 * SIDE], part[:, 4 * SIDE :]], 0)
    block[2 * SIDE :, :] = rows[...]
    mlp_block[:SIDE, :] = mlp_mine[...]
    mlp_block[SIDE:, :] = got[:SIDE, :]


def blocks_of(mine, rows, mlp_mine, got):
    return call(
        blocks_body,
        "blocks",
        [(a, VMEM) for a in (mine, rows, mlp_mine, got)],
        [((2 * SIDE + 16, 4 * SIDE), bf16, VMEM), ((2 * SIDE, 8 * SIDE), bf16, VMEM)],
    )


def piece_copies(info, pieces, target, sems, sup=None):
    copies = []
    sup = info[SUP] if sup is None else sup
    for k in range(4):
        for j in range(2):
            row = ((sup ^ k) * 2 + (info[ORDER] ^ j)) * SIDE
            copies.append(
                pltpu.make_async_copy(
                    pieces[k].at[pl.ds(j * SIDE, SIDE)],
                    target.at[pl.ds(pl.multiple_of(row, 16), SIDE)],
                    sems.at[2 * k + j],
                )
            )
    return copies


def gather_pieces(block):
    return [block] + [over_sup(block, k) for k in (1, 2, 3)]


def whole_pieces(master, core):
    tiles = lax.all_gather(master.astype(bf16), ("sup", "core"), axis=0, tiled=True)
    slab = tiles.reshape(8, 24, SIDE, SIDE).transpose(1, 0, 2, 3).reshape(24, 8 * SIDE, SIDE)
    take = lambda k: lax.dynamic_index_in_dim(slab, k, 0, False)
    attn = jnp.concatenate([take(2 * k + core) for k in range(4)], 1)
    mlp = jnp.concatenate([take(8 + 8 * w + 4 * core + k) for w in range(2) for k in range(4)], 1)
    out = []
    far = over_head(attn, 2)
    pieces = [[part[288 * k : 288 * k + 288] for k in range(4)] for part in (attn, far)]
    return pieces, [p.reshape(4, 288, 2 * UP) for p in (mlp, over_head(mlp, 2))]


def later_body(mine, got, out):
    out[: mine.shape[0], :] = mine[...]
    out[mine.shape[0] :, :] = got[...]


def copies_body(mine, *rest):
    out = rest[-1]
    for k in range(out.shape[0]):
        out[k, : mine.shape[0], :] = mine[...]
        if len(rest) > 1:
            out[k, mine.shape[0] :, :] = rest[0][...]


def copies_of(parts, count):
    rows = sum(p.shape[0] for p in parts)
    return call(
        copies_body, "copies", [(p, VMEM) for p in parts], [((count, rows, parts[0].shape[1]), bf16, VMEM)]
    )[0]


def to_all(values, axis):
    return lax.all_to_all(values, axis, 0, 0)


def later_block(mine, got, after=()):
    rows = mine.shape[0] + got.shape[0]
    return call(
        later_body, "later_block", [(mine, VMEM), (got, VMEM)], [((rows, mine.shape[1]), bf16, VMEM)], after=after
    )[0]


def small_body(info, counts, modulation, tokens, out, part, sem):
    images = out.shape[0]
    copies = started([pltpu.make_async_copy(tokens.at[pl.ds(info[FIRST], part.shape[0])], part, sem)])
    out[:, :6, :] = modulation[...]
    place = lax.broadcasted_iota(jnp.int32, (2, WIDTH), 1)
    for i in range(images):
        row = jnp.zeros((2, WIDTH), f32)
        for s in range(RANGES):
            row = jnp.where(place == s, counts[i, s].astype(f32), row)
        out[i, 6:8, :] = row
    finish(copies)


def small_rows(info, counts, modulation, tokens):
    shape = (modulation.shape[0], 8, WIDTH)
    part = (tokens.shape[0] // 2, *tokens.shape[1:])
    return call(
        small_body,
        "small_rows",
        [(info, SMEM), (counts, SMEM), (modulation, VMEM), (tokens, ANY)],
        [(shape, f32, VMEM), (part, bf16, VMEM)],
        [pltpu.SemaphoreType.DMA],
    )


def kept_target_of(row, slot):
    target = jnp.full(slot.shape, -1.0, f32)
    start = jnp.zeros((1, 1), f32)
    for s in range(RANGES):
        number = row[:, s : s + 1]
        place = slot - s * SLOTS
        target = jnp.where((place >= 0) & (place < number), place + start, target)
        start = start + number
    return target


def rows_body(number, info, small, tokens, cotangent, far_small, far_tokens, act, dm, x_mine, g_mine, tok, cot, x_own, g_own, sems):
    first = info[FIRST]
    copies = started(
        [
            pltpu.make_async_copy(tokens.at[pl.ds(first, number)], tok.at[pl.ds(0, number)], sems.at[0]),
            pltpu.make_async_copy(far_tokens, tok.at[pl.ds(number, number)], sems.at[1]),
            pltpu.make_async_copy(cotangent.at[pl.ds(first, number)], cot, sems.at[2]),
        ]
    )
    finish(copies)
    slots = tok.shape[1]
    slot = lax.broadcasted_iota(jnp.int32, (1, slots), 1).astype(f32)
    place = lax.broadcasted_iota(jnp.int32, (KEPT, slots), 0).astype(f32)
    for i in range(2 * number):
        mod = (small if i < number else far_small)[first + i % number]
        select = (kept_target_of(mod[6:7], slot) == place).astype(f32).astype(bf16)
        rows = slice(i * KEPT, (i + 1) * KEPT)
        x = dot(select, tok[i])
        normed, _ = normalize(x)
        act[rows, :] = (normed * (1.0 + mod[1:2]) + mod[0:1]).astype(bf16)
        if i < number:
            x_own[rows, :] = x.astype(bf16)
            g = dot(select, cot[i])
            g_own[rows, :] = g.astype(bf16)
            dm[rows, :] = (mod[5:6] * g).astype(bf16)
    half = x_mine.shape[0]
    mine = pl.ds(pl.multiple_of(info[HALF] * half, 64), half)
    x_mine[...] = x_own[mine, :]
    g_mine[...] = g_own[mine, :]


def kept_rows(info, small, tokens, cotangent, far_small, far_tokens, number):
    slots = tokens.shape[1]
    rows = number * KEPT
    half = rows // 2
    return call(
        functools.partial(rows_body, number),
        "kept_rows",
        [(info, SMEM), (small, VMEM), (tokens, ANY), (cotangent, ANY), (far_small, VMEM), (far_tokens, ANY)],
        [((2 * rows, WIDTH), bf16, VMEM), ((rows, WIDTH), bf16, VMEM)] + [((half, WIDTH), bf16, VMEM)] * 2,
        [pltpu.VMEM((2 * number, slots, WIDTH), bf16), pltpu.VMEM((number, slots, WIDTH), bf16)]
        + [pltpu.VMEM((rows, WIDTH), bf16)] * 2
        + [pltpu.SemaphoreType.DMA((3,))],
        flops=6 * rows * slots * WIDTH,
    )


def spread_of(counts, image):
    parts = []
    start = 0
    slot = lax.broadcasted_iota(jnp.int32, (SLOTS, KEPT), 0)
    row = lax.broadcasted_iota(jnp.int32, (SLOTS, KEPT), 1)
    for s in range(RANGES):
        number = counts[image, s]
        parts.append(((row == slot + start) & (slot < number)).astype(f32))
        start = start + number
    return jnp.concatenate(parts, 0).astype(bf16)


def expand_body(images, extra, size, places, info, counts, *rest):
    pieces, (out, sums, held, sems) = rest[: len(places)], rest[len(places) :]
    half = size - extra
    copies = []
    for n, (k, at) in enumerate(places):
        row = pl.multiple_of((info[HEAD] ^ k) * size + at, 16)
        copies.append(pltpu.make_async_copy(pieces[n], held.at[pl.ds(row, pieces[n].shape[0])], sems.at[n]))
    finish(started(copies))
    parts = half // 64
    for i in range(images):
        spread = spread_of(counts, i)
        chunks = []
        for chunk in (2 * i, 2 * i + 1):
            row = (chunk // parts) * size + (chunk % parts) * 64
            chunks.append(held[row : row + 64, :])
        out[i] = dot(spread, jnp.concatenate(chunks, 0)).astype(bf16)
        if True:
            total = jnp.zeros((6, WIDTH), f32)
            for chunk in (2 * i, 2 * i + 1):
                base = (chunk // parts) * size + half
                block = held[base : base + extra, :].astype(f32)
                at = (chunk % parts) * 6
                total = total + block[at : at + 6]
            quarter = WIDTH // 4
            picked = total[:, :quarter]
            for k in range(1, 4):
                picked = jnp.where(info[HEAD] == k, total[:, k * quarter : (k + 1) * quarter], picked)
            sums[i] = picked


def expand(info, counts, size, pieces, images, slots, extra):
    return call(
        functools.partial(expand_body, images, extra, size, [(k, at) for _, k, at in pieces]),
        "expand_rows",
        [(info, SMEM), (counts, SMEM)] + [(p, ANY) for p, _, _ in pieces],
        [((images, slots, WIDTH), bf16, VMEM), ((images, 6, WIDTH // 4), f32, VMEM)],
        [pltpu.VMEM((4 * size, WIDTH), bf16), pltpu.SemaphoreType.DMA((len(pieces),))],
        flops=2 * images * slots * KEPT * WIDTH,
    )


def expand_all_body(images, info, counts, rows, out):
    for i in range(images):
        spread = spread_of(counts, i)
        out[i] = dot(spread, rows[i * KEPT : (i + 1) * KEPT, :]).astype(bf16)


def expand_all(info, counts, rows, images, slots):
    return call(
        functools.partial(expand_all_body, images),
        "expand_output",
        [(info, SMEM), (counts, SMEM), (rows, VMEM)],
        [((images, slots, WIDTH), bf16, VMEM)],
        flops=2 * images * slots * KEPT * WIDTH,
    )


def both_copies(own, other, target, sems):
    rows = target.shape[0] // 2
    return [
        pltpu.make_async_copy(ref, target.at[pl.ds(k * rows, rows)], sems.at[k]) for k, ref in enumerate((own, other))
    ]


def first_sum_body(mine, got, send):
    send[: mine.shape[0], :] = (mine[...].astype(f32) + got[...].astype(f32)).astype(send.dtype)
    if send.shape[0] > mine.shape[0]:
        send[mine.shape[0] :, :] = jnp.zeros((send.shape[0] - mine.shape[0], send.shape[1]), send.dtype)


def sum_rows(parts, kind=bf16, spare=0):
    own_send, own_keep, other_send, other_keep = parts
    got, got_keep = over_core(other_send), over_core(other_keep)
    rows, width = own_send.shape
    (send,) = call(first_sum_body, "first_sum", [(own_send, VMEM), (got, VMEM)], [((rows + spare, width), kind, VMEM)])
    return own_keep, got_keep, over_head(send, 1)


def relay_body(got, out):
    out[...] = got[...]


def relay_two_body(got, held, first, second, later):
    later[...] = held[...]
    first[...] = got[: first.shape[0], :]
    second[...] = got[first.shape[0] :, :]


def relay_two(got, held, after):
    part = got.shape[0] // 32 * 16
    shapes = [(part, got.shape[1]), (got.shape[0] - part, got.shape[1])]
    shapes.append(held.shape)
    return call(
        relay_two_body,
        "relay_last",
        [(got, VMEM), (held, VMEM)],
        [(shape, bf16, VMEM) for shape in shapes],
        after=after,
    )


def relay(got, after=(), name="relay"):
    return call(relay_body, name, [(got, VMEM)], [(got.shape, got.dtype, VMEM)], after=after)[0]


def all_terms(terms, rows):
    total = terms[0][rows, :].astype(f32)
    for term in terms[1:]:
        total = total + term[rows, :].astype(f32)
    return total


def share_copies(info, pieces, target, sems):
    half = pieces[0].shape[0]
    copies = []
    for k in range(4):
        row = (k // 2) * 2 * half + (info[HALF] ^ (k % 2)) * half
        copies.append(
            pltpu.make_async_copy(pieces[k], target.at[pl.ds(pl.multiple_of(row, 64), half)], sems.at[k])
        )
    return copies


def split_halves(info, full, outs):
    half = outs[0].shape[0]
    for k in range(4):
        place = info[HALF] if k % 2 else 1 - info[HALF]
        outs[k][...] = full[pl.ds(pl.multiple_of((2 * (k // 2) + place) * half, 64), half), :].astype(bf16)


def head_mask():
    return lax.broadcasted_iota(jnp.int32, (KEPT, PAIRED), 1) < HEAD_DIM


def split_heads(values, mask):
    zero = jnp.zeros_like(values)
    return jnp.concatenate([jnp.where(mask, values, zero), jnp.where(mask, zero, values)], 0)


def sum_of_rows(ref, first):
    rows = ref[...].astype(f32)
    return rows[first : first + 1] + rows[first + 1 : first + 2] + rows[first + 2 : first + 3]


def attend_body(number, info, act, bias, w0, w1, w2, w3, weights, qkv, probs, mixed, sems):
    finish(started(piece_copies(info, (w0, w1, w2, w3), weights, sems)))
    mask = head_mask()
    bias = sum_of_rows(bias, 0)[:, :QKV]
    for rows in chunks_of(act.shape[0], 384):
        qkv[rows, :] = (dot(act[rows, :], weights[:, :QKV]) + bias).astype(bf16)
    for i in range(2 * number):
        rows = slice(i * KEPT, (i + 1) * KEPT)
        here = qkv[rows, :]
        q, k, v = (here[:, j * PAIRED : (j + 1) * PAIRED] for j in range(3))
        scores = dot_t(split_heads(q, mask), k) * score_scale
        raised = jnp.exp(scores - jnp.max(scores, -1, keepdims=True))
        p = raised / jnp.sum(raised, -1, keepdims=True)
        low = p.astype(bf16)
        probs[i] = low
        wide = jnp.concatenate([low[:KEPT], low[KEPT:]], 1)
        mixed[rows, :] = dot(wide, split_heads(v, mask)).astype(bf16)


def attend(info, act, bias, pieces, number):
    rows = 2 * number * KEPT
    return call(
        functools.partial(attend_body, number),
        "attend",
        [(info, SMEM), (act, VMEM), (bias, VMEM)] + [(p, ANY) for p in pieces],
        [
            ((WIDTH, QKV + PAIRED), bf16, VMEM),
            ((rows, QKV), bf16, VMEM),
            ((2 * number, 2 * KEPT, KEPT), bf16, VMEM),
            ((rows, PAIRED), bf16, VMEM),
        ],
        [pltpu.SemaphoreType.DMA((8,))],
        flops=2 * rows * WIDTH * QKV,
    )


def project_body(info, near_w, far_w, near, far, *rest):
    outs, full = rest[:4], rest[4]
    wa = near_w[:, QKV:]
    wb = far_w[:, QKV:]
    for rows in chunks_of(near.shape[0], 384):
        full[rows, :] = (dot_t(near[rows, :], wa) + dot_t(far[rows, :], wb)).astype(bf16)
    split_halves(info, full, outs)


def halves_of(rows):
    return [((rows // 4, WIDTH), bf16, VMEM)] * 4


def project(info, near_w, far_w, near, far):
    rows = near.shape[0]
    return call(
        project_body,
        "project",
        [(info, SMEM), (near_w, VMEM), (far_w, VMEM), (near, VMEM), (far, VMEM)],
        halves_of(rows),
        [pltpu.VMEM((rows, WIDTH), bf16)],
        flops=4 * rows * WIDTH * PAIRED,
    )


def middle_body(number, info, modulation, bias_out, x_mine, *rest):
    terms, (hidden, attn, act) = rest[:-3], rest[-3:]
    half = x_mine.shape[0]
    parts = half // 64
    for t in range(parts):
        rows = slice(t * 64, (t + 1) * 64)
        mod = modulation[info[FIRST] + (info[HALF] * parts + t) // 2]
        a = all_terms(terms, rows) + bias_out[0:1, :]
        h = x_mine[rows, :].astype(f32) + mod[2:3] * a
        attn[rows, :] = a
        hidden[rows, :] = h
        normed, _ = normalize(h)
        act[rows, :] = (normed * (1.0 + mod[4:5]) + mod[3:4]).astype(bf16)


def middle(info, modulation, bias_out, x_mine, terms, number):
    half = x_mine.shape[0]
    return call(
        functools.partial(middle_body, number),
        "middle",
        [(info, SMEM), (modulation, VMEM), (bias_out, VMEM), (x_mine, VMEM)] + [(t, VMEM) for t in terms],
        [((half, WIDTH), f32, VMEM)] * 2 + [((half, WIDTH), bf16, VMEM)],
    )


def mlp_weights_body(relative, info, *refs):
    pieces, (up, down, held, sems) = refs[:4], refs[4:]
    finish(started(piece_copies(info, pieces, held, sems, None if relative else 0)))
    for i in range(8):
        rows = slice(i * SIDE, (i + 1) * SIDE)
        up[rows, :] = held[rows, :UP]
        down[rows, :] = held[rows, UP:]


def whole_body(info, whole, *refs):
    mlp_weights_body(False, info, *[whole.at[k] for k in range(4)], *refs)


def mlp_weights(info, pieces):
    relative = isinstance(pieces, list)
    arrays = pieces if relative else [pieces]
    return call(
        functools.partial(mlp_weights_body, True) if relative else whole_body,
        "mlp_weights",
        [(info, SMEM)] + [(p, ANY) for p in arrays],
        [((WIDTH, UP), bf16, VMEM)] * 2,
        [pltpu.VMEM((WIDTH, 2 * UP), bf16), pltpu.SemaphoreType.DMA((8,))],
    )


def smooth_both(u):
    c = 0.7978845608028654
    cube = 0.044715
    square = u * u
    t = jnp.tanh(c * u * (1.0 + cube * square))
    half_up = 0.5 * (1.0 + t)
    slope = half_up + 0.5 * u * (1.0 - t * t) * (c * (1.0 + 3.0 * cube * square))
    return u * half_up, slope


def mlp_body(number, info, near_bias, far_bias, own, other, near_up, near_down, far_up, far_down, s0, s1, s2, s3, *rest):
    act, f, du, g0, g1, g2, g3, db, dm, dm_sems, sems = rest
    copies = started(both_copies(own, other, dm, dm_sems))
    finish(copies + started(share_copies(info, (s0, s1, s2, s3), act, sems)))
    biases = [sum_of_rows(ref, 3) for ref in (near_bias, far_bias)]
    for rows in chunks_of(act.shape[0], 384):
        values, lows = [], []
        total = 0.0
        for g, (up, down) in enumerate(((near_up, near_down), (far_up, far_down))):
            u = dot(act[rows, :], up[...]) + biases[g]
            value, slope = smooth_both(u)
            low = (dot(dm[rows, :], down[...]) * slope).astype(bf16)
            total = total + dot_t(low, up[...])
            values.append(value.astype(bf16))
            lows.append(low)
        f[rows, :] = jnp.concatenate(values, 1)
        du[rows, :] = jnp.concatenate(lows, 1)
        db[rows, :] = total.astype(bf16)
    split_halves(info, db, (g0, g1, g2, g3))


def mlp(info, biases, own, other, near, far, pieces, number):
    rows = 2 * number * KEPT
    full = ((rows, WIDTH), bf16, VMEM)
    return call(
        functools.partial(mlp_body, number),
        "mlp",
        [(info, SMEM), (biases[0], VMEM), (biases[1], VMEM), (own, ANY), (other, ANY)]
        + [(a, VMEM) for a in (*near, *far)]
        + [(p, ANY) for p in pieces],
        [full] * 3 + halves_of(rows),
        [pltpu.VMEM((rows, WIDTH), bf16)] * 2 + [pltpu.SemaphoreType.DMA((2,)), pltpu.SemaphoreType.DMA((4,))],
        flops=6 * rows * WIDTH * WIDTH,
    )


def down_body(info, f, near_w, far_w, *rest):
    outs, full = rest[:4], rest[4]
    for rows in chunks_of(f.shape[0], 384):
        full[rows, :] = (dot_t(f[rows, :UP], near_w[...]) + dot_t(f[rows, UP:], far_w[...])).astype(bf16)
    split_halves(info, full, outs)


def down_rows(info, f, near_w, far_w):
    rows = f.shape[0]
    return call(
        down_body,
        "down",
        [(info, SMEM), (f, VMEM), (near_w, VMEM), (far_w, VMEM)],
        halves_of(rows),
        [pltpu.VMEM((rows, WIDTH), bf16)],
        flops=2 * rows * WIDTH * WIDTH,
    )


def two_rows(values):
    high = values.astype(bf16)
    return [high.astype(f32), values - high.astype(f32)]


def three_rows(values):
    high, rest = two_rows(values)
    return [high] + two_rows(rest)


def stacked(rows, count):
    width = rows[0].shape[1]
    place = lax.broadcasted_iota(jnp.int32, (count, width), 0)
    out = jnp.zeros((count, width), f32)
    for k, row in enumerate(rows):
        out = jnp.where(place == k, row, out)
    return out


def block_copies(strips, info, full, extra, outs, sems):
    copies = []

    def add(source, target):
        copies.append(pltpu.make_async_copy(source, target, sems.at[len(copies)]))

    if strips:
        moves = ((0, 0, (1, 3)), (1, 1, (2, 3)), (2, 0, (0, 2)), (3, 1, (0, 1)))
        for out, part, places in moves:
            for j, k in enumerate(places):
                row = pl.multiple_of((info[SUP] ^ k) * 288 + part * SIDE, 16)
                add(full.at[pl.ds(row, SIDE)], outs[out].at[j, pl.ds(0, SIDE)])
                if part:
                    add(extra, outs[out].at[j, pl.ds(SIDE, 16)])
    else:
        for k in range(4):
            add(full.at[pl.ds(k * 288, 288)], outs[k].at[pl.ds(0, 288)])
            add(extra, outs[k].at[pl.ds(288, 16)])
    return copies


def column_sums(ref):
    half = ref.shape[0] // 2
    first = jnp.sum(ref[:half, :].astype(f32), 0, keepdims=True)
    return first + jnp.sum(ref[half:, :].astype(f32), 0, keepdims=True)


def mlp_grads_body(strips, info, act, du, f, own, other, o0, o1, o2, o3, vectors, dm, full, dm_sems, sems):
    finish(started(both_copies(own, other, dm, dm_sems)))
    for part in (slice(0, 512), slice(512, WIDTH)):
        up = t_dot(act[:, part], du[...]).astype(bf16)
        down = t_dot(dm[:, part], f[...]).astype(bf16)
        for g in range(2):
            columns = slice(g * UP, (g + 1) * UP)
            full[g, part, :] = jnp.concatenate([up[:, columns], down[:, columns]], 1)
    if strips:
        moves = ((0, o0, (1, 3)), (1, o1, (2, 3)), (0, o2, (0, 2)), (1, o3, (0, 1)))
    else:
        moves = [(g, o, (2 * h, 2 * h + 1)) for g, h, o in ((0, 0, o0), (0, 1, o1), (1, 0, o2), (1, 1, o3))]
    copies = []
    for g, out, places in moves:
        for j, k in enumerate(places):
            row = pl.multiple_of((info[SUP] ^ k) * 288, 16)
            copies.append(pltpu.make_async_copy(full.at[g, pl.ds(row, 288)], out.at[j], sems.at[len(copies)]))
    started(copies)
    vectors[...] = stacked([column_sums(du), column_sums(dm)], 8)
    finish(copies)


def mlp_grads(info, act, du, f, own, other, strips):
    rows = act.shape[0]
    return call(
        functools.partial(mlp_grads_body, strips),
        "mlp_grads",
        [(info, SMEM), (act, VMEM), (du, VMEM), (f, VMEM), (own, ANY), (other, ANY)],
        [((2, 288, WIDTH), bf16, ANY)] * 4 + [((8, WIDTH), f32, VMEM)],
        [pltpu.VMEM((rows, WIDTH), bf16), pltpu.VMEM((2, WIDTH, WIDTH), bf16)]
        + [pltpu.SemaphoreType.DMA((2,)), pltpu.SemaphoreType.DMA((8,))],
        flops=4 * rows * WIDTH * WIDTH,
    )


def half_way_body(near_keep, near_got, far_keep, far_got, near, far, near_send, far_send):
    for keep, got, mine, send in ((near_keep, near_got, near, near_send), (far_keep, far_got, far, far_send)):
        mine[...] = keep[0].astype(f32) + got[0].astype(f32)
        send[...] = (keep[1].astype(f32) + got[1].astype(f32)).astype(bf16)


def half_way(keeps, gots, after):
    return call(
        half_way_body,
        "half_way",
        [(a, VMEM) for a in (keeps[0], gots[0], keeps[1], gots[1])],
        [((288, WIDTH), f32, VMEM)] * 2 + [((288, WIDTH), bf16, VMEM)] * 2,
        after=after,
    )


def mlp_join_body(near_mine, near_got, far_mine, far_got, near, far):
    near[...] = near_mine[...] + near_got[...].astype(f32)
    far[...] = (far_mine[...] + far_got[...].astype(f32)).astype(bf16)


def mlp_join(mines, gots):
    return call(
        mlp_join_body,
        "mlp_join",
        [(a, VMEM) for a in (mines[0], gots[0], mines[1], gots[1])],
        [((288, WIDTH), f32, VMEM), ((288, WIDTH), bf16, VMEM)],
    )


def output_body(number, info, modulation, bias_out, hidden, g_mine, *rest):
    terms, (out, sums) = rest[:-2], rest[-2:]
    half = hidden.shape[0]
    parts = half // 64
    for t in range(parts):
        rows = slice(t * 64, (t + 1) * 64)
        mod = modulation[info[FIRST] + (info[HALF] * parts + t) // 2]
        m = all_terms(terms, rows) + bias_out[1:2, :]
        value = (hidden[rows, :] + mod[5:6] * m).astype(bf16)
        out[rows, :] = value
        sums[t : t + 1, :] = jnp.sum(g_mine[rows, :].astype(f32) * m, 0, keepdims=True)


def output_rows(info, modulation, bias_out, hidden, g_mine, terms, number):
    half = hidden.shape[0]
    return call(
        functools.partial(output_body, number),
        "output_rows",
        [(info, SMEM), (modulation, VMEM), (bias_out, VMEM), (hidden, VMEM), (g_mine, VMEM)]
        + [(t, VMEM) for t in terms],
        [((half, WIDTH), bf16, VMEM), ((half // 64, WIDTH), f32, VMEM)],
    )


def back_middle_body(number, info, modulation, hidden, attn, g_mine, *rest):
    terms, (dh, dat, sums) = rest[:-3], rest[-3:]
    half = hidden.shape[0]
    parts = half // 64
    for t in range(parts):
        rows = slice(t * 64, (t + 1) * 64)
        mod = modulation[info[FIRST] + (info[HALF] * parts + t) // 2]
        db = all_terms(terms, rows)
        normed, inverse = normalize(hidden[rows, :])
        grad = g_mine[rows, :].astype(f32) + norm_back(db * (1.0 + mod[4:5]), normed, inverse)
        dh[rows, :] = grad
        dat[rows, :] = (mod[2:3] * grad).astype(bf16)
        sums[3 * t : 3 * t + 1, :] = jnp.sum(grad * attn[rows, :], 0, keepdims=True)
        sums[3 * t + 1 : 3 * t + 2, :] = jnp.sum(db, 0, keepdims=True)
        sums[3 * t + 2 : 3 * t + 3, :] = jnp.sum(db * normed, 0, keepdims=True)


def back_middle(info, modulation, hidden, attn, g_mine, terms, number):
    half = hidden.shape[0]
    return call(
        functools.partial(back_middle_body, number),
        "back_middle",
        [(info, SMEM), (modulation, VMEM), (hidden, VMEM), (attn, VMEM), (g_mine, VMEM)]
        + [(t, VMEM) for t in terms],
        [((half, WIDTH), f32, VMEM), ((half, WIDTH), bf16, VMEM), ((3 * (half // 64), WIDTH), f32, VMEM)],
    )


def attend_back_body(number, info, near_w, far_w, near_qkv, far_qkv, near_p, far_p, s0, s1, s2, s3, *rest):
    dat, near_grad, far_grad, g0, g1, g2, g3, da, near_do, far_do, sems = rest
    copies = started(share_copies(info, (s0, s1, s2, s3), dat, sems))
    mask = head_mask()
    near_out, far_out = near_w[:, QKV:], far_w[:, QKV:]
    finish(copies)
    for rows in chunks_of(dat.shape[0], 384):
        near_do[rows, :] = dot(dat[rows, :], near_out).astype(bf16)
        far_do[rows, :] = dot(dat[rows, :], far_out).astype(bf16)
    for i in range(2 * number):
        rows = slice(i * KEPT, (i + 1) * KEPT)
        for do, qkv, probs, out in ((near_do, near_qkv, near_p, near_grad), (far_do, far_qkv, far_p, far_grad)):
            here = qkv[rows, :]
            q, k, v = (here[:, j * PAIRED : (j + 1) * PAIRED] for j in range(3))
            low = probs[i]
            p = low.astype(f32)
            both = split_heads(do[rows, :], mask)
            dp = dot_t(both, v)
            ds = (p * (dp - jnp.sum(p * dp, -1, keepdims=True))).astype(bf16)
            wide = jnp.concatenate([ds[:KEPT], ds[KEPT:]], 1)
            dq = dot(wide, split_heads(k, mask)) * score_scale
            dk = t_dot(ds, split_heads(q, mask)) * score_scale
            dv = t_dot(low, both)
            out[rows, :] = jnp.concatenate([dq, dk, dv], 1).astype(bf16)
    near_in, far_in = near_w[:, :QKV], far_w[:, :QKV]
    for rows in chunks_of(dat.shape[0], 384):
        da[rows, :] = (dot_t(near_grad[rows, :], near_in) + dot_t(far_grad[rows, :], far_in)).astype(bf16)
    split_halves(info, da, (g0, g1, g2, g3))


def attend_back(info, near, far, pieces, number):
    rows = 2 * number * KEPT
    return call(
        functools.partial(attend_back_body, number),
        "attend_back",
        [(info, SMEM)]
        + [(a, VMEM) for a in (near[0], far[0], near[1], far[1], near[2], far[2])]
        + [(p, ANY) for p in pieces],
        [((rows, WIDTH), bf16, VMEM)] + [((rows, QKV), bf16, VMEM)] * 2 + halves_of(rows),
        [pltpu.VMEM((rows, WIDTH), bf16)]
        + [pltpu.VMEM((rows, PAIRED), bf16)] * 2
        + [pltpu.SemaphoreType.DMA((4,))],
        flops=4 * rows * WIDTH * 576,
    )


def attn_grads_body(strips, info, act, dat, near_grad, far_grad, near_o, far_o, vectors, o0, o1, o2, o3, mixed, full, extra, sems):
    mixed[...] = jnp.concatenate([near_o[...], far_o[...]], 1)
    for part in (slice(0, 512), slice(512, WIDTH)):
        parts = [t_dot(act[:, part], grad[...]) for grad in (near_grad, far_grad)]
        parts.append(t_dot(dat[:, part], mixed[...]))
        full[part, :] = jnp.concatenate(parts, 1).astype(bf16)
    sums = jnp.concatenate(
        [column_sums(near_grad), column_sums(far_grad), jnp.zeros((1, 2 * PAIRED), f32)], 1
    )
    rows = (sums, column_sums(dat), vectors[0:1, :], vectors[1:2, :])
    extra[...] = stacked([part for row in rows for part in two_rows(row)], 16).astype(bf16)
    finish(started(block_copies(strips, info, full, extra, (o0, o1, o2, o3), sems)))


def attn_grads(info, act, dat, grads, near_o, far_o, vectors, strips, after):
    rows = dat.shape[0]
    return call(
        functools.partial(attn_grads_body, strips),
        "attn_grads",
        [(info, SMEM)] + [(a, VMEM) for a in (act, dat, *grads, near_o, far_o, vectors)],
        [((2, SIDE + 16 * (k % 2), WIDTH) if strips else (304, WIDTH), bf16, ANY) for k in range(4)],
        [
            pltpu.VMEM((rows, 2 * PAIRED), bf16),
            pltpu.VMEM((WIDTH, WIDTH), bf16),
            pltpu.VMEM((16, WIDTH), bf16),
            pltpu.SemaphoreType.DMA((12,)),
        ],
        flops=2 * rows * WIDTH * WIDTH,
        after=after,
    )


def last_rows_body(number, info, modulation, x_mine, dh, *rest):
    terms, (back_sums, gate_sums, out, sums) = rest[:-4], rest[-4:]
    half = x_mine.shape[0]
    parts = half // 64
    sums[...] = jnp.zeros_like(sums)
    for t in range(parts):
        rows = slice(t * 64, (t + 1) * 64)
        mod = modulation[info[FIRST] + (info[HALF] * parts + t) // 2]
        da = all_terms(terms, rows)
        normed, inverse = normalize(x_mine[rows, :].astype(f32))
        out[rows, :] = (dh[rows, :] + norm_back(da * (1.0 + mod[1:2]), normed, inverse)).astype(bf16)
        sums[6 * t : 6 * t + 1, :] = jnp.sum(da, 0, keepdims=True)
        sums[6 * t + 1 : 6 * t + 2, :] = jnp.sum(da * normed, 0, keepdims=True)
        sums[6 * t + 2 : 6 * t + 5, :] = back_sums[3 * t : 3 * t + 3, :]
        sums[6 * t + 5 : 6 * t + 6, :] = gate_sums[t : t + 1, :]
    out[half:, :] = sums[...].astype(bf16)


def gather_last(last, held):
    near, far = over_head(last, 1), over_head(last, 2)
    pieces = [(last, 0, 0), (near, 1, 0)]
    at = 0
    *parts, later = relay_two(far, held, (near,))
    for part in parts:
        pieces += [(part, 2, at), (over_head(part, 1), 3, at)]
        at += part.shape[0]
    return pieces, later


def last_rows(info, modulation, x_mine, dh, terms, back_sums, gate_sums, number):
    half = x_mine.shape[0]
    extra = -(-6 * (half // 64) // 16) * 16
    (out,) = call(
        functools.partial(last_rows_body, number),
        "last_rows",
        [(info, SMEM), (modulation, VMEM), (x_mine, VMEM), (dh, VMEM)]
        + [(t, VMEM) for t in terms]
        + [(back_sums, VMEM), (gate_sums, VMEM)],
        [((half + extra, WIDTH), bf16, VMEM)],
        [pltpu.VMEM((extra, WIDTH), f32)],
        cost=0,
    )
    return out, extra


def attn_half_body(keep_p, got_p, keep_q, got_q, mine_p, mine_q, send_p, send_q):
    for keep, got, mine, send in ((keep_p, got_p, mine_p, send_p), (keep_q, got_q, mine_q, send_q)):
        for j, out in ((0, mine), (1, send)):
            out[:SIDE, :] = (keep[j, :SIDE, :].astype(f32) + got[j, :SIDE, :].astype(f32)).astype(out.dtype)
            if keep.shape[1] > SIDE:
                extra = keep[j, SIDE:, :].astype(f32) + got[j, SIDE:, :].astype(f32)
                rows = [part for k in range(4) for part in two_rows(extra[2 * k : 2 * k + 1] + extra[2 * k + 1 : 2 * k + 2])]
                out[SIDE:, :] = stacked(rows, 16).astype(bf16).astype(out.dtype)


def attn_half(keeps, gots):
    shapes = [(SIDE, WIDTH), (SIDE + 16, WIDTH)]
    return call(
        attn_half_body,
        "attn_half",
        [(a, VMEM) for a in (keeps[0], gots[0], keeps[1], gots[1])],
        [(shape, kind, VMEM) for kind in (f32, bf16) for shape in shapes],
    )


def join_body(mine_p, got_p, mine_q, got_q, near, far, vectors):
    cut = 2 * QKV + PAIRED
    for at, mine, got in ((0, mine_p, got_p), (SIDE, mine_q, got_q)):
        total = mine[:SIDE, :] + got[:SIDE, :].astype(f32)
        near[at : at + SIDE, :] = jnp.concatenate([total[:, :QKV], total[:, 2 * QKV : cut]], 1)
        far[at : at + SIDE, :] = jnp.concatenate([total[:, QKV : 2 * QKV], total[:, cut:]], 1).astype(bf16)
    extra = mine_q[SIDE:, :] + got_q[SIDE:, :].astype(f32)
    qkv, dat, up, dm = (extra[2 * k : 2 * k + 1] + extra[2 * k + 1 : 2 * k + 2] for k in range(4))
    pad = lambda row: jnp.concatenate([row, jnp.zeros((1, UP - QKV), f32)], 1)
    rows = two_rows(pad(qkv[:, QKV : 2 * QKV])) + two_rows(up[:, UP:])
    both = [two_rows(dat), two_rows(dm)]
    rows += [part[:, c : c + UP] for pair in both for part in pair for c in (0, UP)]
    far[288:304, :] = stacked(rows, 16).astype(bf16)
    low = lambda value: value.astype(bf16).astype(f32)
    wide = lambda row: jnp.concatenate([row, jnp.zeros((1, WIDTH - UP), f32)], 1)
    vectors[...] = stacked(
        [wide(pad(qkv[:, :QKV])), wide(up[:, :UP])] + [low(pair[0]) + low(pair[1]) for pair in both], 8
    )


def join(mines, gots):
    return call(
        join_body,
        "attn_join",
        [(a, VMEM) for a in (mines[0], gots[0], mines[1], gots[1])],
        [((288, UP), f32, VMEM), ((304, UP), bf16, VMEM), ((8, WIDTH), f32, VMEM)],
    )


def strip_rows(info, near, got, keep, send):
    mine = pl.ds(pl.multiple_of(info[CORE] * SIDE, 16), SIDE)
    theirs = pl.ds(pl.multiple_of((1 - info[CORE]) * SIDE, 16), SIDE)
    keep[...] = near[mine, :] + got[mine, :].astype(f32)
    send[:SIDE, :] = (near[theirs, :] + got[theirs, :].astype(f32)).astype(bf16)


def mlp_strip(info, near, got):
    width = near.shape[1]
    return call(
        strip_rows,
        "mlp_strip",
        [(info, SMEM), (near, VMEM), (got, VMEM)],
        [((SIDE, width), f32, VMEM), ((SIDE, width), bf16, VMEM)],
    )


def attn_strip_body(info, near, vectors, got, keep, send, total):
    strip_rows(info, near, got, keep, send)
    extra = got[288:304, :].astype(f32)
    low = lambda value: value.astype(bf16).astype(f32)
    wide = lambda row: jnp.concatenate([row, jnp.zeros((1, WIDTH - UP), f32)], 1)
    rows, totals = [], []
    for k in range(2):
        pair = two_rows(vectors[k : k + 1, :UP] + extra[2 * k : 2 * k + 1] + extra[2 * k + 1 : 2 * k + 2])
        rows += pair
        totals.append(wide(low(pair[0]) + low(pair[1])))
    for k in range(2):
        at = 4 + 4 * k
        row = jnp.concatenate([extra[at + j : at + j + 1] + extra[at + 2 + j : at + 3 + j] for j in range(2)], 1)
        totals.append(vectors[2 + k : 3 + k, :] + row)
    send[SIDE:, :] = stacked(rows, 16).astype(bf16)
    total[...] = stacked(totals, 8)


def attn_strip(info, near, vectors, got):
    width = near.shape[1]
    return call(
        attn_strip_body,
        "attn_strip",
        [(info, SMEM), (near, VMEM), (vectors, VMEM), (got, VMEM)],
        [((SIDE, width), f32, VMEM), ((SIDE + 16, width), bf16, VMEM), ((8, WIDTH), f32, VMEM)],
    )


def shampoo_body(wide, chained, info, keep, got, left, right, left_root, right_root, master, *rest):
    out_g, out_l, out_r, out_m = rest[4:] if chained else rest
    core = info[CORE]
    for step in range(4 if wide else 2):

        @pl.when(pl.program_id(0) == step)
        def _(step=step):
            for j in range(4):
                column, half = (4 * (step // 2) + j, step % 2) if wide else (2 * step + j // 2, j % 2)
                columns = slice(column * SIDE, (column + 1) * SIDE)
                value = jnp.where(core == half, keep[:, columns], got[:SIDE, columns].astype(f32))
                out_g[j] = value
                low = value.astype(bf16)
                out_l[j] = decay_rate * left[j] + (1.0 - decay_rate) * dot_t(low, low)
                out_r[j] = decay_rate * right[j] + (1.0 - decay_rate) * t_dot(low, low)
                first = dot(left_root[j].astype(bf16), low).astype(bf16)
                out_m[j] = master[j] - weight_rate * dot(first, right_root[j].astype(bf16))


def shampoo(info, keep, got, states, previous, wide):
    first = 2 if wide else 0
    tiles = pl.BlockSpec((4, SIDE, SIDE), lambda i: (first + i, 0, 0))
    whole = lambda a: pl.BlockSpec(a.shape, lambda i: (0, 0))
    inputs = [(info, SMEM), (keep, whole(keep)), (got, whole(got))] + [(s, tiles) for s in states]
    aliases = None
    if previous is not None:
        aliases = {len(inputs) + k: k for k in range(4)}
        inputs += [(p, ANY) for p in previous]
    return call(
        functools.partial(shampoo_body, wide, previous is not None),
        "shampoo",
        inputs,
        [(states[0].shape, f32, tiles)] * 4,
        aliases=aliases,
        grid=(4 if wide else 2,),
    )


def heads_of(qkv, up):
    rows = []
    for j in range(2):
        rows.append(
            jnp.concatenate(
                [
                    qkv[:, j * HEAD_DIM : (j + 1) * HEAD_DIM],
                    qkv[:, 2 * PAIRED + j * HEAD_DIM : 2 * PAIRED + (j + 1) * HEAD_DIM],
                    up[:, j * 288 : (j + 1) * 288],
                ],
                1,
            )
        )
    return rows


def bias_body(info, total, got, b_in, s_in, b_out, s_out, g_in, m_in, n_in, g_out, m_out, n_out):
    there = got[SIDE : SIDE + 16, :].astype(f32)
    mine = heads_of(total[0:1, :QKV], total[1:2, :UP])
    theirs = heads_of((there[0:1] + there[1:2])[:, :QKV], there[2:3] + there[3:4])
    zero = info[CORE] == 0
    rows = [jnp.where(zero, a, b) for a, b in zip(mine, theirs)]
    rows += [jnp.where(zero, b, a) for a, b in zip(mine, theirs)]
    for grad, base, square, g_ref, m_ref, n_ref in (
        (stacked(rows, 4), b_in, s_in, g_in, m_in, n_in),
        (total[2:4, :], b_out, s_out, g_out, m_out, n_out),
    ):
        new = decay_rate * square[...] + (1.0 - decay_rate) * grad * grad
        g_ref[...] = grad
        m_ref[...] = new
        n_ref[...] = base[...] - bias_rate * grad / (jnp.sqrt(new) + root_epsilon)


def bias_step(info, total, got, bias_in, bias_in_sq, bias_out, bias_out_sq):
    arrays = [total, got, bias_in, bias_in_sq, bias_out, bias_out_sq]
    return call(
        bias_body,
        "bias_step",
        [(info, SMEM)] + [(a, VMEM) for a in arrays],
        [(bias_in.shape, f32, VMEM)] * 3 + [(bias_out.shape, f32, VMEM)] * 3,
    )


def pass_body(far, block, rows):
    size = block.shape[0]
    block[...] = far[:size, :]
    rows[...] = far[size:, :]


def pass_on(far, after):
    width = far.shape[1]
    return call(
        pass_body,
        "pass_on",
        [(far, VMEM)],
        [((far.shape[0] - 16, width), bf16, VMEM), ((16, width), bf16, VMEM)],
        after=after,
    )


def finish_whole(attn_blocks, mlp_blocks, states, biases, core, head):
    left_stat, right_stat, left_root, right_root, master = states
    bias_in, bias_in_sq, bias_out, bias_out_sq = biases
    far_of = lambda v: over_head(v, 2)

    def halves(near):
        both = lax.all_gather(near.astype(bf16), "core").astype(f32)
        return [part.reshape(8, SIDE, -1, SIDE).transpose(2, 0, 1, 3) for part in (both[0], both[1])]

    full = jnp.concatenate([b[:288] for b in attn_blocks], 0)
    near, far = (
        jnp.concatenate([full[:, a : a + QKV], full[:, b : b + PAIRED]], 1) for a, b in ((0, 864), (432, 1008))
    )
    a0, a1 = halves(near.astype(f32) + far_of(far).astype(f32))
    near, far = (jnp.concatenate(mlp_blocks[2 * g : 2 * g + 2], 0).reshape(WIDTH, WIDTH) for g in range(2))
    m0, m1 = halves(near.astype(f32) + far_of(far).astype(f32))
    attn = jnp.stack([a0, a1], 1).reshape(8, 8, SIDE, SIDE)
    tiles = jnp.concatenate([attn, m0[:4], m1[:4], m0[4:], m1[4:]], 0)
    tiles = tiles.transpose(1, 0, 2, 3).reshape(192, SIDE, SIDE)
    tiles = lax.psum_scatter(tiles, "sup", scatter_dimension=0, tiled=True)
    count = master.shape[0]
    grad = lax.dynamic_slice_in_dim(tiles, core * count, count, 0)
    low = grad.astype(bf16)
    product = lambda spec, a, b: jnp.einsum(spec, a.astype(bf16), b.astype(bf16), preferred_element_type=f32)
    left_new = decay_rate * left_stat + (1.0 - decay_rate) * product("kab,kcb->kac", low, low)
    right_new = decay_rate * right_stat + (1.0 - decay_rate) * product("kba,kbc->kac", low, low)
    step = product("kab,kbc->kac", product("kab,kbc->kac", left_root, low), right_root)
    master_new = master - weight_rate * step
    attn_rows = attn_blocks[0][288:304].astype(f32)
    rows = [attn_rows[2 * k] + attn_rows[2 * k + 1] for k in range(4)]
    vector = lax.psum(jnp.stack(rows, 0), "sup")
    qkv, dat, up, dm = vector[0][: 2 * QKV], vector[1], vector[2], vector[3]
    rows = jnp.stack([dat, dm], 0)
    swap = lax.psum(rows, HEAD_AXES) * 0.5
    qkv = qkv[:QKV] + far_of(qkv[QKV:])
    up = up[:UP] + far_of(up[UP:])
    parts = [jnp.concatenate(heads_of(qkv[None], up[None]), 0)]
    grad_in = lax.all_gather(parts[0], "core", axis=0, tiled=True)
    out = [grad, left_new, right_new, master_new]
    for g, b, s in ((grad_in, bias_in, bias_in_sq), (swap, bias_out, bias_out_sq)):
        new = decay_rate * s + (1.0 - decay_rate) * g * g
        out += [g, new, b - bias_rate * g / (jnp.sqrt(new) + root_epsilon)]
    return out


def on_device(
    tokens,
    cotangent,
    modulation,
    counts,
    master,
    left_stat,
    right_stat,
    left_root,
    right_root,
    bias_in,
    bias_in_sq,
    bias_out,
    bias_out_sq,
):
    images, slots, _ = tokens.shape
    core = lax.axis_index("core")
    head = lax.axis_index(HEAD_AXES)
    number = images // 2
    strips = master.shape[0] == 24
    place = lax.axis_index("sup") if strips else 0
    order = core if strips else 0
    info = jnp.stack(
        [jnp.asarray(v, jnp.int32) for v in (place, order, core, head, head % 2, (head // 2) * number, head // 2, 0)]
    )
    LAST[0] = None
    attn_mine, bias_mine, mlp_mine, strips_other = pack(
        info, master if strips else jnp.zeros((24, SIDE, SIDE), f32), bias_in
    )
    if strips:
        block, mlp_block = blocks_of(attn_mine, bias_mine, mlp_mine, over_core(strips_other))
    small, part = small_rows(info, counts, modulation, tokens)
    far_tokens, far_small = over_core(part), over_core(small)
    if strips:
        mlp_near = lax.all_gather(mlp_block, "sup")
        far_block = over_head(block, 2)
        attn_near = gather_pieces(block)
    else:
        (attn_near, attn_far), (mlp_near, mlp_far) = whole_pieces(master, core)
        far_block = jnp.concatenate([attn_far[0], over_head(bias_mine, 2)], 0)
    act, dm_own, x_mine, g_mine = kept_rows(info, small, tokens, cotangent, far_small, far_tokens, number)
    dm_other = over_core(dm_own)
    if strips:
        mlp_far = over_head(relay(mlp_block, (far_block,)), 2)
    far_block, bias_far = pass_on(far_block, attn_near[1:])
    if strips:
        attn_far = gather_pieces(far_block)
    near = attend(info, act, bias_mine, attn_near, number)
    far = attend(info, act, bias_far, attn_far, number)
    if strips:
        mlp_far = lax.all_gather(relay(mlp_far), "sup")
    terms = sum_rows(project(info, near[0], far[0], near[3], far[3]))
    w_near = mlp_weights(info, mlp_near)
    hidden, attn, act_mine = middle(info, modulation, bias_out, x_mine, terms, number)
    act_far = over_head(act_mine, 1)
    w_far = mlp_weights(info, mlp_far)
    act_far = relay(act_far)
    pieces = (act_mine, act_far, over_core(act_mine), over_core(act_far))
    act_two, f, du, *db_parts = mlp(info, (bias_mine, bias_far), dm_own, dm_other, w_near, w_far, pieces, number)
    db_terms = sum_rows(db_parts, spare=32)
    mlp_parts = down_rows(info, f, w_near[1], w_far[1])
    mlp_terms = sum_rows(mlp_parts)
    dh, dat_mine, back_sums = back_middle(info, modulation, hidden, attn, g_mine, db_terms, number)
    dat_far = over_head(dat_mine, 1)
    *mlp_blocks, vectors = mlp_grads(info, act_two, du, f, dm_own, dm_other, strips)
    if strips:
        gots = [over_sup(mlp_blocks[0], 1), over_sup(mlp_blocks[1], 2)]
    output_mine, gate_sums = output_rows(info, modulation, bias_out, hidden, g_mine, mlp_terms, number)
    output_all = lax.all_gather(output_mine, HEAD_AXES, axis=0, tiled=True)
    dat_far = relay(dat_far, name="relay_dat")
    dat_pieces = (dat_mine, dat_far, over_core(dat_mine), over_core(dat_far))
    dat, near_grad, far_grad, *da_parts = attend_back(info, near, far, dat_pieces, number)
    da_terms = sum_rows(da_parts, spare=0)
    attn_blocks = attn_grads(info, act, dat, (near_grad, far_grad), near[3], far[3], vectors, strips, (da_terms[1],))
    if strips:
        near_mine, far_mine, near_send, far_send = half_way(mlp_blocks[2:], gots, ())
        gots = [over_sup(near_send, 2), over_sup(far_send, 1)]
    last, extra = last_rows(info, modulation, x_mine, dh, da_terms, back_sums, gate_sums, number)
    half = x_mine.shape[0]

    states = (left_stat, right_stat, left_root, right_root, master)
    biases = (bias_in, bias_in_sq, bias_out, bias_out_sq)
    if strips:
        (output,) = expand_all(info, counts, output_all, images, slots)
        attn_gots = [over_sup(attn_blocks[0], 1), over_sup(attn_blocks[1], 2)]
        mine_p, mine_q, send_p, send_q = attn_half(attn_blocks[2:], attn_gots)
        attn_gots = [over_sup(send_p, 2), over_sup(send_q, 1)]
        mlp_near_sum, mlp_far_sum = mlp_join((near_mine, far_mine), gots)
        near_sum, far_sum, sums = join((mine_p, mine_q), attn_gots)
        far_got = over_head(far_sum, 2)
        last_pieces, mlp_far_sum = gather_last(last, mlp_far_sum)
        mlp_far_got = over_head(mlp_far_sum, 2)
        keep, send, total = attn_strip(info, near_sum, sums, far_got)
        got = over_core(send)
        previous = shampoo(info, keep, got, states, None, False)
        grad_tokens, grad_modulation = expand(info, counts, half + extra, last_pieces, images, slots, extra)
        steps = bias_step(info, total, got, *biases)
        mlp_keep, mlp_send = mlp_strip(info, mlp_near_sum, mlp_far_got)
        mlp_got = over_core(mlp_send)
        weights = shampoo(info, mlp_keep, mlp_got, states, previous, True)
        tail = list(weights) + list(steps)
    else:
        last_pieces, _ = gather_last(last, act_mine)
        grad_tokens, grad_modulation = expand(info, counts, half + extra, last_pieces, images, slots, extra)
        (output,) = expand_all(info, counts, output_all, images, slots)
        tail = finish_whole(attn_blocks, mlp_blocks, states, biases, core, head)
    return (output, grad_tokens, grad_modulation, *tail)


def solution(mesh):
    devices = mesh.devices
    inner = Mesh(
        devices.reshape(devices.shape[0] // 2, 2, 2, devices.shape[1] // 2), ("sup", "core", *HEAD_AXES)
    )
    seq = ("sup", "core")
    tile = P(("sup", "core", *HEAD_AXES), None, None)
    rows = P(seq, None, None)
    return jax.shard_map(
        on_device,
        mesh=inner,
        in_specs=(rows, rows, rows, P(seq, None), tile, tile, tile, tile, tile)
        + (P(HEAD_AXES, None), P(HEAD_AXES, None), P(), P()),
        out_specs=(rows, rows, P(seq, None, HEAD_AXES), tile, tile, tile, tile)
        + (P(HEAD_AXES, None),) * 3
        + (P(),) * 3,
        check_vma=False,
    )
```
